32 devices in a mesh: dp: 4 (over y, x), vocab: 8 (over z, core).
Axes of the slice: x: 2, y: 2, z: 4, core: 2. Of those that a mesh axis runs over, the one named last changes fastest.
Arguments:
- x_clean: int32 [32, 256], P(('dp', 'vocab')), may hold values from 0 to 50256
- mask_index: int32 [32, 96], P(('dp', 'vocab')), may hold values from 0 to 256, as said below
- segment_ids: int32 [32, 256], P(('dp', 'vocab')), may hold values from 0 to 15, never falling along the last dimension, each value on 1 to 128 neighbouring positions
- noise_level: float32 [32], P('dp'), may hold values from 0.01 to 1
- embedding: float32 [50304, 768], P('vocab', 'dp'), may hold values from -6 to 6
- head_table: float32 [768, 50304], P('dp', 'vocab'), may hold values from -1 to 1
- w_time: float32 [256, 128], P(('dp', 'vocab')), may hold values from -0.375 to 0.375
- w_ada: float32 [128, 6144], P(None, ('dp', 'vocab')), may hold values from -0.5 to 0.5
- norm_gains: float32 [3, 768], P(None, ('dp', 'vocab')), may hold values from 0.3 to 2.5
- w_qkv: float32 [768, 2304], P(('dp', 'vocab')), may hold values from -0.21875 to 0.21875
- w_out: float32 [768, 768], P(('dp', 'vocab')), may hold values from -0.875 to 0.875
- w_up: float32 [768, 3072], P(('dp', 'vocab')), may hold values from -0.21875 to 0.21875
- w_down: float32 [3072, 768], P(('dp', 'vocab')), may hold values from -0.109375 to 0.109375
- moment_embedding: float32 [50304, 768], P('vocab', 'dp'), may hold values from -0.00061035156 to 0.00061035156
- moment_head_table: float32 [768, 50304], P('dp', 'vocab'), may hold values from -0.00061035156 to 0.00061035156
- moment_w_time: float32 [256, 128], P(('dp', 'vocab')), may hold values from -0.00061035156 to 0.00061035156
- moment_w_ada: float32 [128, 6144], P(None, ('dp', 'vocab')), may hold values from -0.00061035156 to 0.00061035156
- moment_norm_gains: float32 [3, 768], P(None, ('dp', 'vocab')), may hold values from -0.00061035156 to 0.00061035156
- moment_w_qkv: float32 [768, 2304], P(('dp', 'vocab')), may hold values from -0.00061035156 to 0.00061035156
- moment_w_out: float32 [768, 768], P(('dp', 'vocab')), may hold values from -0.00061035156 to 0.00061035156
- moment_w_up: float32 [768, 3072], P(('dp', 'vocab')), may hold values from -0.00061035156 to 0.00061035156
- moment_w_down: float32 [3072, 768], P(('dp', 'vocab')), may hold values from -0.00061035156 to 0.00061035156
- average_embedding: float32 [50304, 768], P('vocab', 'dp'), may hold values from -6 to 6
- average_head_table: float32 [768, 50304], P('dp', 'vocab'), may hold values from -0.21875 to 0.21875
- average_w_time: float32 [256, 128], P(('dp', 'vocab')), may hold values from -0.375 to 0.375
- average_w_ada: float32 [128, 6144], P(None, ('dp', 'vocab')), may hold values from -0.5 to 0.5
- average_norm_gains: float32 [3, 768], P(None, ('dp', 'vocab')), may hold values from 0.5 to 1.5
- average_w_qkv: float32 [768, 2304], P(('dp', 'vocab')), may hold values from -0.21875 to 0.21875
- average_w_out: float32 [768, 768], P(('dp', 'vocab')), may hold values from -0.875 to 0.875
- average_w_up: float32 [768, 3072], P(('dp', 'vocab')), may hold values from -0.21875 to 0.21875
- average_w_down: float32 [3072, 768], P(('dp', 'vocab')), may hold values from -0.109375 to 0.109375
Outputs:
- new_embedding: float32 [50304, 768], P('vocab', 'dp')
- new_head_table: float32 [768, 50304], P('dp', 'vocab')
- new_w_time: float32 [256, 128], P(('dp', 'vocab'))
- new_w_ada: float32 [128, 6144], P(None, ('dp', 'vocab'))
- new_norm_gains: float32 [3, 768], P(None, ('dp', 'vocab'))
- new_w_qkv: float32 [768, 2304], P(('dp', 'vocab'))
- new_w_out: float32 [768, 768], P(('dp', 'vocab'))
- new_w_up: float32 [768, 3072], P(('dp', 'vocab'))
- new_w_down: float32 [3072, 768], P(('dp', 'vocab'))
- new_moment_embedding: float32 [50304, 768], P('vocab', 'dp')
- new_moment_head_table: float32 [768, 50304], P('dp', 'vocab')
- new_moment_w_time: float32 [256, 128], P(('dp', 'vocab'))
- new_moment_w_ada: float32 [128, 6144], P(None, ('dp', 'vocab'))
- new_moment_norm_gains: float32 [3, 768], P(None, ('dp', 'vocab'))
- new_moment_w_qkv: float32 [768, 2304], P(('dp', 'vocab'))
- new_moment_w_out: float32 [768, 768], P(('dp', 'vocab'))
- new_moment_w_up: float32 [768, 3072], P(('dp', 'vocab'))
- new_moment_w_down: float32 [3072, 768], P(('dp', 'vocab'))
- new_average_embedding: float32 [50304, 768], P('vocab', 'dp')
- new_average_head_table: float32 [768, 50304], P('dp', 'vocab')
- new_average_w_time: float32 [256, 128], P(('dp', 'vocab'))
- new_average_w_ada: float32 [128, 6144], P(None, ('dp', 'vocab'))
- new_average_norm_gains: float32 [3, 768], P(None, ('dp', 'vocab'))
- new_average_w_qkv: float32 [768, 2304], P(('dp', 'vocab'))
- new_average_w_out: float32 [768, 768], P(('dp', 'vocab'))
- new_average_w_up: float32 [768, 3072], P(('dp', 'vocab'))
- new_average_w_down: float32 [3072, 768], P(('dp', 'vocab'))
- loss_sum: float32 [], replicated
- masked_count: float32 [], replicated
- grad_norm: float32 [], replicated
The draws below stay inside these ranges and needn't reach their ends.
Inputs may be any that keep to these rules, and one draw needn't show every extreme that they name: `mask_index`: each sequence's list names, in rising order, 32 to 96 distinct positions of that sequence, followed by 256 in the other slots; some sequence lists exactly 96 positions and another exactly 32.
All inputs are finite; a program needn't handle non-finite values.
Results may differ from the reference program's by a relative error of at most 0.011.
The reference program's roundings to bfloat16 on the way count: a program that leaves them out, or rounds other values in their place, can miss the bound.
Values may be sent and summed in bfloat16 or wider, within the bound.
No kernel may reach another device: no remote copies, remote signals or barrier semaphores. Data moves between devices by JAX's collectives and lax.ppermute only.
A program may use at most 320 MiB of HBM per device.

```python
import math
import jax
import jax.numpy as jnp
import numpy as np
from jax import lax

D = 768
HEADS = 12
HEAD_DIM = 64
FF = 3072
VOCAB = 50258
VP = 50304
COND = 128
FREQ = 256
LEN = 256
SLOTS = 96
ROWS = 32
NPARAM = 85166336


def draw_mask_index(key, part):
    key = jax.random.fold_in(key, 11)
    count_key, order_key, chosen_key = jax.random.split(key, 3)
    fewest = SLOTS // 3
    counts = jax.random.randint(count_key, (ROWS,), fewest, SLOTS + 1)
    chosen = jax.random.permutation(chosen_key, ROWS)
    counts = counts.at[chosen[0]].set(SLOTS).at[chosen[1]].set(fewest)
    row_keys = jax.random.split(order_key, ROWS)
    orders = jax.vmap(lambda row_key: jax.random.permutation(row_key, LEN)[:SLOTS])(row_keys)
    filled = jnp.where(jnp.arange(SLOTS)[None, :] < counts[:, None], orders, LEN)
    return jnp.sort(filled, axis=1).astype(jnp.int32)


def draw_head_table(key, part):
    key = jax.random.fold_in(key, 23)
    column = jnp.arange(VP, dtype=jnp.float32) / VP
    base_values = jnp.clip(jax.random.normal(key, (D, VP), jnp.float32), -5.0, 5.0)
    rising = 1.0 + 2.0 * column
    return base_values * rising[None, :] * D ** (-0.5)


def draw_norm_gains(key, part):
    key = jax.random.fold_in(key, 37)
    place = jnp.arange(D, dtype=jnp.float32) / D
    jitter = jax.random.uniform(key, (3, D), jnp.float32, -1.0, 1.0)
    rising = 0.5 + place
    spread_factor = 0.15
    return rising[None, :] * (1.0 + spread_factor * jitter)


def set_ends(result, own_key, smallest, high):
    index_at = [jax.random.randint(jax.random.fold_in(own_key, axis), (), 0, length) for axis, length in enumerate(result.shape)]
    widest = result.shape.index(max(result.shape))
    next_to = index_at[:widest] + [(index_at[widest] + 1) % result.shape[widest]] + index_at[widest + 1:]
    return result.at[tuple(index_at)].set(smallest).at[tuple(next_to)].set(high)


def steps_of(rng, shape, cuts, low, top_value):
    def one(axis_at, blocks):
        steps = jax.random.uniform(jax.random.fold_in(jax.random.fold_in(rng, 6), axis_at), (blocks,), jnp.float32, low / len(cuts), top_value / len(cuts))
        return jnp.repeat(jnp.exp(steps), shape[axis_at] // blocks).reshape((-1,) + (1,) * (len(shape) - axis_at - 1))

    level = one(*cuts[0])
    for cut in cuts[1:]:
        level = level * one(*cut)
    return level


def rank_table(number_of, skew):
    weights = [(1 << 20) // math.isqrt(grade ** skew) + 1 for grade in range(1, number_of + 1)]
    scale = 1 + sum(weights) // (1 << 30)
    return np.cumsum(np.array([max(1, weight // scale) for weight in weights]))


def skewed_ids(key, extent, number_of, lean):
    grid = rank_table(number_of, lean)
    ticket = jax.random.randint(jax.random.fold_in(key, 1), extent, 0, int(grid[number_of - 1]))
    grade = jnp.searchsorted(jnp.asarray(grid, jnp.int32), ticket, side="right")
    return jax.random.permutation(jax.random.fold_in(key, 2), number_of)[grade].astype(jnp.int32)


def profile(count, total, limit, lean):
    portions = [(1 << 20) // math.isqrt(grade ** lean) + 1 for grade in range(2, count + 1)]
    surplus, given = total - limit - (count - 1), [1] * (count - 1)
    while surplus > 0:
        movable = [i for i in range(count - 1) if given[i] < limit]
        mass, left = sum([portions[i] for i in movable]), surplus
        for i in movable:
            extra = min(limit - given[i], max(1, left * portions[i] // mass), surplus)
            given[i] = given[i] + extra
            surplus = surplus - extra
    return np.array([limit] + given)


def ragged_sizes(stream_key, count, total, bound, slope):
    if count == 2:
        one = jax.random.randint(stream_key, (), max(1, total - bound), min(bound, total - 1) + 1)
        return jnp.stack([one, total - one])
    tallies = jnp.asarray(profile(count, total, bound, slope), jnp.int32)
    pairs = (count - 1) // 2
    donor, taker = tallies[1:1 + 2 * pairs:2], tallies[2:2 + 2 * pairs:2]
    margin = jnp.minimum(donor - 1, bound - taker)
    passed = jax.random.randint(jax.random.fold_in(stream_key, 1), (pairs,), 0, 1 << 20) % (margin + 1)
    tallies = tallies.at[1:1 + 2 * pairs:2].set(donor - passed).at[2:2 + 2 * pairs:2].set(taker + passed)
    return tallies[jax.random.permutation(jax.random.fold_in(stream_key, 2), count)]


def gaussian(key, dims, scale, limit, cuts=(), kind=jnp.bfloat16):
    result = jax.random.normal(key, dims, jnp.float32) * scale
    if len(cuts) > 0:
        result = steps_of(key, dims, cuts, -0.22, 0.18) * result
    return jnp.clip(result, min=-limit, max=limit).astype(kind)


def setup_inputs(seed: int = 0) -> dict:
    seeds = jax.random.split(jax.random.key(seed), 32)
    return {
        "x_clean": set_ends(skewed_ids(seeds[0], (ROWS, LEN), VOCAB - 1, 2), jax.random.fold_in(seeds[0], 3), 0, (VOCAB - 1) - 1).astype(jnp.int32),
        "mask_index": draw_mask_index(jax.random.fold_in(seeds[31], 71), 0),
        "segment_ids": jax.vmap(lambda own: jnp.searchsorted(jnp.cumsum(ragged_sizes(own, 16, LEN, LEN // 2, 2)), jnp.arange(LEN), side="right"))(jax.random.split(seeds[2], ROWS)).reshape((ROWS, LEN)).astype(jnp.int32),
        "noise_level": jnp.clip(jnp.exp(math.log(1.0) - 4.6051702 * jax.random.uniform(seeds[3], (ROWS,), jnp.float32) ** steps_of(seeds[3], (ROWS,), ((0, 4),), -0.2, 0.2)), 0.01, 1.0),
        "embedding": gaussian(seeds[4], (VP, D), 1.0, 6.0, ((0, 8), (1, 4)), jnp.float32),
        "head_table": draw_head_table(jax.random.fold_in(seeds[31], 71), 0),
        "w_time": gaussian(seeds[6], (FREQ, COND), FREQ ** -0.5, 0.375, ((0, 32),), jnp.float32),
        "w_ada": gaussian(seeds[7], (COND, 8 * D), COND ** -0.5, 0.5, ((1, 32),), jnp.float32),
        "norm_gains": draw_norm_gains(jax.random.fold_in(seeds[31], 71), 0),
        "w_qkv": gaussian(seeds[9], (D, 3 * D), D ** -0.5, 0.21875, ((0, 32),), jnp.float32),
        "w_out": gaussian(seeds[10], (D, D), (D // 16) ** -0.5, 0.875, ((0, 32),), jnp.float32),
        "w_up": gaussian(seeds[11], (D, FF), D ** -0.5, 0.21875, ((0, 32),), jnp.float32),
        "w_down": gaussian(seeds[12], (FF, D), FF ** -0.5, 0.109375, ((0, 32),), jnp.float32),
        "moment_embedding": gaussian(seeds[13], (VP, D), (NPARAM ** -0.5), 0.00061035156, ((0, 8), (1, 4)), jnp.float32),
        "moment_head_table": gaussian(seeds[14], (D, VP), (NPARAM ** -0.5), 0.00061035156, ((0, 4), (1, 8)), jnp.float32),
        "moment_w_time": gaussian(seeds[15], (FREQ, COND), (NPARAM ** -0.5), 0.00061035156, ((0, 32),), jnp.float32),
        "moment_w_ada": gaussian(seeds[16], (COND, 8 * D), (NPARAM ** -0.5), 0.00061035156, ((1, 32),), jnp.float32),
        "moment_norm_gains": gaussian(seeds[17], (3, D), (NPARAM ** -0.5), 0.00061035156, ((1, 32),), jnp.float32),
        "moment_w_qkv": gaussian(seeds[18], (D, 3 * D), (NPARAM ** -0.5), 0.00061035156, ((0, 32),), jnp.float32),
        "moment_w_out": gaussian(seeds[19], (D, D), (NPARAM ** -0.5), 0.00061035156, ((0, 32),), jnp.float32),
        "moment_w_up": gaussian(seeds[20], (D, FF), (NPARAM ** -0.5), 0.00061035156, ((0, 32),), jnp.float32),
        "moment_w_down": gaussian(seeds[21], (FF, D), (NPARAM ** -0.5), 0.00061035156, ((0, 32),), jnp.float32),
        "average_embedding": gaussian(seeds[22], (VP, D), 1.0, 6.0, ((0, 8), (1, 4)), jnp.float32),
        "average_head_table": gaussian(seeds[23], (D, VP), D ** -0.5, 0.21875, ((0, 4), (1, 8)), jnp.float32),
        "average_w_time": gaussian(seeds[24], (FREQ, COND), FREQ ** -0.5, 0.375, ((0, 32),), jnp.float32),
        "average_w_ada": gaussian(seeds[25], (COND, 8 * D), COND ** -0.5, 0.5, ((1, 32),), jnp.float32),
        "average_norm_gains": jnp.clip(1.0 + 0.1 * jax.random.normal(seeds[26], (3, D), jnp.float32), 0.5, 1.5),
        "average_w_qkv": gaussian(seeds[27], (D, 3 * D), D ** -0.5, 0.21875, ((0, 32),), jnp.float32),
        "average_w_out": gaussian(seeds[28], (D, D), (D // 16) ** -0.5, 0.875, ((0, 32),), jnp.float32),
        "average_w_up": gaussian(seeds[29], (D, FF), D ** -0.5, 0.21875, ((0, 32),), jnp.float32),
        "average_w_down": gaussian(seeds[30], (FF, D), FF ** -0.5, 0.109375, ((0, 32),), jnp.float32),
    }


@jax.custom_vjp
def low(v):
    return lax.optimization_barrier(v.astype(jnp.bfloat16)).astype(jnp.float32)

@jax.custom_vjp
def low_back(v):
    return v

def low_keep(v):
    return (low(v), None)

def low_pass(kept, grad):
    return (grad,)

def back_keep(v):
    return (v, None)

def back_low(kept, grad):
    return (low(grad),)
low.defvjp(low_keep, low_pass)
low_back.defvjp(back_keep, back_low)
norm_epsilon = 1e-06
weight_cap = 20.0
clip_level = 1.0
learn_rate = 30.0
embed_rate = 2000.0
momentum_rate = 0.9
average_rate = 0.5
highest = lax.Precision.HIGHEST

def features(level, freq_count):
    sigma_level = -jnp.log1p(-(1.0 - 0.001) * level)
    half_count = freq_count // 2
    frequency = jnp.exp(-jnp.log(10000.0) * jnp.arange(half_count, dtype=jnp.float32) / half_count)
    angles = sigma_level * frequency
    return jnp.concatenate([jnp.cos(angles), jnp.sin(angles)])

def nelbo_weight(level):
    sigma_level = -jnp.log1p(-(1.0 - 0.001) * level)
    rate_value = (1.0 - 0.001) / (1.0 - (1.0 - 0.001) * level)
    return jnp.minimum(rate_value / jnp.expm1(sigma_level), weight_cap)

def norm_mod(values, gain_row, shift_row, scale_row):
    center = values - lax.optimization_barrier(jnp.mean(values, -1, keepdims=True))
    spread = lax.optimization_barrier(jnp.mean(center * center, -1, keepdims=True))
    return center * lax.rsqrt(spread + norm_epsilon) * gain_row * (1.0 + scale_row) + shift_row

def condition(w_time, w_ada, spectrum):
    hidden_time = jax.nn.silu(jnp.dot(spectrum, w_time, precision=highest))
    return jnp.dot(hidden_time, w_ada, precision=highest).reshape(8, -1)

def sequence_loss(params, x_clean, slot_list, segment, level):
    embedding, head_table, w_time, w_ada, norm_gains, w_qkv, w_out, w_up, w_down = params
    positions = jnp.arange(LEN)
    masked = jnp.any(slot_list[:, None] == positions[None, :], axis=0)
    noisy = jnp.where(masked, VOCAB - 1, x_clean)
    hidden_start = low_back(embedding[noisy])
    modulation = condition(w_time, w_ada, features(level, FREQ))
    normed_a = low(norm_mod(hidden_start, norm_gains[0], modulation[0], modulation[1]))
    triple = low(low_back(jnp.dot(normed_a, w_qkv, precision=highest))).reshape(LEN, 3, HEADS, HEAD_DIM)
    scores = low_back(jnp.einsum('qhd,khd->hqk', triple[:, 0], triple[:, 1], precision=highest) * HEAD_DIM ** (-0.5))
    same_doc = segment[:, None] == segment[None, :]
    scores = jnp.where(same_doc[None], scores, -1e+30)
    probs = low(jax.nn.softmax(scores, axis=-1))
    attended = jnp.einsum('hqk,khd->qhd', probs, triple[:, 2], precision=highest).reshape(LEN, D)
    attended = low(low_back(attended))
    branch_a = low_back(jnp.dot(attended, w_out, precision=highest))
    hidden_mid = hidden_start + modulation[2] * branch_a
    normed_b = low(norm_mod(hidden_mid, norm_gains[1], modulation[3], modulation[4]))
    up_values = low_back(jnp.dot(normed_b, w_up, precision=highest))
    active = low(jax.nn.gelu(up_values, approximate=True))
    branch_m = low_back(jnp.dot(active, w_down, precision=highest))
    hidden_end = hidden_mid + modulation[5] * branch_m
    final_rows = norm_mod(hidden_end, norm_gains[2], modulation[6], modulation[7])
    spots = jnp.minimum(slot_list, LEN - 1)
    live = (slot_list < LEN).astype(jnp.float32)
    picked = low(final_rows[spots])
    logits = low_back(jnp.dot(picked, head_table, precision=highest))
    logits = jnp.where((jnp.arange(VP) < VOCAB)[None, :], logits, -1e+30)
    log_probs = jax.nn.log_softmax(logits, axis=-1)
    targets = x_clean[spots]
    chosen = jnp.take_along_axis(log_probs, targets[:, None], 1)[:, 0]
    return jnp.sum(nelbo_weight(level) * live * -chosen)

def reference(x_clean, mask_index, segment_ids, noise_level, embedding, head_table, w_time, w_ada, norm_gains, w_qkv, w_out, w_up, w_down, moment_embedding, moment_head_table, moment_w_time, moment_w_ada, moment_norm_gains, moment_w_qkv, moment_w_out, moment_w_up, moment_w_down, average_embedding, average_head_table, average_w_time, average_w_ada, average_norm_gains, average_w_qkv, average_w_out, average_w_up, average_w_down):
    weights = (embedding, head_table, w_time, w_ada, norm_gains, w_qkv, w_out, w_up, w_down)
    moments = (moment_embedding, moment_head_table, moment_w_time, moment_w_ada, moment_norm_gains, moment_w_qkv, moment_w_out, moment_w_up, moment_w_down)
    averages = (average_embedding, average_head_table, average_w_time, average_w_ada, average_norm_gains, average_w_qkv, average_w_out, average_w_up, average_w_down)
    masked_count = jnp.sum((mask_index < LEN).astype(jnp.float32))

    def objective(params):
        rounded = tuple((low(weight_now) for weight_now in params))

        def one_sequence(items):
            return sequence_loss(rounded, items[0], items[1], items[2], items[3])
        per_sequence = lax.map(jax.checkpoint(one_sequence), (x_clean, mask_index, segment_ids, noise_level))
        total = jnp.sum(per_sequence)
        return (total / masked_count, total)
    loss_value, back_fn, loss_sum = jax.vjp(objective, weights, has_aux=True)
    grads = back_fn(jnp.ones((), loss_value.dtype))[0]
    squares = jnp.sum(jnp.stack([jnp.sum(gradient * gradient) for gradient in grads]))
    grad_norm = jnp.sqrt(squares)
    clip_factor = jnp.minimum(1.0, clip_level / (grad_norm + 1e-06))
    new_weights = []
    new_moments = []
    new_averages = []
    for weight_place, (weight_now, moment_now, average_now, gradient) in enumerate(zip(weights, moments, averages, grads)):
        rate_now = embed_rate if weight_place == 0 else learn_rate
        clipped = gradient * clip_factor
        moment_next = momentum_rate * moment_now + clipped
        weight_next = weight_now - rate_now * (clipped + momentum_rate * moment_next)
        new_weights.append(weight_next)
        new_moments.append(moment_next)
        new_averages.append(average_rate * average_now + (1.0 - average_rate) * weight_next)
    return (*new_weights, *new_moments, *new_averages, loss_sum, masked_count, grad_norm)
```

```python
import functools

import jax
import jax.numpy as jnp
from jax import lax
from jax.experimental import pallas as pl
from jax.experimental.pallas import tpu as pltpu
from jax.sharding import PartitionSpec as P

HEAD_DIM = 64
VOCAB = 50258
FREQ = 256
FEWEST_MASKED = 32
LANES = 128


norm_epsilon = 1e-06
weight_cap = 20.0
clip_level = 1.0
learn_rate = 30.0
embed_rate = 2000.0
momentum_rate = 0.9
average_rate = 0.5
highest = lax.Precision.HIGHEST
low = jnp.bfloat16
wide = jnp.float32


class Links:
    def __init__(self, dp_count, vocab_count):
        core = 2 if vocab_count % 2 == 0 else 1
        side = 1
        while side * side < dp_count:
            side *= 2
        self.dp_count, self.vocab_count = dp_count, vocab_count
        self.axes = {
            "u": ("dp", side, dp_count // side),
            "v": ("dp", 1, side),
            "z": ("vocab", core, vocab_count // core),
            "c": ("vocab", 1, core),
            "dp": ("dp", 1, dp_count),
        }

    def size(self, axis):
        return self.axes[axis][2]

    def place(self, axis):
        group, unit, size = self.axes[axis]
        return (lax.axis_index(group) // unit) % size

    def hop(self, value, axis, step):
        group, unit, _ = self.axes[axis]
        flip = step * unit
        across, along = (flip, 0) if group == "dp" else (0, flip)
        pairs = [
            (d * self.vocab_count + w, (d ^ across) * self.vocab_count + (w ^ along))
            for d in range(self.dp_count)
            for w in range(self.vocab_count)
        ]
        return lax.ppermute(value, ("dp", "vocab"), pairs)

    def heard(self, value, axis):
        return [value] + [self.hop(value, axis, k) for k in range(1, self.size(axis))]

    def ordered(self, pieces, axis):
        place, count = self.place(axis), len(pieces)
        slots = []
        for slot in range(count):
            value = pieces[slot]
            for other in range(1, count):
                value = jnp.where(place == other, pieces[slot ^ other], value)
            slots.append(value)
        return slots

    def stack(self, value, axis):
        return jnp.stack(self.ordered(self.heard(value, axis), axis))

    def fold(self, value, axis, dim):
        place, count = self.place(axis), self.size(axis)
        own = lax.dynamic_index_in_dim(value, place, dim, keepdims=False)
        total = own.astype(wide)
        for k in range(1, count):
            part = lax.dynamic_index_in_dim(value, place ^ k, dim, keepdims=False)
            total = total + self.hop(part, axis, k).astype(wide)
        return total

    def stack_all_small(self, value):
        shape = value.shape
        value = self.stack(value, "z")
        value = self.stack(value, "dp")
        value = self.stack(value, "c")
        value = jnp.moveaxis(value, 0, 2)
        return value.reshape((self.dp_count * self.vocab_count,) + shape)

    def stack_all(self, value, cut):
        rows, width = value.shape
        value = self.stack(value, "z")
        left, right = value[..., :cut], value[..., cut:]
        left = self.stack(self.stack(left, "v"), "u")
        if cut == width:
            return jnp.stack(self.ordered(self.heard(left, "c"), "c"), 3).reshape(-1, width)
        right = jnp.swapaxes(self.stack(self.stack(right, "u"), "v"), 0, 1)
        parts = [jnp.stack(self.ordered(self.heard(part, "c"), "c"), 3) for part in (left, right)]
        return jnp.concatenate(parts, -1).reshape(-1, width)

    def fold_all(self, value, cut):
        rows, width = value.shape
        value = value.reshape(
            self.size("u"), self.size("v"), self.size("z"), self.size("c"), -1, width
        )
        value = self.fold(value, "c", 3).astype(low)
        left, right = value[..., :cut], value[..., cut:]
        left = self.fold(self.fold(left, "u", 0).astype(low), "v", 0)
        right = self.fold(self.fold(right, "v", 1).astype(low), "u", 0)
        value = jnp.concatenate([left, right], -1).astype(low)
        return self.fold(value, "z", 0)

    def exchange(self, pieces):
        came = [pieces(0)] + [self.hop(pieces(k), "dp", k) for k in range(1, self.dp_count)]
        return self.ordered(came, "dp")

    def total(self, value, join):
        for axis in ("z", "dp", "c"):
            value = join(self.heard(value, axis))
        return value


def half_cut(width):
    return max(LANES, (width // (2 * LANES)) * LANES) if width > LANES else width


def features(level, freq_count):
    sigma_level = -jnp.log1p(-(1.0 - 0.001) * level)
    half_count = freq_count // 2
    frequency = jnp.exp(-jnp.log(10000.0) * jnp.arange(half_count, dtype=wide) / half_count)
    angles = sigma_level[..., None] * frequency
    return jnp.concatenate([jnp.cos(angles), jnp.sin(angles)], -1)


def nelbo_weight(level):
    sigma_level = -jnp.log1p(-(1.0 - 0.001) * level)
    rate_value = (1.0 - 0.001) / (1.0 - (1.0 - 0.001) * level)
    return jnp.minimum(rate_value / jnp.expm1(sigma_level), weight_cap)


def norm_mod(values, gain_row, shift_row, scale_row):
    center = values - jnp.mean(values, -1, keepdims=True)
    spread = jnp.mean(center * center, -1, keepdims=True)
    return center * lax.rsqrt(spread + norm_epsilon) * gain_row * (1.0 + scale_row) + shift_row


def times_rows(left_matrix, right_matrix):
    return lax.dot_general(
        left_matrix, right_matrix, (((0,), (0,)), ((), ())), preferred_element_type=wide
    )


def times_transposed(left_matrix, right_matrix):
    return lax.dot_general(
        left_matrix, right_matrix, (((1,), (1,)), ((), ())), preferred_element_type=wide
    )


def look_up_kernel(kept, first_ref, last_ref, base_ref, ids_ref, table_ref, out_ref, rows_ref):
    rows_ref[...] = jnp.zeros_like(rows_ref)
    base = base_ref[0]

    def one_sequence(s, carry):
        first, last = first_ref[s], last_ref[s]

        def some(i, inner):
            for q in range(4):
                at = s * kept + jnp.minimum(first + 4 * i + q, last - 1)
                row = ids_ref[at] - base
                rows_ref[pl.ds(at, 1), :] = table_ref[pl.ds(row, 1), :]
            return inner

        return lax.fori_loop(0, (last - first + 3) // 4, some, carry)

    lax.fori_loop(0, first_ref.shape[0], one_sequence, 0)
    out_ref[...] = rows_ref[...].astype(out_ref.dtype)


def look_up(first, last, base, ids, table, kept):
    count, width = ids.shape[0], table.shape[1]
    smem = pl.BlockSpec(memory_space=pltpu.SMEM)
    vmem = pl.BlockSpec(memory_space=pltpu.VMEM)
    return pl.pallas_call(
        functools.partial(look_up_kernel, kept),
        out_shape=jax.ShapeDtypeStruct((count, width), low),
        in_specs=[smem, smem, smem, smem, vmem],
        out_specs=vmem,
        scratch_shapes=[pltpu.VMEM((count, width), wide)],
        compiler_params=pltpu.CompilerParams(vmem_limit_bytes=56 * 2**20),
    )(first, last, base, ids, table)


def add_up_kernel(kept, first_ref, last_ref, base_ref, ids_ref, grad_ref, out_ref, sum_ref):
    span = out_ref.shape[1]
    sum_ref[...] = jnp.zeros_like(sum_ref)
    base = base_ref[0]

    def one_sequence(s, carry):
        first, last = first_ref[s], last_ref[s]

        def some(i, inner):
            for q in range(4):
                k = first + 4 * i + q
                at = s * kept + jnp.minimum(k, last - 1)
                row = jnp.where(k < last, ids_ref[at] - base, span)
                sum_ref[pl.ds(row, 1), :] = sum_ref[pl.ds(row, 1), :] + grad_ref[pl.ds(at, 1), :]
            return inner

        return lax.fori_loop(0, (last - first + 3) // 4, some, carry)

    lax.fori_loop(0, first_ref.shape[0], one_sequence, 0)
    whole = span // LANES

    def turn(b, carry):
        at = pl.multiple_of(b * LANES, LANES)
        out_ref[:, pl.ds(at, LANES)] = sum_ref[pl.ds(at, LANES), :].T
        return carry

    lax.fori_loop(0, whole, turn, 0)
    if span > whole * LANES:
        rest = span - whole * LANES
        out_ref[:, whole * LANES :] = sum_ref[whole * LANES : (whole + 1) * LANES, :].T[:, :rest]


def add_up(first, last, base, ids, grads, span, kept):
    count, width = grads.shape
    smem = pl.BlockSpec(memory_space=pltpu.SMEM)
    vmem = pl.BlockSpec(memory_space=pltpu.VMEM)
    padded = (span // LANES + 1) * LANES
    return pl.pallas_call(
        functools.partial(add_up_kernel, kept),
        out_shape=jax.ShapeDtypeStruct((width, span), wide),
        in_specs=[smem, smem, smem, smem, vmem],
        out_specs=vmem,
        scratch_shapes=[pltpu.VMEM((padded, width), wide)],
        compiler_params=pltpu.CompilerParams(vmem_limit_bytes=56 * 2**20),
    )(first, last, base, ids, grads)


def attend(queries, keys_all, values_all, segment):
    factor = HEAD_DIM ** (-0.5)
    scores = jnp.einsum("qhd,khd->hqk", queries, keys_all, preferred_element_type=wide) * factor
    scores = jnp.where((segment[:, None] == segment[None, :])[None], scores, -1e30)
    peak_value = jnp.max(scores, -1, keepdims=True)
    expo = jnp.exp(scores - peak_value)
    probs = expo / jnp.sum(expo, -1, keepdims=True)
    result = jnp.einsum("hqk,khd->qhd", probs.astype(low), values_all, preferred_element_type=wide)
    return result.reshape(queries.shape[0], -1), probs


def attend_back(queries, keys_all, values_all, probs, grad_attended):
    factor = HEAD_DIM ** (-0.5)
    grad_values = jnp.einsum(
        "hqk,qhd->khd", probs.astype(low), grad_attended, preferred_element_type=wide
    )
    grad_probs = jnp.einsum("qhd,khd->hqk", grad_attended, values_all, preferred_element_type=wide)
    grad_scores = (probs * (grad_probs - jnp.sum(probs * grad_probs, -1, keepdims=True))).astype(
        low
    )
    grad_query = (
        jnp.einsum("hqk,khd->qhd", grad_scores, keys_all, preferred_element_type=wide) * factor
    )
    grad_keys = (
        jnp.einsum("hqk,qhd->khd", grad_scores, queries, preferred_element_type=wide) * factor
    )
    return (grad_query, grad_keys, grad_values)


def layer_forward(weights, gains, hidden_start, modulation, segment):
    total_rows, model_width = hidden_start.shape
    head_count = model_width // HEAD_DIM
    normed_a = norm_mod(hidden_start, gains[0], modulation[0], modulation[1]).astype(low)
    triple = jnp.dot(normed_a, weights["qkv"], preferred_element_type=wide).astype(low)
    triple = triple.reshape(total_rows, 3, head_count, HEAD_DIM)
    attended, probs = attend(triple[:, 0], triple[:, 1], triple[:, 2], segment)
    attended = attended.astype(low)
    branch_a = jnp.dot(attended, weights["out"], preferred_element_type=wide)
    hidden_mid = hidden_start + modulation[2] * branch_a
    normed_b = norm_mod(hidden_mid, gains[1], modulation[3], modulation[4]).astype(low)
    up_values = jnp.dot(normed_b, weights["up"], preferred_element_type=wide)
    active = jax.nn.gelu(up_values, approximate=True).astype(low)
    branch_m = jnp.dot(active, weights["down"], preferred_element_type=wide)
    hidden_end = hidden_mid + modulation[5] * branch_m
    final_rows = norm_mod(hidden_end, gains[2], modulation[6], modulation[7])
    kept = (
        normed_a,
        triple,
        attended,
        probs,
        branch_a,
        hidden_mid,
        normed_b,
        up_values,
        active,
        branch_m,
        hidden_end,
    )
    return (final_rows, kept)


def layer_backward(weights, gains, hidden_start, modulation, kept, grad_final):
    (
        normed_a,
        triple,
        attended,
        probs,
        branch_a,
        hidden_mid,
        normed_b,
        up_values,
        active,
        branch_m,
        hidden_end,
    ) = kept
    total_rows = hidden_start.shape[0]
    _, back_third = jax.vjp(norm_mod, hidden_end, gains[2], modulation[6], modulation[7])
    grad_end, grad_gain3, grad_shift3, grad_scale3 = back_third(grad_final)
    grad_gate2 = jnp.sum(grad_end * branch_m, 0)
    grad_branch_m = (modulation[5] * grad_end).astype(low)
    grad_down = times_rows(active, grad_branch_m).astype(low)
    grad_active = times_transposed(grad_branch_m, weights["down"])
    _, back_gelu = jax.vjp(lambda inputs: jax.nn.gelu(inputs, approximate=True), up_values)
    grad_upper = back_gelu(grad_active)[0].astype(low)
    grad_up = times_rows(normed_b, grad_upper).astype(low)
    grad_normed_b = times_transposed(grad_upper, weights["up"])
    _, back_second = jax.vjp(norm_mod, hidden_mid, gains[1], modulation[3], modulation[4])
    grad_mid_norm, grad_gain2, grad_shift2, grad_scale2 = back_second(grad_normed_b)
    grad_mid = grad_end + grad_mid_norm
    grad_gate1 = jnp.sum(grad_mid * branch_a, 0)
    grad_branch_a = (modulation[2] * grad_mid).astype(low)
    grad_out = times_rows(attended, grad_branch_a).astype(low)
    grad_attended = times_transposed(grad_branch_a, weights["out"]).astype(low)
    grad_attended = grad_attended.reshape(total_rows, triple.shape[2], HEAD_DIM)
    grad_query, grad_keys, grad_values = attend_back(
        triple[:, 0], triple[:, 1], triple[:, 2], probs, grad_attended
    )
    grad_triple = (
        jnp.stack([grad_query, grad_keys, grad_values], 1).reshape(total_rows, -1).astype(low)
    )
    grad_qkv = times_rows(normed_a, grad_triple).astype(low)
    grad_normed_a = times_transposed(grad_triple, weights["qkv"])
    _, back_first = jax.vjp(norm_mod, hidden_start, gains[0], modulation[0], modulation[1])
    grad_start_norm, grad_gain1, grad_shift1, grad_scale1 = back_first(grad_normed_a)
    grad_start = grad_mid + grad_start_norm
    grad_mod = jnp.concatenate(
        [
            grad_shift1,
            grad_scale1,
            grad_gate1,
            grad_shift2,
            grad_scale2,
            grad_gate2,
            grad_shift3,
            grad_scale3,
        ]
    )
    grad_gains = jnp.concatenate([grad_gain1, grad_gain2, grad_gain3])
    grads = {"qkv": grad_qkv, "out": grad_out, "up": grad_up, "down": grad_down}
    return (grad_start, grad_mod, grad_gains, grads)


def advance(weight_now, moment_now, average_now, gradient, clip_factor, rate_now):
    clipped = gradient * clip_factor
    moment_next = momentum_rate * moment_now + clipped
    weight_next = weight_now - rate_now * (clipped + momentum_rate * moment_next)
    return (
        weight_next,
        moment_next,
        average_rate * average_now + (1.0 - average_rate) * weight_next,
    )


def padded_rows(value, rows_of):
    size = value.shape[0]
    rows = -(-size // (rows_of * LANES)) * rows_of
    return jnp.pad(value, (0, rows * LANES - size)).reshape(rows, LANES)


def join_stats(pieces):
    peak_value = functools.reduce(jnp.maximum, [piece[0] for piece in pieces])
    summed = sum(piece[1] * jnp.exp(piece[0] - peak_value) for piece in pieces)
    return jnp.stack([peak_value, summed, sum(piece[2] for piece in pieces)])


def shards(
    x_clean,
    mask_index,
    segment_ids,
    noise_level,
    embedding,
    head_table,
    w_time,
    w_ada,
    norm_gains,
    w_qkv,
    w_out,
    w_up,
    w_down,
    *states,
):
    vocab_index = lax.axis_index("vocab")
    dp_index = lax.axis_index("dp")
    vocab_count = lax.axis_size("vocab")
    dp_count = lax.axis_size("dp")
    links = Links(dp_count, vocab_count)
    device_count = dp_count * vocab_count
    device_index = dp_index * vocab_count + vocab_index
    length = x_clean.shape[1]
    slot_count = mask_index.shape[1]
    kept_count = length - FEWEST_MASKED
    span = embedding.shape[0]
    columns = head_table.shape[1]
    slice_width = embedding.shape[1]
    model_width = slice_width * dp_count
    cond_width = w_time.shape[1]
    mask_id = VOCAB - 1

    positions = jnp.arange(length)
    own_slots = mask_index[0]
    hit = own_slots[:, None] == positions[None, :]
    masked = jnp.any(hit, axis=0)
    sort_key = jnp.where(masked, mask_id, x_clean[0]) * length + positions
    rank = jnp.sum((sort_key[None, :] < sort_key[:, None]).astype(jnp.int32), 1)
    to_sorted = rank[:, None] == jnp.arange(kept_count)[None, :]
    sorted_ids = jnp.sum(jnp.where(to_sorted, sort_key[:, None], 0), 0) // length
    spots = jnp.minimum(own_slots, length - 1)
    at_spot = spots[:, None] == positions[None, :]
    targets_own = jnp.sum(jnp.where(at_spot, x_clean[0][None, :], 0), 1)
    targets_own = jnp.where(own_slots < length, targets_own, -1)
    numbers = links.stack_all_small(
        padded_rows(jnp.concatenate([sorted_ids, targets_own]), 1)
    ).reshape(device_count, -1)
    ids_all = numbers[:, :kept_count]
    targets = numbers[:, kept_count : kept_count + slot_count].reshape(-1)
    live = (targets >= 0).astype(wide)
    masked_count = jnp.sum(live)

    level = lax.dynamic_index_in_dim(noise_level, vocab_index, keepdims=False)
    mask_local = mask_id - vocab_index * span
    mask_owner = (mask_local >= 0) & (mask_local < span)
    table_flat = embedding.T
    mask_row = lax.dynamic_index_in_dim(
        table_flat, jnp.clip(mask_local, 0, span - 1), 1, keepdims=False
    )
    mask_row = jnp.where(mask_owner, mask_row, 0.0)
    sizes = (w_time.size, norm_gains.size, slice_width, 1)
    small = jnp.concatenate(
        [w_time.reshape(-1), norm_gains.reshape(-1), mask_row]
    ).astype(low).astype(wide)
    small = links.stack_all_small(
        padded_rows(jnp.concatenate([small, level[None]]), 8)
    ).reshape(device_count, -1)
    starts = [sum(sizes[:n]) for n in range(5)]
    time_weight, gains_all, mask_rows, levels = [
        small[:, starts[n] : starts[n + 1]] for n in range(4)
    ]
    time_weight = time_weight.reshape(-1, cond_width)
    gains = jnp.swapaxes(gains_all.reshape(device_count, 3, -1), 0, 1).reshape(3, model_width)
    mask_row_full = jnp.sum(mask_rows.reshape(dp_count, vocab_count, slice_width), 1).reshape(-1)
    levels = levels[:, 0]

    first = jnp.sum((ids_all < vocab_index * span).astype(jnp.int32), 1)
    stop_id = jnp.minimum((vocab_index + 1) * span, mask_id)
    last = jnp.maximum(jnp.sum((ids_all < stop_id).astype(jnp.int32), 1), first)
    base = (vocab_index * span)[None].astype(jnp.int32)
    flat_ids = ids_all.reshape(-1)
    looked = look_up(first, last, base, flat_ids, embedding, kept_count)
    looked = looked.reshape(
        dp_count, links.size("z"), links.size("c"), kept_count, slice_width
    )
    looked = links.fold(looked, "c", 2).astype(low)
    looked = links.fold(looked, "z", 1).astype(low)
    looked = links.exchange(
        lambda k: lax.dynamic_index_in_dim(looked, dp_index ^ k, 0, keepdims=False)
    )
    looked = jnp.concatenate(looked, 1)
    spread = to_sorted.astype(low)
    hidden_start = jnp.dot(spread, looked, preferred_element_type=wide)
    hidden_start = jnp.where(masked[:, None], mask_row_full[None, :], hidden_start)

    shard_of = {"ada": w_ada.T, "qkv": w_qkv, "out": w_out, "up": w_up, "down": w_down}
    cut_of = {name: half_cut(shard.shape[1]) for name, shard in shard_of.items()}
    weights = {
        name: links.stack_all(shard.astype(low), cut_of[name]) for name, shard in shard_of.items()
    }
    piece = -(-columns // (dp_count * LANES)) * LANES
    head_low = jnp.pad(head_table.astype(low), ((0, 0), (0, piece * dp_count - columns)))
    head_columns = jnp.concatenate(
        links.exchange(
            lambda k: lax.dynamic_slice_in_dim(head_low, (dp_index ^ k) * piece, piece, 1)
        ),
        0,
    )

    ada_weight = weights["ada"].astype(wide)
    spectrum_all = features(levels, FREQ)
    spectrum = features(level[None], FREQ)
    before_time = jnp.dot(spectrum, time_weight, precision=highest)
    hidden_time, back_silu = jax.vjp(jax.nn.silu, before_time)
    modulation = lax.dot_general(
        hidden_time, ada_weight, (((1,), (1,)), ((), ())), precision=highest
    ).reshape(8, -1)
    segment = segment_ids[0]
    final_rows, kept = layer_forward(weights, gains, hidden_start, modulation, segment)

    picked = jnp.dot(
        at_spot.astype(low), final_rows.astype(low), preferred_element_type=wide
    ).astype(low)
    rows_all = links.stack_all(picked, half_cut(model_width))
    logits = jnp.dot(rows_all, head_columns, preferred_element_type=wide)
    local_columns = jnp.arange(piece)
    own_columns = dp_index * piece + local_columns
    inside = (own_columns < columns) & (vocab_index * columns + own_columns < VOCAB)
    logits = jnp.where(inside[None, :], logits, -1e30)
    peak_value = jnp.max(logits, 1)
    expo_total = jnp.sum(jnp.exp(logits - peak_value[:, None]), 1)
    target_local = targets - vocab_index * columns - dp_index * piece
    onehot = (local_columns[None, :] == target_local[:, None]) & inside[None, :]
    target_logit = jnp.sum(jnp.where(onehot, logits, 0.0), 1)
    stats = jnp.stack([peak_value, expo_total, target_logit]).reshape(3, -1, LANES)
    stats = links.total(stats, join_stats).reshape(3, -1)
    log_total = stats[0] + jnp.log(stats[1])
    row_weight = jnp.repeat(nelbo_weight(levels), slot_count) * live
    loss_sum = jnp.sum(row_weight * (log_total - stats[2]))
    grad_logits = (row_weight / masked_count)[:, None] * (
        jnp.exp(logits - log_total[:, None]) - onehot.astype(wide)
    )
    grad_logits = grad_logits.astype(low)
    grad_rows = times_transposed(grad_logits, head_columns).astype(low)
    grad_mine = links.fold_all(grad_rows, half_cut(model_width)).astype(low)
    alive_spot = (at_spot & (own_slots < length)[:, None]).astype(low)
    grad_final = times_rows(alive_spot, grad_mine)
    grad_head = times_rows(rows_all, grad_logits).astype(low)
    grad_head = grad_head.reshape(dp_count, slice_width, piece)
    grad_head = jnp.concatenate(
        links.exchange(
            lambda k: lax.dynamic_index_in_dim(grad_head, dp_index ^ k, 0, keepdims=False)
        ),
        1,
    )[:, :columns].astype(wide)

    grad_start, grad_mod, grad_gains, layer_grads = layer_backward(
        weights, gains, hidden_start, modulation, kept, grad_final
    )
    layer_grads = {
        name: links.fold_all(grad, cut_of[name]) for name, grad in layer_grads.items()
    }

    start_low = grad_start.astype(low)
    mask_grad = jnp.sum(jnp.where(masked[:, None], start_low.astype(wide), 0.0), 0)
    sent = times_rows(spread, start_low).astype(low).reshape(kept_count, dp_count, slice_width)
    came = jnp.stack(
        links.exchange(
            lambda k: lax.dynamic_index_in_dim(sent, dp_index ^ k, 1, keepdims=False)
        )
    )
    came = links.stack(links.stack(came, "z"), "c")
    came = came.transpose(2, 1, 0, 3, 4).reshape(-1, slice_width)
    grad_table = add_up(first, last, base, flat_ids, came.astype(wide), span, kept_count)

    grad_hidden_time = jnp.dot(grad_mod[None, :], ada_weight, precision=highest)
    grad_before = back_silu(grad_hidden_time)[0]
    parts = (hidden_time[0], grad_before[0], mask_grad, grad_gains, grad_mod)
    part_sizes = [part.shape[0] for part in parts]
    part_starts = [sum(part_sizes[:n]) for n in range(len(parts) + 1)]
    vectors = links.stack_all_small(padded_rows(jnp.concatenate(parts), 8)).reshape(
        device_count, -1
    )
    hidden_time_all, grad_before_all, mask_grads, gains_each, mods_each = [
        vectors[:, part_starts[n] : part_starts[n + 1]] for n in range(len(parts))
    ]
    time_rows = w_time.shape[0]
    grad_time = lax.dot_general(
        lax.dynamic_slice_in_dim(spectrum_all, device_index * time_rows, time_rows, 1),
        grad_before_all,
        (((0,), (0,)), ((), ())),
        precision=highest,
    )
    ada_columns = w_ada.shape[1]
    grad_ada = lax.dot_general(
        lax.dynamic_slice_in_dim(mods_each, device_index * ada_columns, ada_columns, 1),
        hidden_time_all,
        (((0,), (0,)), ((), ())),
        precision=highest,
    )
    gain_columns = norm_gains.shape[1]
    grad_gain_rows = lax.dynamic_slice_in_dim(
        jnp.sum(gains_each, 0).reshape(3, model_width), device_index * gain_columns, gain_columns, 1
    )
    mask_grad_own = lax.dynamic_slice_in_dim(
        jnp.sum(mask_grads, 0), dp_index * slice_width, slice_width, 0
    )
    mask_column = (jnp.arange(span) == mask_local)[None, :]
    grad_table = grad_table + jnp.where(mask_column, mask_grad_own[:, None], 0.0)

    grads_all = (
        grad_table,
        grad_head,
        grad_time,
        grad_ada,
        grad_gain_rows,
        layer_grads["qkv"],
        layer_grads["out"],
        layer_grads["up"],
        layer_grads["down"],
    )
    squares = sum(jnp.sum(gradient * gradient) for gradient in grads_all)
    square_total = links.total(jnp.broadcast_to(squares, (8, LANES)), sum)[0, 0]
    grad_norm = jnp.sqrt(square_total)
    clip_factor = jnp.minimum(1.0, clip_level / (grad_norm + 1e-06))
    weights_now = (embedding, head_table, w_time, w_ada, norm_gains, w_qkv, w_out, w_up, w_down)
    turned = (0, 3)
    updated = []
    for place, (weight_now, gradient) in enumerate(zip(weights_now, grads_all)):
        state = (weight_now, states[place], states[len(weights_now) + place])
        if place in turned:
            state = tuple(array.T for array in state)
        rate = embed_rate if place == 0 else learn_rate
        result = advance(*state, gradient, clip_factor, rate)
        if place in turned:
            result = tuple(array.T for array in result)
        updated.append(result)
    new_arrays = tuple(result[n] for n in range(3) for result in updated)
    return (*new_arrays, loss_sum, masked_count, grad_norm)


def solution(mesh):
    both = ("dp", "vocab")
    weights_placed = (
        P("vocab", "dp"),
        P("dp", "vocab"),
        P(both, None),
        P(None, both),
        P(None, both),
        P(both, None),
        P(both, None),
        P(both, None),
        P(both, None),
    )
    return jax.shard_map(
        shards,
        mesh=mesh,
        in_specs=(P(both, None), P(both, None), P(both, None), P("dp")) + 3 * weights_placed,
        out_specs=3 * weights_placed + (P(), P(), P()),
        check_vma=False,
    )
```

```python
import functools

import jax
import jax.numpy as jnp
from jax import lax
from jax.experimental import pallas as pl
from jax.experimental.pallas import tpu as pltpu
from jax.sharding import PartitionSpec as P

HEAD_DIM = 64
VOCAB = 50258
FREQ = 256
FEWEST_MASKED = 32
LANES = 128


norm_epsilon = 1e-06
weight_cap = 20.0
clip_level = 1.0
learn_rate = 30.0
embed_rate = 2000.0
momentum_rate = 0.9
average_rate = 0.5
highest = lax.Precision.HIGHEST
low = jnp.bfloat16
wide = jnp.float32


def tie(*values):
    return lax.optimization_barrier(values)


class Links:
    def __init__(self, dp_count, vocab_count):
        core = 2 if vocab_count % 2 == 0 else 1
        side = 1
        while side * side < dp_count:
            side *= 2
        self.dp_count, self.vocab_count = dp_count, vocab_count
        self.axes = {
            "u": ("dp", side, dp_count // side),
            "v": ("dp", 1, side),
            "z": ("vocab", core, vocab_count // core),
            "c": ("vocab", 1, core),
            "dp": ("dp", 1, dp_count),
        }

    def size(self, axis):
        return self.axes[axis][2]

    def place(self, axis):
        group, unit, size = self.axes[axis]
        return (lax.axis_index(group) // unit) % size

    def hop(self, value, axis, step):
        group, unit, _ = self.axes[axis]
        flip = step * unit
        across, along = (flip, 0) if group == "dp" else (0, flip)
        pairs = [
            (d * self.vocab_count + w, (d ^ across) * self.vocab_count + (w ^ along))
            for d in range(self.dp_count)
            for w in range(self.vocab_count)
        ]
        return lax.ppermute(value, ("dp", "vocab"), pairs)

    def heard(self, value, axis):
        return [value] + [self.hop(value, axis, k) for k in range(1, self.size(axis))]

    def ordered(self, pieces, axis):
        place, count = self.place(axis), len(pieces)
        slots = []
        for slot in range(count):
            value = pieces[slot]
            for other in range(1, count):
                value = jnp.where(place == other, pieces[slot ^ other], value)
            slots.append(value)
        return slots

    def near(self, value, axis):
        return [value[0]] + [self.hop(value[k], axis, k) for k in range(1, self.size(axis))]

    def piled(self, pieces, axis, dim=0):
        return jnp.stack(self.ordered(pieces, axis), dim)

    def own(self, value, axis, dim=0):
        return lax.dynamic_index_in_dim(value, self.place(axis), dim, keepdims=False)

    def given(self, value, axis, dim=0):
        place = self.place(axis)
        return [
            self.hop(lax.dynamic_index_in_dim(value, place ^ k, dim, keepdims=False), axis, k)
            for k in range(1, self.size(axis))
        ]

    def slot(self, n, place):
        step = n ^ place
        along = self.size("v")
        return (step % along) * self.size("u") + step // along

    def exchange(self, value):
        value = value.reshape((self.size("v"), self.size("u")) + value.shape[1:])
        return self.near(value, "v")

    def exchanged(self, came):
        pieces = [piece[0] for piece in came]
        for step in range(1, self.size("u")):
            further = self.hop(jnp.stack([piece[step] for piece in came]), "u", step)
            pieces += [further[n] for n in range(self.size("v"))]
        return pieces

    def doubled(self, value, axis):
        place, step, shape = self.place(axis), 1, value.shape
        value = value[None]
        while step < self.size(axis):
            came = self.hop(value, axis, step)
            upper = (place // step) % 2 == 1
            value = jnp.concatenate(
                [jnp.where(upper, came, value), jnp.where(upper, value, came)], 0
            )
            step *= 2
        return value.reshape((self.size(axis),) + shape)


    def half(self, value, other=False):
        width = value.shape[-1] // 2
        place = self.place("c")
        place = 1 - place if other else place
        return lax.dynamic_slice_in_dim(value, place * width, width, value.ndim - 1)

    def halves_back(self, mine, other):
        first = self.place("c") == 0
        return jnp.concatenate(
            [jnp.where(first, mine, other), jnp.where(first, other, mine)], -1
        )

    def pair_rows(self, mine, theirs):
        came = self.hop(theirs, "c", 1)
        return self.piled([mine, came], "c").reshape(-1, mine.shape[-1])

    def wide_across(self, pieces):
        block = lax.all_gather(self.piled(pieces, "z"), "dp", axis=0, tiled=False)
        return block.reshape(-1, block.shape[-1])

    def across_first(self, pieces, cut):
        block = self.piled(pieces, "z")
        return self.heard(block[..., :cut], "v"), self.heard(block[..., cut:], "u")

    def across_second(self, sides):
        return self.heard(self.piled(sides[0], "v"), "u"), self.heard(
            self.piled(sides[1], "u"), "v"
        )

    def across_done(self, sides):
        block = jnp.concatenate([self.piled(sides[0], "u"), self.piled(sides[1], "v", 1)], -1)
        return block.reshape(-1, block.shape[-1])


    def summed(self, state):
        return sum([piece.astype(wide) for piece in state[1]], state[0].astype(wide))

    def by_place(self, block):
        return block.reshape(
            self.size("u"), self.size("v"), self.size("z"), -1, block.shape[-1]
        )

    def fold_first(self, block, cut):
        left, right = block[..., :cut], block[..., cut:]
        return [
            (self.own(left, "u", 0), self.given(left, "u", 0)),
            (self.own(right, "v", 1), self.given(right, "v", 1)),
        ]

    def fold_second(self, states):
        left, right = [self.summed(state).astype(low) for state in states]
        return [
            (self.own(left, "v", 0), self.given(left, "v", 0)),
            (self.own(right, "u", 0), self.given(right, "u", 0)),
        ]

    def fold_third(self, states):
        return jnp.concatenate([self.summed(state).astype(low) for state in states], -1)

    def fold_z(self, block):
        return self.own(block, "z"), self.given(block, "z")

    def fold_across(self, block):
        block = block.reshape((self.dp_count,) + block.shape[2:])
        return lax.psum_scatter(block, "dp", scatter_dimension=0, tiled=False)

    def own_rows(self, state):
        block = state
        block = block.reshape(2, -1, block.shape[-1])
        return self.halves_back(self.own(block, "c"), self.given(block, "c")[0])

    def small_done(self, pieces):
        return self.piled(pieces, "c", 2).reshape(self.dp_count * self.vocab_count, -1)

    def total(self, value, join):
        for axis in ("z", "dp", "c"):
            value = join(self.heard(value, axis))
        return value


def half_cut(width):
    return max(LANES, (width // (2 * LANES)) * LANES) if width > LANES else width // 2


def features(level, freq_count):
    sigma_level = -jnp.log1p(-(1.0 - 0.001) * level)
    half_count = freq_count // 2
    frequency = jnp.exp(-jnp.log(10000.0) * jnp.arange(half_count, dtype=wide) / half_count)
    angles = sigma_level[..., None] * frequency
    return jnp.concatenate([jnp.cos(angles), jnp.sin(angles)], -1)


def nelbo_weight(level):
    sigma_level = -jnp.log1p(-(1.0 - 0.001) * level)
    rate_value = (1.0 - 0.001) / (1.0 - (1.0 - 0.001) * level)
    return jnp.minimum(rate_value / jnp.expm1(sigma_level), weight_cap)


def norm_mod(values, gain_row, shift_row, scale_row):
    center = values - jnp.mean(values, -1, keepdims=True)
    spread = jnp.mean(center * center, -1, keepdims=True)
    return center * lax.rsqrt(spread + norm_epsilon) * gain_row * (1.0 + scale_row) + shift_row


def times_rows(left_matrix, right_matrix):
    return lax.dot_general(
        left_matrix, right_matrix, (((0,), (0,)), ((), ())), preferred_element_type=wide
    )


def times_transposed(left_matrix, right_matrix):
    return lax.dot_general(
        left_matrix, right_matrix, (((1,), (1,)), ((), ())), preferred_element_type=wide
    )


def cost(megabytes):
    return pl.CostEstimate(flops=0, transcendentals=0, bytes_accessed=megabytes * 2**20)


def turn_kernel(in_ref, out_ref):
    out_ref[...] = in_ref[...].T


def turned(array):
    rows, columns = array.shape
    block = 8 * LANES
    return pl.pallas_call(
        turn_kernel,
        grid=(-(-columns // block),),
        out_shape=jax.ShapeDtypeStruct((columns, rows), array.dtype),
        in_specs=[pl.BlockSpec((rows, block), lambda i: (0, i))],
        out_specs=pl.BlockSpec((block, rows), lambda i: (i, 0)),
        cost_estimate=cost(24),
    )(array)


def block_of(s, grid, spot_ref):
    dp_count, z_count, core = grid
    along = lax.rem(s, z_count * core)
    across = lax.div(s, z_count * core) ^ spot_ref[0]
    deep = lax.div(along, core) ^ spot_ref[1]
    near = lax.rem(along, core) ^ spot_ref[2]
    return (near * z_count + deep) * dp_count + across


def look_up_kernel(
    grid, spot_ref, first_ref, last_ref, ids_ref, table_ref, mine_ref, theirs_ref, rows_ref, pair_ref
):
    half, width = mine_ref.shape[1], mine_ref.shape[2] // 2
    kept = 2 * half
    rows_ref[...] = jnp.zeros_like(rows_ref)
    base = spot_ref[3]

    def one_sequence(s, carry):
        first, last = first_ref[s], last_ref[s]
        to = block_of(s, grid, spot_ref) * kept

        def some(i, inner):
            places = [jnp.minimum(first + 8 * i + q, last - 1) for q in range(8)]
            found = [table_ref[pl.ds(ids_ref[s, k] - base, 1), :] for k in places]
            for k, row in zip(places, found):
                rows_ref[pl.ds(to + k, 1), :] = row
            return inner

        return lax.fori_loop(0, lax.div(last - first + 7, 8), some, carry)

    lax.fori_loop(0, first_ref.shape[0], one_sequence, 0)
    count = mine_ref.shape[0]
    for n, out_ref in enumerate((mine_ref, theirs_ref)):

        def rounded(b, carry):
            at = pl.multiple_of((n * count + b) * kept, 16)
            pair_ref[:, :width] = rows_ref[pl.ds(at, half), :]
            pair_ref[:, width:] = rows_ref[pl.ds(at + half, half), :]
            out_ref[b] = pair_ref[...].astype(out_ref.dtype)
            return carry

        lax.fori_loop(0, count, rounded, 0)


def fits(count, kept):
    return count * kept <= 16384


def by_steps(values, spot, grid):
    for axis, size in enumerate(grid):
        values = jnp.take(values, jnp.arange(size) ^ spot[axis], axis=axis)
    return values


def owned(first, last, ids):
    place = jnp.arange(ids.shape[1])[None]
    return (place >= first[:, None]) & (place < last[:, None])


def look_up_plain(spot, first, last, ids, table, grid):
    count, kept = ids.shape
    rows = table[jnp.clip(ids - spot[3], 0, table.shape[0] - 1)]
    rows = jnp.where(owned(first, last, ids)[..., None], rows, 0).astype(low)
    rows = jnp.swapaxes(rows.reshape(count, 2, kept // 2, -1), 1, 2).reshape(count, kept // 2, -1)
    rows = by_steps(rows.reshape(grid + rows.shape[1:]), spot, grid)
    rows = rows.transpose(2, 1, 0, 3, 4).reshape((2, count // 2) + rows.shape[3:])
    return rows[0], rows[1]


def add_up_plain(spot, first, last, ids, mine, theirs, span, grid):
    count, kept = ids.shape
    rows = jnp.stack([mine, theirs]).reshape(grid[::-1] + mine.shape[1:])
    rows = by_steps(rows.transpose(2, 1, 0, 3, 4), spot, grid)
    rows = jnp.swapaxes(rows.reshape(count, kept // 2, 2, -1), 1, 2).astype(wide)
    places = jnp.where(owned(first, last, ids), ids - spot[3], span).reshape(-1)
    rows = rows.reshape(count * kept, -1)
    sums = jax.ops.segment_sum(rows, places, num_segments=span + 1)[:span].T
    return sums, jnp.sum(sums * sums, 0, keepdims=True)


def look_up(spot, first, last, ids, table, grid):
    count, kept = ids.shape
    width = 2 * table.shape[1]
    if not fits(count, kept):
        return look_up_plain(spot, first, last, ids, table, grid)
    smem = pl.BlockSpec(memory_space=pltpu.SMEM)
    vmem = pl.BlockSpec(memory_space=pltpu.VMEM)
    out = jax.ShapeDtypeStruct((count // 2, kept // 2, width), low)
    return pl.pallas_call(
        functools.partial(look_up_kernel, grid),
        out_shape=(out, out),
        in_specs=[smem, smem, smem, smem, vmem],
        out_specs=(vmem, vmem),
        scratch_shapes=[
            pltpu.VMEM((count * kept, width // 2), wide),
            pltpu.VMEM((kept // 2, width), wide),
        ],
        compiler_params=pltpu.CompilerParams(vmem_limit_bytes=56 * 2**20),
        cost_estimate=cost(36),
    )(spot, first, last, ids, table)


def add_up_kernel(
    grid,
    spot_ref,
    first_ref,
    last_ref,
    ids_ref,
    mine_ref,
    theirs_ref,
    out_ref,
    square_ref,
    sum_ref,
    wide_ref,
):
    span = out_ref.shape[1]
    sum_ref[...] = jnp.zeros_like(sum_ref)
    base = spot_ref[3]
    half, width, count = mine_ref.shape[1], mine_ref.shape[2] // 2, mine_ref.shape[0]
    kept = 2 * half
    for n, in_ref in enumerate((mine_ref, theirs_ref)):

        def widen(b, carry):
            at = pl.multiple_of((n * count + b) * kept, 16)
            rows = in_ref[b].astype(wide)
            wide_ref[pl.ds(at, half), :] = rows[:, :width]
            wide_ref[pl.ds(at + half, half), :] = rows[:, width:]
            return carry

        lax.fori_loop(0, count, widen, 0)

    def one_sequence(s, carry):
        first, last = first_ref[s], last_ref[s]
        start = block_of(s, grid, spot_ref) * kept

        def some(i, inner):
            places = [first + 8 * i + q for q in range(8)]
            near = [jnp.minimum(k, last - 1) for k in places]
            rows = [
                jnp.where(k < last, ids_ref[s, m] - base, span) for k, m in zip(places, near)
            ]
            parts = [wide_ref[pl.ds(start + m, 1), :] for m in near]
            for row, part in zip(rows, parts):
                sum_ref[pl.ds(row, 1), :] = sum_ref[pl.ds(row, 1), :] + part
            return inner

        return lax.fori_loop(0, lax.div(last - first + 7, 8), some, carry)

    lax.fori_loop(0, first_ref.shape[0], one_sequence, 0)
    whole = span // LANES

    def turn(b, squares):
        at = pl.multiple_of(b * LANES, LANES)
        part = sum_ref[pl.ds(at, LANES), :].T
        out_ref[:, pl.ds(at, LANES)] = part
        return squares + jnp.sum(part * part, 0, keepdims=True)

    squares = lax.fori_loop(0, whole, turn, jnp.zeros((1, LANES), wide))
    if span > whole * LANES:
        rest = span - whole * LANES
        part = sum_ref[whole * LANES : (whole + 1) * LANES, :].T
        out_ref[:, whole * LANES :] = part[:, :rest]
        lane = lax.broadcasted_iota(jnp.int32, part.shape, 1)
        part = jnp.where(lane < rest, part, 0.0)
        squares = squares + jnp.sum(part * part, 0, keepdims=True)
    square_ref[...] = squares


def add_up(spot, first, last, ids, mine, theirs, span, grid):
    count, kept = ids.shape
    if not fits(count, kept):
        return add_up_plain(spot, first, last, ids, mine, theirs, span, grid)
    width = mine.shape[2] // 2
    smem = pl.BlockSpec(memory_space=pltpu.SMEM)
    vmem = pl.BlockSpec(memory_space=pltpu.VMEM)
    padded = (span // LANES + 1) * LANES
    return pl.pallas_call(
        functools.partial(add_up_kernel, grid),
        out_shape=(
            jax.ShapeDtypeStruct((width, span), wide),
            jax.ShapeDtypeStruct((1, LANES), wide),
        ),
        in_specs=[smem, smem, smem, smem, vmem, vmem],
        out_specs=(vmem, vmem),
        scratch_shapes=[
            pltpu.VMEM((padded, width), wide),
            pltpu.VMEM((count * kept, width), wide),
        ],
        compiler_params=pltpu.CompilerParams(vmem_limit_bytes=56 * 2**20),
        cost_estimate=cost(50),
    )(spot, first, last, ids, mine, theirs)


def pack_kernel(core_ref, *refs):
    *in_refs, mine_ref, theirs_ref = refs
    first = core_ref[0] == 0
    at = 0
    rows = mine_ref.shape[0]
    for ref, tall in in_refs_of(in_refs):
        width = ref.shape[1]
        blocks = [(n * rows, (n + 1) * rows) for n in range(ref.shape[0] // rows)]
        if tall:
            sides = [
                [(blocks[n], (0, width)) for n in range(k, k + len(blocks) // 2)]
                for k in (0, len(blocks) // 2)
            ]
        else:
            sides = [
                [(block, (k, k + width // 2)) for block in blocks] for k in (0, width // 2)
            ]
        for left, right in zip(*sides):
            values = [
                ref[row[0] : row[1], column[0] : column[1]] for row, column in (left, right)
            ]
            to = slice(at, at + values[0].shape[1])
            mine_ref[:, to] = jnp.where(first, values[0], values[1]).astype(low)
            theirs_ref[:, to] = jnp.where(first, values[1], values[0]).astype(low)
            at = to.stop


def in_refs_of(refs):
    return [(ref, n == 2) for n, ref in enumerate(refs)]


def packed(core, w_qkv, w_out, ada_turned, w_up, w_down):
    rows = w_up.shape[0]
    arrays = (w_qkv, w_out, ada_turned, w_up, w_down)
    width = sum(array.size for array in arrays) // rows // 2
    out = jax.ShapeDtypeStruct((rows, width), low)
    vmem = pl.BlockSpec(memory_space=pltpu.VMEM)
    return pl.pallas_call(
        pack_kernel,
        out_shape=(out, out),
        in_specs=[pl.BlockSpec(memory_space=pltpu.SMEM)] + [vmem] * 5,
        out_specs=(vmem, vmem),
    )(core, *arrays)


def prepare_kernel(
    mask_id,
    place_ref,
    level_ref,
    clean_ref,
    slots_ref,
    time_ref,
    gains_ref,
    mask_row_ref,
    small_ref,
    first_ref,
    second_ref,
    collect_ref,
    spot_ref,
    alive_ref,
    masked_ref,
):
    length, slots = clean_ref.shape[1], slots_ref.shape[1]
    kept = collect_ref.shape[0]

    def iota(shape, dim):
        return lax.broadcasted_iota(jnp.int32, shape, dim)

    def stood(row):
        size = row.shape[1]
        same = iota((size, size), 0) == iota((size, size), 1)
        return jnp.sum(jnp.where(same, row, 0.0), 1, keepdims=True)

    def laid(column):
        size = column.shape[0]
        same = iota((size, size), 0) == iota((size, size), 1)
        return jnp.sum(jnp.where(same, column, 0.0), 0, keepdims=True)

    clean = clean_ref[...].astype(wide)
    slot = stood(slots_ref[...].astype(wide))
    across = iota((slots, length), 1).astype(wide)
    masked = jnp.sum((across == slot).astype(wide), 0, keepdims=True)
    ids = jnp.where(masked > 0, wide(mask_id), clean)
    key = ids * length + iota((1, length), 1).astype(wide)
    key_column = stood(key)
    rank_column = jnp.sum((key < key_column).astype(wide), 1, keepdims=True)
    rank = jnp.sum((key_column < key).astype(wide), 0, keepdims=True)
    spread = (rank_column == iota((length, kept), 1).astype(wide)).astype(wide)
    half = kept // 2
    first_ref[...] = (rank_column == iota((length, half), 1).astype(wide)).astype(low)
    second_ref[...] = (rank_column == (iota((length, half), 1) + half).astype(wide)).astype(low)
    collect_ref[...] = (rank == iota((kept, length), 0).astype(wide)).astype(low)
    masked_ref[...] = stood(masked)
    at_spot = across == jnp.minimum(slot, length - 1.0)
    spot_ref[...] = at_spot.astype(low)
    alive_ref[...] = (across == slot).astype(low)
    target = jnp.sum(jnp.where(at_spot, clean, 0.0), 1, keepdims=True)
    target = laid(jnp.where(slot < length, target, -1.0))
    small_ref[...] = jnp.zeros_like(small_ref)
    small_ref[0:1, :kept] = jnp.sum(spread * stood(ids), 0, keepdims=True)
    small_ref[1:2, :slots] = target
    small_ref[2:3, :] = jnp.full((1, small_ref.shape[1]), level_ref[place_ref[0]], wide)
    small_ref[3:4, : mask_row_ref.shape[1]] = mask_row_ref[...].astype(low).astype(wide)
    small_ref[4:7, : gains_ref.shape[1]] = gains_ref[...].astype(low).astype(wide)
    small_ref[8 : 8 + time_ref.shape[0], : time_ref.shape[1]] = time_ref[...].astype(low).astype(wide)


def prepare(mask_id, place, level, clean, slots, w_time, gains, mask_row, kept):
    length, slot_count = clean.shape[1], slots.shape[1]
    smem = pl.BlockSpec(memory_space=pltpu.SMEM)
    vmem = pl.BlockSpec(memory_space=pltpu.VMEM)
    rows = 8 + -(-w_time.shape[0] // 8) * 8
    shapes = (
        ((rows, length), wide),
        ((length, kept // 2), low),
        ((length, kept // 2), low),
        ((kept, length), low),
        ((slot_count, length), low),
        ((slot_count, length), low),
        ((length, 1), wide),
    )
    return pl.pallas_call(
        functools.partial(prepare_kernel, mask_id),
        out_shape=tuple(jax.ShapeDtypeStruct(*shape) for shape in shapes),
        in_specs=[smem, smem] + [vmem] * 5,
        out_specs=(vmem,) * len(shapes),
    )(place, level, clean, slots, w_time, gains, mask_row)


def enter_kernel(first_ref, second_ref, masked_ref, mask_row_ref, *refs):
    *piece_refs, out_ref = refs
    width = piece_refs[0].shape[1] // 2
    for n, piece_ref in enumerate(piece_refs):
        at = slice(n * width, (n + 1) * width)
        left = jnp.dot(first_ref[...], piece_ref[...], preferred_element_type=wide)
        right = jnp.dot(second_ref[...], piece_ref[...], preferred_element_type=wide)
        rows = left[:, :width] + right[:, width:]
        out_ref[:, at] = rows + masked_ref[...] * mask_row_ref[:, at]


def enter(first, second, masked, mask_row, pieces):
    width = pieces[0].shape[1] // 2
    return pl.pallas_call(
        enter_kernel,
        out_shape=jax.ShapeDtypeStruct((first.shape[0], width * len(pieces)), wide),
    )(first, second, masked, mask_row[None, :], *pieces)


def tell_kernel(core_ref, sums_1, sums_2, sums_3, ada_ref, hidden_ref, before_ref, out_ref):
    sums_1, sums_2, sums_3 = sums_1[...], sums_2[...], sums_3[...]
    rows = [sums_1[n : n + 1] for n in (1, 2)] + [sums_2[n : n + 1] for n in (3, 1, 2)]
    rows += [sums_3[n : n + 1] for n in (3, 1, 2)]
    which = iota(sums_1.shape, 0)
    mods = jnp.zeros(sums_1.shape, wide)
    for n, row in enumerate(rows):
        mods = jnp.where(which == n, row, mods)
    columns, width = mods.T, mods.shape[1]
    total = jnp.zeros((8, ada_ref.shape[1]), wide)
    for n in range(8):
        part = columns[:, n : n + 1] * ada_ref[n * width : (n + 1) * width, :].astype(wide)
        total = total + jnp.sum(part.reshape(-1, 8, part.shape[1]), 0)
    slope = jnp.sum(total, 0, keepdims=True)
    before = before_ref[...]
    gate = 1.0 / (1.0 + jnp.exp(-before))
    slope = slope * (gate + before * gate * (1.0 - gate))
    out_ref[...] = jnp.zeros_like(out_ref)
    out_ref[0:8, :] = mods
    out_ref[8:12, :] = sums_1[0:4]
    out_ref[12:16, :] = sums_2[0:4]
    out_ref[16:20, :] = sums_3[0:4]
    out_ref[20:21, : slope.shape[1]] = hidden_ref[...]
    out_ref[21:22, : slope.shape[1]] = slope


def tell(sums_1, sums_2, sums_3, ada, hidden_time, before_time):
    (rows,) = kernel_call(
        tell_kernel,
        jnp.zeros((1,), jnp.int32),
        (sums_1, sums_2, sums_3, ada, hidden_time, before_time),
        (((24, sums_1.shape[1]), wide),),
    )
    return rows


def finish_kernel(
    scalar_ref, vectors_ref, spectrum_ref, ada_ref, time_ref, gains_ref, mask_ref, square_ref
):
    device, width = scalar_ref[0], vectors_ref.shape[2]
    size = ada_ref.shape[0]
    row = lax.div(device, width // size)
    mods = vectors_ref[:, 0, :]
    for n in range(1, 8):
        mods = jnp.where(row == n, vectors_ref[:, n, :], mods)

    def chosen(values, at, count):
        place = (iota((width, count), 0) == iota((width, count), 1) + at).astype(wide)
        return jnp.dot(values, place, precision=highest, preferred_element_type=wide)

    def times(left, right):
        return lax.dot_general(
            left,
            right,
            (((0,), (0,)), ((), ())),
            precision=highest,
            preferred_element_type=wide,
        )

    cond = ada_ref.shape[1]
    mods = chosen(mods, lax.rem(device, width // size) * size, size)
    ada_ref[...] = times(mods, vectors_ref[:, 20, :cond])
    time_ref[...] = times(spectrum_ref[...], vectors_ref[:, 21, :cond])
    rows = [jnp.sum(vectors_ref[:, n, :], 0, keepdims=True) for n in (8, 12, 16, 11)]
    which = iota((8, width), 0)
    block = jnp.zeros((8, width), wide)
    for n, values in enumerate(rows):
        block = jnp.where(which == n, values, block)
    gains_ref[...] = chosen(block, device * gains_ref.shape[1], gains_ref.shape[1])[:3]
    mask = chosen(block, scalar_ref[1] * mask_ref.shape[1], mask_ref.shape[1])[3:4]
    mask_ref[...] = mask * scalar_ref[2].astype(wide)
    total = sum(
        jnp.sum(jnp.sum(ref[...] * ref[...], 0, keepdims=True), 1, keepdims=True)
        for ref in (ada_ref, time_ref, gains_ref, mask_ref)
    )
    square_ref[...] = jnp.broadcast_to(total, square_ref.shape)


def finish(scalars, vectors, spectrum, ada_rows, cond, gain_width, mask_width):
    return kernel_call(
        finish_kernel,
        scalars,
        (vectors, spectrum),
        (
            ((ada_rows, cond), wide),
            ((spectrum.shape[1], cond), wide),
            ((3, gain_width), wide),
            ((1, mask_width), wide),
            ((1, LANES), wide),
        ),
    )


def laid_out(block, count, rows, width):
    parts = [
        block[:, at : at + width].reshape(count, 1, rows, width)
        for at in range(0, block.shape[1], width)
    ]
    return jnp.concatenate(parts, 1).reshape(-1, width)


def beside_blocks(block, count, rows):
    width = block.shape[1]
    block = block.reshape(count, -1, rows, width)
    return [block[:, n].reshape(count * rows, width) for n in range(block.shape[1])]


def column_of(info, n):
    return info[:, n : n + 1]


ROW_BLOCK = 256


def split_kernel(columns, place_ref, in_ref, out_ref):
    values = in_ref[...]
    column = lax.broadcasted_iota(jnp.int32, values.shape, 1)
    column = column + pl.program_id(0) * values.shape[1]
    out_ref[0] = jnp.where(column < columns, values, 0.0).astype(out_ref.dtype)


def split_head(links, place, table, piece):
    rows, columns = table.shape
    return pl.pallas_call(
        functools.partial(split_kernel, columns),
        out_shape=jax.ShapeDtypeStruct((links.dp_count, rows, piece), low),
        grid_spec=pltpu.PrefetchScalarGridSpec(
            num_scalar_prefetch=1,
            grid=(links.dp_count,),
            in_specs=[pl.BlockSpec((rows, piece), lambda i, at: (0, i))],
            out_specs=pl.BlockSpec(
                (1, rows, piece), lambda i, at: (links.slot(i, at[0]), 0, 0)
            ),
        ),
        cost_estimate=cost(8),
    )(place, table)


def stood(rows):
    which = lax.broadcasted_iota(jnp.int32, (8, rows[0].shape[1]), 0)
    block = jnp.broadcast_to(rows[0], which.shape)
    for n, row in enumerate(rows[1:]):
        block = jnp.where(which == n + 1, row, block)
    return block.T


def row_place():
    half = pl.num_programs(0) // 2
    return lambda core: lax.rem(pl.program_id(0) + core * half, 2 * half)


def logits_kernel(scalar_ref, mine_ref, theirs_ref, head_ref, info_ref, out_ref, stats_ref):
    is_mine = pl.program_id(0) < pl.num_programs(0) // 2
    block = row_place()(scalar_ref[0])
    limit = scalar_ref[1]
    rows = jnp.where(is_mine, mine_ref[...], theirs_ref[...])
    target = column_of(stood([info_ref[pl.ds(block, 1), :]]), 0).astype(jnp.int32)
    parts = []
    for at in head_parts(head_ref.shape[1]):
        values = jnp.dot(rows, head_ref[:, at], preferred_element_type=wide)
        column = lax.broadcasted_iota(jnp.int32, values.shape, 1) + at.start
        values = jnp.where(column < limit, values, -1e30)
        out_ref[:, at] = values
        found = jnp.sum(jnp.where(column == target, values, 0.0), 1, keepdims=True)
        peak = jnp.max(values, 1, keepdims=True)
        parts.append((peak, jnp.sum(jnp.exp(values - peak), 1, keepdims=True), found))
    peak = functools.reduce(jnp.maximum, [part[0] for part in parts])
    summed = sum(part[1] * jnp.exp(part[0] - peak) for part in parts)
    found = sum(part[2] for part in parts)
    lane = lax.broadcasted_iota(jnp.int32, (peak.shape[0], LANES), 1)
    columns = jnp.where(lane == 0, peak, jnp.where(lane == 1, summed, found)).T
    for n in range(3):
        stats_ref[n, pl.ds(block, 1), :] = columns[n : n + 1]


def head_parts(width):
    size = 4 * LANES
    return [slice(at, min(at + size, width)) for at in range(0, width, size)]


def head_specs(half, rows=ROW_BLOCK):
    by_step = lambda width: pl.BlockSpec((rows, width), lambda i, at: (i, 0))
    mine = lambda width: pl.BlockSpec((rows, width), lambda i, at: (jnp.minimum(i, half - 1), 0))
    theirs = lambda width: pl.BlockSpec((rows, width), lambda i, at: (jnp.maximum(i - half, 0), 0))
    whole = lambda shape: pl.BlockSpec(shape, lambda i, at: (0,) * len(shape))
    return by_step, mine, theirs, whole


def head_call(kernel, half, out_shape, in_specs, out_specs, scratch=(), cost=None):
    return pl.pallas_call(
        kernel,
        out_shape=out_shape,
        grid_spec=pltpu.PrefetchScalarGridSpec(
            num_scalar_prefetch=1,
            grid=(2 * half,),
            in_specs=in_specs,
            out_specs=out_specs,
            scratch_shapes=scratch,
        ),
        compiler_params=pltpu.CompilerParams(vmem_limit_bytes=50 * 2**20),
        cost_estimate=cost,
    )


def head_cost(rows, width, columns):
    return pl.CostEstimate(
        flops=2 * rows * width * columns,
        bytes_accessed=4 * rows * columns,
        transcendentals=rows * columns,
    )


def head_logits(scalars, mine, theirs, head, target):
    count, width = mine.shape
    half, columns = count // ROW_BLOCK, head.shape[1]
    by_step, by_mine, by_theirs, whole = head_specs(half)
    stats = (3, 2 * half, ROW_BLOCK)
    return head_call(
        logits_kernel,
        half,
        (
            jax.ShapeDtypeStruct((2 * count, columns), wide),
            jax.ShapeDtypeStruct(stats, wide),
        ),
        [by_mine(width), by_theirs(width), whole(head.shape), whole(target.shape)],
        (by_step(columns), whole(stats)),
        cost=head_cost(2 * count, width, columns),
    )(scalars, mine, theirs, head, target)


def slopes_kernel(
    scalar_ref, value_ref, head_ref, info_ref, slope_ref, mine_ref, theirs_ref
):
    block = row_place()(scalar_ref[0])
    info = stood([info_ref[n, pl.ds(block, 1), :] for n in range(3)])
    target, total, weight = [column_of(info, n) for n in range(3)]
    target = target.astype(jnp.int32)
    back = 0.0
    for at in head_parts(value_ref.shape[1]):
        values = value_ref[:, at]
        column = lax.broadcasted_iota(jnp.int32, values.shape, 1) + at.start
        odds = jnp.exp(values - total)
        slope = (jnp.where(column == target, odds - 1.0, odds) * weight).astype(low)
        slope_ref[:, at] = slope
        back = back + times_transposed(slope, head_ref[:, at])
    back = back.astype(mine_ref.dtype)
    is_mine = pl.program_id(0) < pl.num_programs(0) // 2

    @pl.when(is_mine)
    def _():
        mine_ref[...] = back

    @pl.when(jnp.logical_not(is_mine))
    def _():
        theirs_ref[...] = back


def head_slopes(scalars, values, head, info):
    count, (width, columns) = values.shape[0] // 2, head.shape
    half = count // ROW_BLOCK
    by_step, by_mine, by_theirs, whole = head_specs(half)
    return head_call(
        slopes_kernel,
        half,
        (
            jax.ShapeDtypeStruct((2 * count, columns), low),
            jax.ShapeDtypeStruct((count, width), low),
            jax.ShapeDtypeStruct((count, width), low),
        ),
        [by_step(columns), whole(head.shape), whole(info.shape)],
        (by_step(columns), by_mine(width), by_theirs(width)),
        cost=head_cost(2 * count, width, columns),
    )(scalars, values, head, info)


def head_grads_kernel(
    links, scalar_ref, mine_ref, theirs_ref, slope_ref, out_ref, square_ref, sum_ref
):
    step = pl.program_id(0)
    rows = jnp.where(step < pl.num_programs(0) // 2, mine_ref[...], theirs_ref[...])

    @pl.when(step == 0)
    def _():
        sum_ref[...] = jnp.zeros_like(sum_ref)

    for at in head_parts(slope_ref.shape[1]):
        sum_ref[:, at] += times_rows(rows, slope_ref[:, at])

    @pl.when(step == pl.num_programs(0) - 1)
    def _():
        size = out_ref.shape[1]
        squares = 0.0
        for n in range(out_ref.shape[0]):
            part = sum_ref[n * size : (n + 1) * size, :].astype(out_ref.dtype)
            out_ref[links.slot(n, scalar_ref[2])] = part
            part = part.astype(wide)
            squares = squares + jnp.sum(part * part, 0, keepdims=True)
        square_ref[...] = squares


def head_grads(links, scalars, mine, theirs, slopes):
    (count, width), columns = mine.shape, slopes.shape[1]
    rows = 3 * ROW_BLOCK if count % (3 * ROW_BLOCK) == 0 else ROW_BLOCK
    by_step, by_mine, by_theirs, whole = head_specs(count // rows, rows)
    out = (links.dp_count, width // links.dp_count, columns)
    return head_call(
        functools.partial(head_grads_kernel, links),
        count // rows,
        (jax.ShapeDtypeStruct(out, low), jax.ShapeDtypeStruct((1, columns), wide)),
        [by_mine(width), by_theirs(width), by_step(columns)],
        (whole(out), whole((1, columns))),
        [pltpu.VMEM((width, columns), wide)],
        head_cost(2 * count, width, columns),
    )(scalars, mine, theirs, slopes)


def iota(shape, dim):
    return lax.broadcasted_iota(jnp.int32, shape, dim)


def as_column(row):
    size = row.shape[1]
    same = iota((size, size), 0) == iota((size, size), 1)
    return jnp.sum(jnp.where(same, row, 0.0), 1, keepdims=True)


def kernel_call(kernel, scalar, arrays, shapes, scratch=(), megabytes=8):
    vmem = pl.BlockSpec(memory_space=pltpu.VMEM)
    out = [jax.ShapeDtypeStruct(*shape) for shape in shapes]
    return pl.pallas_call(
        kernel,
        out_shape=out,
        in_specs=[pl.BlockSpec(memory_space=pltpu.SMEM)] + [vmem] * len(arrays),
        out_specs=[vmem] * len(out),
        scratch_shapes=list(scratch),
        compiler_params=pltpu.CompilerParams(vmem_limit_bytes=50 * 2**20),
        cost_estimate=cost(megabytes),
    )(scalar, *arrays)


def part_of(core_ref, width, other=False):
    core = 1 - core_ref[0] if other else core_ref[0]
    return pl.ds(pl.multiple_of(core * width, LANES), width)


def product(core_ref, left, mine, theirs, out_ref):
    width = mine.shape[1]
    for matrix, other in ((mine, False), (theirs, True)):
        values = jnp.dot(left, matrix, preferred_element_type=wide)
        out_ref[:, part_of(core_ref, width, other)] = values.astype(out_ref.dtype)


def product_back(core_ref, slope_ref, mine, theirs):
    width = mine.shape[1]
    return times_transposed(slope_ref[:, part_of(core_ref, width)], mine) + times_transposed(
        slope_ref[:, part_of(core_ref, width, True)], theirs
    )


def norm_parts(values):
    center = values - jnp.mean(values, -1, keepdims=True)
    spread = jnp.mean(center * center, -1, keepdims=True)
    factor = lax.rsqrt(spread + norm_epsilon)
    return center * factor, factor


def norm_rows(values, mods, gains, n, shift):
    hat, _ = norm_parts(values)
    gain, at = gains[n : n + 1, :], slice(shift + 1, shift + 2)
    return hat * gain * (1.0 + mods[at, :]) + mods[shift : shift + 1, :]


def norm_back(values, slope, mods, gains, n, shift):
    hat, factor = norm_parts(values)
    gain, scale = gains[n : n + 1, :], 1.0 + mods[shift + 1 : shift + 2, :]
    along = jnp.sum(slope * hat, 0, keepdims=True)
    inner = slope * gain * scale
    inner = inner - jnp.mean(inner, -1, keepdims=True) - hat * jnp.mean(inner * hat, -1, keepdims=True)
    return inner * factor, (along * scale, jnp.sum(slope, 0, keepdims=True), along * gain)


def store_rows(out_ref, rows):
    which = iota(out_ref.shape, 0)
    block = jnp.zeros(out_ref.shape, wide)
    for n, row in enumerate(rows):
        block = jnp.where(which == n, row, block)
    out_ref[...] = block


ROOT = (2.0 / 3.141592653589793) ** 0.5


def gelu_parts(values):
    bend = jnp.tanh(ROOT * (values + 0.044715 * values * values * values))
    return 0.5 * values * (1.0 + bend), bend


def gelu_slope(values):
    _, bend = gelu_parts(values)
    inner = ROOT * (1.0 + 3.0 * 0.044715 * values * values)
    return 0.5 * (1.0 + bend) + 0.5 * values * (1.0 - bend * bend) * inner


def qkv_kernel(cut, core_ref, hidden_ref, mods, gains, mine, theirs, normed_ref, triple_ref):
    normed_ref[...] = norm_rows(hidden_ref[...], mods, gains, 0, 0).astype(low)
    product(core_ref, normed_ref[...], mine[:, :cut], theirs[:, :cut], triple_ref)


def head_pair(at, triple_ref):
    third = triple_ref.shape[1] // 3
    return [triple_ref[:, n * third + at : n * third + at + 2 * HEAD_DIM] for n in range(3)]


def head_probs(query, key, same):
    scores = times_transposed(query, key) * HEAD_DIM ** (-0.5)
    scores = jnp.where(same, scores, -1e30)
    expo = jnp.exp(scores - jnp.max(scores, -1, keepdims=True))
    return expo / jnp.sum(expo, -1, keepdims=True)


def masks_of(segment_ref, triple_ref):
    segment = segment_ref[...].astype(wide)
    same = as_column(segment) == segment
    lane = iota((triple_ref.shape[0], 2 * HEAD_DIM), 1)
    return same, (lane < HEAD_DIM, lane >= HEAD_DIM)


def attend_kernel(core_ref, triple_ref, segment_ref, out_ref):
    same, sides = masks_of(segment_ref, triple_ref)
    for at in range(0, out_ref.shape[1], 2 * HEAD_DIM):
        query, key, value = head_pair(at, triple_ref)
        results = []
        for side in sides:
            probs = head_probs(jnp.where(side, query, 0.0).astype(low), key, same)
            results.append(jnp.dot(probs.astype(low), value, preferred_element_type=wide))
        out_ref[:, at : at + 2 * HEAD_DIM] = jnp.where(sides[0], *results).astype(low)


def attend_back_kernel(core_ref, triple_ref, grad_ref, segment_ref, out_ref):
    same, sides = masks_of(segment_ref, triple_ref)
    third = triple_ref.shape[1] // 3
    factor = HEAD_DIM ** (-0.5)
    for at in range(0, third, 2 * HEAD_DIM):
        query, key, value = head_pair(at, triple_ref)
        grad = grad_ref[:, at : at + 2 * HEAD_DIM]
        queries, key_back, value_back = [], 0.0, 0.0
        for side in sides:
            own_query = jnp.where(side, query, 0.0).astype(low)
            own_grad = jnp.where(side, grad, 0.0).astype(low)
            probs = head_probs(own_query, key, same)
            value_back = value_back + times_rows(probs.astype(low), own_grad)
            slope = times_transposed(own_grad, value)
            slope = probs * (slope - jnp.sum(probs * slope, -1, keepdims=True))
            slope = slope.astype(low)
            queries.append(jnp.dot(slope, key, preferred_element_type=wide))
            key_back = key_back + times_rows(slope, own_query)
        parts = (jnp.where(sides[0], *queries) * factor, key_back * factor, value_back)
        for n, part in enumerate(parts):
            out_ref[:, n * third + at : n * third + at + 2 * HEAD_DIM] = part.astype(low)


def out_kernel(
    cuts, core_ref, attended_ref, hidden_ref, mods, gains, mine, theirs, branch_ref, mid_ref, normed_ref
):
    at = slice(*cuts)
    product(core_ref, attended_ref[...], mine[:, at], theirs[:, at], branch_ref)
    mid_ref[...] = hidden_ref[...] + mods[2:3, :] * branch_ref[...]
    normed_ref[...] = norm_rows(mid_ref[...], mods, gains, 1, 3).astype(low)


def up_kernel(core_ref, normed_ref, mine, theirs, up_ref, active_ref):
    product(core_ref, normed_ref[...], mine[...], theirs[...], up_ref)
    active_ref[...] = gelu_parts(up_ref[...])[0].astype(low)


def down_kernel(
    core_ref, active_ref, mid_ref, mods, gains, spot_ref, mine, theirs, branch_ref, end_ref, picked_ref
):
    product(core_ref, active_ref[...], mine[...], theirs[...], branch_ref)
    end_ref[...] = mid_ref[...] + mods[5:6, :] * branch_ref[...]
    final = norm_rows(end_ref[...], mods, gains, 2, 6).astype(low)
    picked_ref[...] = jnp.dot(spot_ref[...], final, preferred_element_type=wide).astype(low)


def down_back_kernel(
    core_ref,
    picked_ref,
    alive_ref,
    end_ref,
    branch_ref,
    mods,
    gains,
    up_ref,
    mine,
    theirs,
    end_back_ref,
    branch_back_ref,
    up_back_ref,
    sums_ref,
):
    slope = times_rows(alive_ref[...], picked_ref[...])
    slope, sums = norm_back(end_ref[...], slope, mods, gains, 2, 6)
    end_back_ref[...] = slope
    gate = jnp.sum(slope * branch_ref[...], 0, keepdims=True)
    store_rows(sums_ref, sums + (gate,))
    branch_back_ref[...] = (mods[5:6, :] * slope).astype(low)
    active = product_back(core_ref, branch_back_ref, mine[...], theirs[...])
    up_back_ref[...] = (active * gelu_slope(up_ref[...])).astype(low)


def up_back_kernel(
    cuts,
    core_ref,
    up_back_ref,
    mid_ref,
    end_back_ref,
    branch_ref,
    mods,
    gains,
    mine,
    theirs,
    mine_out,
    theirs_out,
    mid_back_ref,
    branch_back_ref,
    attended_back_ref,
    sums_ref,
):
    slope = product_back(core_ref, up_back_ref, mine[...], theirs[...])
    slope, sums = norm_back(mid_ref[...], slope, mods, gains, 1, 3)
    slope = end_back_ref[...] + slope
    mid_back_ref[...] = slope
    gate = jnp.sum(slope * branch_ref[...], 0, keepdims=True)
    store_rows(sums_ref, sums + (gate,))
    branch_back_ref[...] = (mods[2:3, :] * slope).astype(low)
    at = slice(*cuts)
    back = product_back(core_ref, branch_back_ref, mine_out[:, at], theirs_out[:, at])
    attended_back_ref[...] = back.astype(low)


def start_back_kernel(
    cut,
    core_ref,
    triple_back_ref,
    start_ref,
    mid_back_ref,
    mods,
    gains,
    mine,
    theirs,
    collect_ref,
    masked_ref,
    sent_ref,
    sums_ref,
    pair_ref,
):
    slope = product_back(core_ref, triple_back_ref, mine[:, :cut], theirs[:, :cut])
    slope, sums = norm_back(start_ref[...], slope, mods, gains, 0, 0)
    slope = (mid_back_ref[...] + slope).astype(low)
    mask = jnp.sum(masked_ref[...] * slope.astype(wide), 0, keepdims=True)
    store_rows(sums_ref, sums + (mask,))
    rows = jnp.dot(collect_ref[...], slope, preferred_element_type=wide)
    half, width = sent_ref.shape[1], sent_ref.shape[2] // 2
    for n in range(sent_ref.shape[0]):
        pair_ref[:, :width] = rows[:half, n * width : (n + 1) * width]
        pair_ref[:, width:] = rows[half:, n * width : (n + 1) * width]
        sent_ref[core_ref[1] ^ n] = pair_ref[...].astype(low)


def advance(weight_now, moment_now, average_now, gradient, clip_factor, rate_now):
    clipped = gradient * clip_factor
    moment_next = momentum_rate * moment_now + clipped
    weight_next = weight_now - rate_now * (clipped + momentum_rate * moment_next)
    return (
        weight_next,
        moment_next,
        average_rate * average_now + (1.0 - average_rate) * weight_next,
    )


def join_stats(pieces):
    peak_value = functools.reduce(jnp.maximum, [piece[0] for piece in pieces])
    summed = sum(piece[1] * jnp.exp(piece[0] - peak_value) for piece in pieces)
    return jnp.stack([peak_value, summed, sum(piece[2] for piece in pieces)])


def shards(
    x_clean,
    mask_index,
    segment_ids,
    noise_level,
    embedding,
    head_table,
    w_time,
    w_ada,
    norm_gains,
    w_qkv,
    w_out,
    w_up,
    w_down,
    *states,
):
    vocab_index = lax.axis_index("vocab")
    dp_index = lax.axis_index("dp")
    vocab_count = lax.axis_size("vocab")
    dp_count = lax.axis_size("dp")
    links = Links(dp_count, vocab_count)
    device_count = dp_count * vocab_count
    device_index = dp_index * vocab_count + vocab_index
    length = x_clean.shape[1]
    slot_count = mask_index.shape[1]
    kept_count = length - FEWEST_MASKED
    span = embedding.shape[0]
    columns = head_table.shape[1]
    slice_width = embedding.shape[1]
    model_width = slice_width * dp_count
    cond_width = w_time.shape[1]
    mask_id = VOCAB - 1

    place = vocab_index.astype(jnp.int32)[None]
    mask_local = mask_id - vocab_index * span
    mask_owner = (mask_local >= 0) & (mask_local < span)
    mask_row = lax.dynamic_slice_in_dim(embedding.T, jnp.clip(mask_local, 0, span - 1), 1, 1)
    mask_row = jnp.where(mask_owner, mask_row, 0.0).reshape(1, -1)
    small, first_half, second_half, collect, at_spot, alive_spot, masked = prepare(
        mask_id, place, noise_level, x_clean, mask_index, w_time, norm_gains, mask_row, kept_count
    )
    core = links.place("c").astype(jnp.int32)
    pack_mine, pack_theirs = packed(core[None], w_qkv, w_out, w_ada.T, w_up, w_down)
    pair = links.pair_rows(pack_mine, pack_theirs)
    rows = w_up.shape[0]
    qkv_width, ada_width = w_qkv.shape[1], w_ada.shape[1] // rows * cond_width
    ends = [0]
    for width in (qkv_width, model_width, ada_width, w_up.shape[1], w_down.size // rows):
        ends.append(ends[-1] + width // 2)
    pair_a, pair_bc = pair[:, : ends[3]], pair[:, ends[3] :]
    width_c = model_width // 2

    piece = -(-columns // (dp_count * LANES)) * LANES
    dp_place = dp_index.astype(jnp.int32)[None]
    small_z = links.heard(small, "z")
    head_slots = split_head(links, dp_place, head_table, piece)
    small_z, head_slots, table = tie(small_z, head_slots, embedding)
    small_dp = links.doubled(links.piled(small_z, "z"), "dp")
    a_z = links.heard(pair_a, "z")
    table = turned(table.T)
    small_dp, table, a_z = tie(small_dp, table, a_z)
    a_mine = links.wide_across(a_z)
    small_c = links.heard(small_dp, "c")
    head_came = links.exchange(head_slots)
    small_c, pair_bc = tie(small_c, pair_bc)
    bc_z = links.heard(pair_bc, "z")

    numbers = links.piled(small_c, "c", 2).reshape((device_count,) + small.shape)
    ids_all = numbers[:, 0, :kept_count].astype(jnp.int32)
    targets = numbers[:, 1, :slot_count].astype(jnp.int32)
    levels = numbers[:, 2, 0]
    mask_row_full = jnp.sum(
        numbers[:, 3, :slice_width].reshape(dp_count, vocab_count, slice_width), 1
    ).reshape(-1)
    gains = jnp.swapaxes(numbers[:, 4:7, : norm_gains.shape[1]], 0, 1).reshape(3, model_width)
    time_weight = numbers[:, 8 : 8 + w_time.shape[0], :cond_width].reshape(-1, cond_width)
    live = (targets >= 0).astype(wide)
    masked_count = jnp.sum(live)

    first = jnp.sum((ids_all < vocab_index * span).astype(jnp.int32), 1)
    stop_id = jnp.minimum((vocab_index + 1) * span, mask_id)
    last = jnp.maximum(jnp.sum((ids_all < stop_id).astype(jnp.int32), 1), first)
    spot = jnp.stack(
        [dp_index, links.place("z"), links.place("c"), vocab_index * span]
    ).astype(jnp.int32)
    grid = (dp_count, links.size("z"), links.size("c"))
    looked = look_up(spot, first, last, ids_all, table, grid)
    looked, bc_z, head_came = tie(looked, bc_z, head_came)
    looked_c = looked[0], [links.hop(looked[1], "c", 1)]
    looked = links.summed(looked_c).astype(low)
    looked = looked.reshape((grid[1], grid[0]) + looked.shape[1:])
    looked_z = links.near(looked, "z")
    half_up = w_up.shape[1] // 2
    b_first = links.across_first([piece[:, :half_up] for piece in bc_z], half_cut(half_up))
    c_mine = links.wide_across([laid_out(piece[:, half_up:], 2, rows, width_c) for piece in bc_z])

    by_core = lambda values: jnp.moveaxis(
        values.reshape(dp_count * links.size("z"), links.size("c"), -1), 1, 0
    ).reshape(-1, ROW_BLOCK)
    limit = jnp.minimum(columns, VOCAB - vocab_index * columns) - dp_index * piece
    target_local = by_core(targets) - vocab_index * columns - dp_index * piece
    target_local = jnp.where((target_local >= 0) & (target_local < limit), target_local, -1)
    target_local = target_local.astype(wide)
    row_weight = by_core(nelbo_weight(levels)[:, None] * live)
    row_share = row_weight / masked_count
    scalars = jnp.stack([core, limit.astype(jnp.int32), dp_place[0]])

    level = lax.dynamic_index_in_dim(noise_level, vocab_index, keepdims=False)
    spectrum = features(level[None], FREQ)
    before_time = jnp.dot(spectrum, time_weight, precision=highest)
    hidden_time = jax.nn.silu(before_time)
    time_rows = w_time.shape[0]
    spectrum_rows = lax.dynamic_slice_in_dim(
        features(levels, FREQ), device_index * time_rows, time_rows, 1
    )
    spectrum_rows = spectrum_rows.reshape(grid + (time_rows,))
    spectrum_rows = jnp.swapaxes(spectrum_rows, 1, 2).reshape(device_count, time_rows)
    early = (hidden_time, gains, mask_row_full, target_local, row_share, scalars, spectrum_rows)
    looked_z, early, b_first = tie(looked_z, early, b_first)
    b_second = links.across_second(b_first)
    hidden_time, gains, mask_row_full, target_local, row_share, scalars, spectrum_rows = early
    looked = links.summed((looked_z[0], looked_z[1:])).astype(low)
    looked_dp = links.near(looked, "dp")
    looked_dp, a_mine = tie(looked_dp, a_mine)
    a_other = links.hop(a_mine, "c", 1)
    hidden_start = enter(
        first_half, second_half, masked, mask_row_full, links.ordered(looked_dp, "dp")
    )

    ada_weight = links.halves_back(a_mine[:, ends[2] :], a_other[:, ends[2] :])
    ada_weight = ada_weight.reshape(device_count, rows, -1, cond_width)
    ada_weight = jnp.swapaxes(ada_weight, 1, 2).reshape(-1, cond_width)
    mods = lax.dot_general(
        hidden_time, ada_weight.astype(wide), (((1,), (1,)), ((), ())), precision=highest
    ).reshape(8, -1)
    here = jnp.stack([core, dp_place[0]])
    square, inner = (length, model_width), (length, w_up.shape[1])
    normed_a, triple = kernel_call(
        functools.partial(qkv_kernel, ends[1]),
        here,
        (hidden_start, mods, gains, a_mine, a_other),
        ((square, low), ((length, qkv_width), low)),
    )
    (attended,) = kernel_call(attend_kernel, here, (triple, segment_ids), ((square, low),))
    attended, b_second = tie(attended, b_second)
    branch_a, hidden_mid, normed_b = kernel_call(
        functools.partial(out_kernel, ends[1:3]),
        here,
        (attended, hidden_start, mods, gains, a_mine, a_other),
        ((square, wide), (square, wide), (square, low)),
    )
    b_mine = links.across_done(b_second)
    b_other = links.hop(b_mine, "c", 1)
    c_other = links.hop(c_mine, "c", 1)
    up_values, active = kernel_call(
        up_kernel, here, (normed_b, b_mine, b_other), ((inner, wide), (inner, low))
    )
    branch_m, hidden_end, picked = kernel_call(
        down_kernel,
        here,
        (active, hidden_mid, mods, gains, at_spot, c_mine, c_other),
        ((square, wide), (square, wide), ((slot_count, model_width), low)),
    )

    cut_rows = half_cut(model_width)
    picked, head_came = tie(picked, head_came)
    picked_z = links.heard(picked, "z")
    head_pieces = links.exchanged(head_came)
    picked_z, head_pieces = tie(picked_z, head_pieces)
    head = jnp.concatenate(links.ordered(head_pieces, "dp"), 0)
    rows_first = links.across_first(picked_z, cut_rows)
    rows_second = links.across_second(rows_first)
    rows_mine = links.across_done(rows_second)
    rows_theirs = links.hop(rows_mine, "c", 1)
    values, stats = head_logits(scalars, rows_mine, rows_theirs, head, target_local)
    stats = links.total(stats, join_stats)
    log_total = stats[0] + jnp.log(stats[1])
    slopes, rows_own, rows_given = head_slopes(
        scalars, values, head, jnp.stack([target_local, log_total, row_share])
    )
    loss_sum = jnp.sum(row_share * (log_total - stats[2])) * masked_count
    rows_fold = rows_own, [links.hop(rows_given, "c", 1)]
    rows_fold, slopes = tie(rows_fold, slopes)
    rows_fold = links.by_place(links.summed(rows_fold).astype(low))
    rows_fold = links.fold_first(rows_fold, cut_rows)
    grad_head, head_squares = head_grads(links, scalars, rows_mine, rows_theirs, slopes)
    rows_fold, grad_head = tie(rows_fold, grad_head)
    rows_fold = links.fold_second(rows_fold)
    rows_fold, grad_head = tie(rows_fold, grad_head)
    back_came = links.exchange(grad_head)
    grad_mine = links.summed(links.fold_z(links.fold_third(rows_fold))).astype(low)

    def weight_given(left_matrix, slopes):
        return times_rows(left_matrix, links.half(slopes, True)).astype(low)

    def weight_own(left_matrix, slopes):
        return times_rows(left_matrix, links.half(slopes))

    grad_end, grad_branch_m, grad_upper, sums_3 = kernel_call(
        down_back_kernel,
        here,
        (
            grad_mine,
            alive_spot,
            hidden_end,
            branch_m,
            mods,
            gains,
            up_values,
            c_mine,
            c_other,
        ),
        ((square, wide), (square, low), (inner, low), ((8, model_width), wide)),
        megabytes=16,
    )
    grad_upper, back_came = tie(grad_upper, back_came)
    down_came = links.hop(weight_given(active, grad_branch_m), "c", 1)
    up_came = links.hop(weight_given(normed_b, grad_upper), "c", 1)
    grad_mid, grad_branch_a, grad_attended, sums_2 = kernel_call(
        functools.partial(up_back_kernel, ends[1:3]),
        here,
        (
            grad_upper,
            hidden_mid,
            grad_end,
            branch_a,
            mods,
            gains,
            b_mine,
            b_other,
            a_mine,
            a_other,
        ),
        ((square, wide), (square, low), (square, low), ((8, model_width), wide)),
        megabytes=16,
    )
    grad_attended, down_came, up_came = tie(grad_attended, down_came, up_came)
    up_sum = (weight_own(normed_b, grad_upper) + up_came.astype(wide)).astype(low)
    down_sum = (weight_own(active, grad_branch_m) + down_came.astype(wide)).astype(low)
    layer_sum = jnp.concatenate([up_sum] + beside_blocks(down_sum, device_count, rows), 1)
    layer_wide = links.fold_across(links.by_place(layer_sum))
    (grad_triple,) = kernel_call(
        attend_back_kernel,
        here,
        (triple, grad_attended, segment_ids),
        (((length, qkv_width), low),),
        megabytes=16,
    )
    sent, sums_1 = kernel_call(
        functools.partial(start_back_kernel, ends[1]),
        here,
        (
            grad_triple,
            hidden_start,
            grad_mid,
            mods,
            gains,
            a_mine,
            a_other,
            collect,
            masked,
        ),
        (
            ((dp_count, kept_count // 2, 2 * slice_width), low),
            ((8, model_width), wide),
        ),
        [pltpu.VMEM((kept_count // 2, 2 * slice_width), wide)],
        megabytes=16,
    )

    start_dp = links.near(sent, "dp")
    a_given = [weight_given(normed_a, grad_triple), weight_given(attended, grad_branch_a)]
    a_came = links.hop(jnp.concatenate(a_given, 1), "c", 1)
    vector = tell(sums_1, sums_2, sums_3, ada_weight, hidden_time, before_time)
    vector = links.doubled(vector, "z")
    start_dp, a_came, vector = tie(start_dp, a_came, vector)
    start_z = links.heard(jnp.stack(start_dp), "z")
    a_own = [weight_own(normed_a, grad_triple), weight_own(attended, grad_branch_a)]
    a_sum = (jnp.concatenate(a_own, 1) + a_came.astype(wide)).astype(low)
    a_fold = links.fold_first(links.by_place(a_sum), half_cut(a_sum.shape[1]))
    start_z, a_fold = tie(start_z, a_fold)
    start_mine = jnp.concatenate(start_z, 0)
    start_theirs = links.hop(start_mine, "c", 1)
    a_fold = links.fold_second(a_fold)
    vector = links.heard(vector, "c")
    start_theirs, a_fold, layer_wide, back_came, vector = tie(
        start_theirs, a_fold, layer_wide, back_came, vector
    )
    vectors = links.doubled(links.piled(vector, "c"), "dp")
    vectors = vectors.reshape((device_count,) + vectors.shape[3:])
    back_pieces = links.exchanged(back_came)
    a_block = links.fold_third(a_fold)
    all_fold = links.fold_z(jnp.concatenate([a_block, layer_wide], 2))
    grad_table, table_squares = add_up(
        spot, first, last, ids_all, start_mine, start_theirs, span, grid
    )
    grad_table, all_fold, vectors, back_pieces = tie(grad_table, all_fold, vectors, back_pieces)
    all_sums = links.summed(all_fold)
    cuts = (0, a_block.shape[2], a_block.shape[2] + half_up, all_sums.shape[1])
    sum_a, sum_up, sum_down = [all_sums[:, cuts[n] : cuts[n + 1]] for n in range(3)]
    sum_down = laid_out(sum_down, 2, rows, width_c)
    sums = [sum_a, sum_up, sum_down]
    grad_a, grad_up, grad_down = [links.own_rows(block) for block in sums]
    grad_a = [grad_a[:, : grad_a.shape[1] // 2], grad_a[:, grad_a.shape[1] // 2 :]]
    grad_qkv = jnp.concatenate([side[:, : ends[1]] for side in grad_a], 1)
    grad_out = jnp.concatenate([side[:, ends[1] :] for side in grad_a], 1)
    grad_head = jnp.concatenate(links.ordered(back_pieces, "dp"), 1)[:, :columns].astype(wide)
    grad_ada, grad_time, grad_gain_rows, mask_grad_own, small_square = finish(
        jnp.stack([device_index, dp_index, mask_owner.astype(jnp.int32)]).astype(jnp.int32),
        vectors,
        spectrum_rows,
        w_ada.shape[1],
        cond_width,
        norm_gains.shape[1],
        slice_width,
    )
    mask_column = (jnp.arange(span) == mask_local)[None, :]
    grad_table = grad_table + jnp.where(mask_column, mask_grad_own.reshape(-1, 1), 0.0)

    grads_all = (
        grad_table,
        grad_head,
        grad_time,
        grad_ada,
        grad_gain_rows,
        grad_qkv,
        grad_out,
        grad_up,
        grad_down,
    )
    squares = jnp.sum(table_squares) + jnp.sum(head_squares) + small_square[0, 0]
    squares = squares + jnp.sum(all_sums * all_sums)
    square_total = links.total(jnp.broadcast_to(squares, (8, LANES)), sum)[0, 0]
    grad_norm = jnp.sqrt(square_total)
    clip_factor = jnp.minimum(1.0, clip_level / (grad_norm + 1e-06))
    weights_now = (embedding, head_table, w_time, w_ada, norm_gains, w_qkv, w_out, w_up, w_down)
    on_side = (0, 3)
    updated = []
    for place, (weight_now, gradient) in enumerate(zip(weights_now, grads_all)):
        state = (weight_now, states[place], states[len(weights_now) + place])
        if place in on_side:
            state = tuple(array.T for array in state)
        rate = embed_rate if place == 0 else learn_rate
        result = advance(*state, gradient, clip_factor, rate)
        if place in on_side:
            result = tuple(array.T for array in result)
        updated.append(result)
    new_arrays = tuple(result[n] for n in range(3) for result in updated)
    return (*new_arrays, loss_sum, masked_count, grad_norm)


def solution(mesh):
    both = ("dp", "vocab")
    weights_placed = (
        P("vocab", "dp"),
        P("dp", "vocab"),
        P(both, None),
        P(None, both),
        P(None, both),
        P(both, None),
        P(both, None),
        P(both, None),
        P(both, None),
    )
    return jax.shard_map(
        shards,
        mesh=mesh,
        in_specs=(P(both, None), P(both, None), P(both, None), P("dp")) + 3 * weights_placed,
        out_specs=3 * weights_placed + (P(), P(), P()),
        check_vma=False,
    )
```

```python
import functools

import jax
import jax.numpy as jnp
from jax import lax
from jax.experimental import pallas as pl
from jax.experimental.pallas import tpu as pltpu
from jax.sharding import PartitionSpec as P

HEAD_DIM = 64
VOCAB = 50258
FREQ = 256
FEWEST_MASKED = 32
LANES = 128


norm_epsilon = 1e-06
weight_cap = 20.0
clip_level = 1.0
learn_rate = 30.0
embed_rate = 2000.0
momentum_rate = 0.9
average_rate = 0.5
highest = lax.Precision.HIGHEST
low = jnp.bfloat16
wide = jnp.float32


def tie(*values):
    return lax.optimization_barrier(values)


class Links:
    def __init__(self, dp_count, vocab_count):
        core = 2 if vocab_count % 2 == 0 else 1
        side = 1
        while side * side < dp_count:
            side *= 2
        self.dp_count, self.vocab_count = dp_count, vocab_count
        self.axes = {
            "u": ("dp", side, dp_count // side),
            "v": ("dp", 1, side),
            "z": ("vocab", core, vocab_count // core),
            "c": ("vocab", 1, core),
            "dp": ("dp", 1, dp_count),
        }

    def size(self, axis):
        return self.axes[axis][2]

    def place(self, axis):
        group, unit, size = self.axes[axis]
        return (lax.axis_index(group) // unit) % size

    def hop(self, value, axis, step):
        group, unit, _ = self.axes[axis]
        flip = step * unit
        across, along = (flip, 0) if group == "dp" else (0, flip)
        pairs = [
            (d * self.vocab_count + w, (d ^ across) * self.vocab_count + (w ^ along))
            for d in range(self.dp_count)
            for w in range(self.vocab_count)
        ]
        return lax.ppermute(value, ("dp", "vocab"), pairs)

    def heard(self, value, axis):
        return [value] + [self.hop(value, axis, k) for k in range(1, self.size(axis))]

    def ordered(self, pieces, axis):
        place, count = self.place(axis), len(pieces)
        slots = []
        for slot in range(count):
            value = pieces[slot]
            for other in range(1, count):
                value = jnp.where(place == other, pieces[slot ^ other], value)
            slots.append(value)
        return slots

    def near(self, value, axis):
        return [value[0]] + [self.hop(value[k], axis, k) for k in range(1, self.size(axis))]

    def piled(self, pieces, axis, dim=0):
        return jnp.stack(self.ordered(pieces, axis), dim)

    def own(self, value, axis, dim=0):
        return lax.dynamic_index_in_dim(value, self.place(axis), dim, keepdims=False)

    def given(self, value, axis, dim=0):
        place = self.place(axis)
        return [
            self.hop(lax.dynamic_index_in_dim(value, place ^ k, dim, keepdims=False), axis, k)
            for k in range(1, self.size(axis))
        ]

    def slot(self, n, place):
        step = n ^ place
        along = self.size("v")
        return (step % along) * self.size("u") + step // along

    def exchange(self, value):
        value = value.reshape((self.size("v"), self.size("u")) + value.shape[1:])
        return self.near(value, "v")

    def exchanged(self, came):
        pieces = [piece[0] for piece in came]
        for step in range(1, self.size("u")):
            further = self.hop(jnp.stack([piece[step] for piece in came]), "u", step)
            pieces += [further[n] for n in range(self.size("v"))]
        return pieces

    def doubled(self, value, axis, step):
        came = self.hop(value, axis, step)
        upper = (self.place(axis) // step) % 2 == 1
        return jnp.concatenate([jnp.where(upper, came, value), jnp.where(upper, value, came)], 0)


    def half(self, value, other=False):
        width = value.shape[-1] // 2
        place = self.place("c")
        place = 1 - place if other else place
        return lax.dynamic_slice_in_dim(value, place * width, width, value.ndim - 1)

    def halves_back(self, mine, other):
        first = self.place("c") == 0
        return jnp.concatenate(
            [jnp.where(first, mine, other), jnp.where(first, other, mine)], -1
        )

    def pair_rows(self, mine, theirs):
        came = self.hop(theirs, "c", 1)
        return self.piled([mine, came], "c").reshape(-1, mine.shape[-1])

    def wide_across(self, pieces):
        block = lax.all_gather(self.piled(pieces, "z"), "dp", axis=0, tiled=False)
        return block.reshape(-1, block.shape[-1])

    def across_first(self, pieces, cut):
        block = self.piled(pieces, "z")
        return self.heard(block[..., :cut], "v"), self.heard(block[..., cut:], "u")

    def across_second(self, sides):
        return self.heard(self.piled(sides[0], "v"), "u"), self.heard(
            self.piled(sides[1], "u"), "v"
        )

    def across_done(self, sides):
        blocks = self.piled(sides[0], "u"), self.piled(sides[1], "v", 1)
        return [block.reshape(-1, block.shape[-1]) for block in blocks]


    def summed(self, state):
        return sum([piece.astype(wide) for piece in state[1]], state[0].astype(wide))

    def by_place(self, block):
        return block.reshape(
            self.size("u"), self.size("v"), self.size("z"), -1, block.shape[-1]
        )

    def fold_first(self, block, cut):
        left, right = block[..., :cut], block[..., cut:]
        return [
            (self.own(left, "u", 0), self.given(left, "u", 0)),
            (self.own(right, "v", 1), self.given(right, "v", 1)),
        ]

    def fold_second(self, states):
        left, right = [self.summed(state).astype(low) for state in states]
        return [
            (self.own(left, "v", 0), self.given(left, "v", 0)),
            (self.own(right, "u", 0), self.given(right, "u", 0)),
        ]

    def fold_third(self, states):
        return jnp.concatenate([self.summed(state).astype(low) for state in states], -1)

    def fold_z(self, block):
        return self.own(block, "z"), self.given(block, "z")

    def fold_across(self, block):
        block = block.reshape((self.dp_count,) + block.shape[2:])
        return lax.psum_scatter(block, "dp", scatter_dimension=0, tiled=False)

    def own_rows(self, state):
        block = state
        block = block.reshape(2, -1, block.shape[-1])
        return self.halves_back(self.own(block, "c"), self.given(block, "c")[0])

    def small_done(self, pieces):
        return self.piled(pieces, "c", 2).reshape(self.dp_count * self.vocab_count, -1)

    def total(self, value, join):
        for axis in ("z", "dp", "c"):
            value = join(self.heard(value, axis))
        return value


def half_cut(width):
    return max(LANES, (width // (2 * LANES)) * LANES) if width > LANES else width // 2


def features(level, freq_count):
    sigma_level = -jnp.log1p(-(1.0 - 0.001) * level)
    half_count = freq_count // 2
    frequency = jnp.exp(-jnp.log(10000.0) * jnp.arange(half_count, dtype=wide) / half_count)
    angles = sigma_level[..., None] * frequency
    return jnp.concatenate([jnp.cos(angles), jnp.sin(angles)], -1)


def nelbo_weight(level):
    sigma_level = -jnp.log1p(-(1.0 - 0.001) * level)
    rate_value = (1.0 - 0.001) / (1.0 - (1.0 - 0.001) * level)
    return jnp.minimum(rate_value / jnp.expm1(sigma_level), weight_cap)


def norm_mod(values, gain_row, shift_row, scale_row):
    center = values - jnp.mean(values, -1, keepdims=True)
    spread = jnp.mean(center * center, -1, keepdims=True)
    return center * lax.rsqrt(spread + norm_epsilon) * gain_row * (1.0 + scale_row) + shift_row


def times_rows(left_matrix, right_matrix):
    return lax.dot_general(
        left_matrix, right_matrix, (((0,), (0,)), ((), ())), preferred_element_type=wide
    )


def times_transposed(left_matrix, right_matrix):
    return lax.dot_general(
        left_matrix, right_matrix, (((1,), (1,)), ((), ())), preferred_element_type=wide
    )


def cost(megabytes):
    return pl.CostEstimate(flops=0, transcendentals=0, bytes_accessed=megabytes * 2**20)


def turn_kernel(in_ref, out_ref):
    out_ref[...] = in_ref[...].T


def turned(array):
    rows, columns = array.shape
    block = 8 * LANES
    return pl.pallas_call(
        turn_kernel,
        grid=(-(-columns // block),),
        out_shape=jax.ShapeDtypeStruct((columns, rows), array.dtype),
        in_specs=[pl.BlockSpec((rows, block), lambda i: (0, i))],
        out_specs=pl.BlockSpec((block, rows), lambda i: (i, 0)),
        cost_estimate=cost(24),
    )(array)


def block_of(s, grid, spot_ref):
    dp_count, z_count, core = grid
    along = lax.rem(s, z_count * core)
    across = lax.div(s, z_count * core) ^ spot_ref[0]
    deep = lax.div(along, core) ^ spot_ref[1]
    near = lax.rem(along, core) ^ spot_ref[2]
    return (near * z_count + deep) * dp_count + across


def look_up_kernel(
    grid, spot_ref, first_ref, last_ref, ids_ref, table_ref, mine_ref, theirs_ref, rows_ref, pair_ref
):
    half, width = mine_ref.shape[1], mine_ref.shape[2] // 2
    kept = 2 * half
    rows_ref[...] = jnp.zeros_like(rows_ref)
    base = spot_ref[3]

    def one_sequence(s, carry):
        first, last = first_ref[s], last_ref[s]
        to = block_of(s, grid, spot_ref) * kept

        def some(i, inner):
            places = [jnp.minimum(first + 8 * i + q, last - 1) for q in range(8)]
            found = [table_ref[pl.ds(ids_ref[s, k] - base, 1), :] for k in places]
            for k, row in zip(places, found):
                rows_ref[pl.ds(to + k, 1), :] = row
            return inner

        return lax.fori_loop(0, lax.div(last - first + 7, 8), some, carry)

    lax.fori_loop(0, first_ref.shape[0], one_sequence, 0)
    count = mine_ref.shape[0]
    for n, out_ref in enumerate((mine_ref, theirs_ref)):

        def rounded(b, carry):
            at = pl.multiple_of((n * count + b) * kept, 16)
            pair_ref[:, :width] = rows_ref[pl.ds(at, half), :]
            pair_ref[:, width:] = rows_ref[pl.ds(at + half, half), :]
            out_ref[b] = pair_ref[...].astype(out_ref.dtype)
            return carry

        lax.fori_loop(0, count, rounded, 0)


def fits(count, kept):
    return count * kept <= 16384


def by_steps(values, spot, grid):
    for axis, size in enumerate(grid):
        values = jnp.take(values, jnp.arange(size) ^ spot[axis], axis=axis)
    return values


def owned(first, last, ids):
    place = jnp.arange(ids.shape[1])[None]
    return (place >= first[:, None]) & (place < last[:, None])


def look_up_plain(spot, first, last, ids, table, grid):
    count, kept = ids.shape
    rows = table[jnp.clip(ids - spot[3], 0, table.shape[0] - 1)]
    rows = jnp.where(owned(first, last, ids)[..., None], rows, 0).astype(low)
    rows = jnp.swapaxes(rows.reshape(count, 2, kept // 2, -1), 1, 2).reshape(count, kept // 2, -1)
    rows = by_steps(rows.reshape(grid + rows.shape[1:]), spot, grid)
    rows = rows.transpose(2, 1, 0, 3, 4).reshape((2, count // 2) + rows.shape[3:])
    return rows[0], rows[1]


def add_up_plain(spot, first, last, ids, mine, theirs, span, grid):
    count, kept = ids.shape
    rows = jnp.stack([mine, theirs])[:, :, : kept // 2]
    rows = rows.reshape(grid[::-1] + rows.shape[2:])
    rows = by_steps(rows.transpose(2, 1, 0, 3, 4), spot, grid)
    rows = jnp.swapaxes(rows.reshape(count, kept // 2, 2, -1), 1, 2).astype(wide)
    places = jnp.where(owned(first, last, ids), ids - spot[3], span).reshape(-1)
    rows = rows.reshape(count * kept, -1)
    sums = jax.ops.segment_sum(rows, places, num_segments=span + 1)[:span].T
    return sums, jnp.sum(sums * sums, 0, keepdims=True)


def look_up(spot, first, last, ids, table, grid):
    count, kept = ids.shape
    width = 2 * table.shape[1]
    if not fits(count, kept):
        return look_up_plain(spot, first, last, ids, table, grid)
    smem = pl.BlockSpec(memory_space=pltpu.SMEM)
    vmem = pl.BlockSpec(memory_space=pltpu.VMEM)
    out = jax.ShapeDtypeStruct((count // 2, kept // 2, width), low)
    return pl.pallas_call(
        functools.partial(look_up_kernel, grid),
        out_shape=(out, out),
        in_specs=[smem, smem, smem, smem, vmem],
        out_specs=(vmem, vmem),
        scratch_shapes=[
            pltpu.VMEM((count * kept, width // 2), wide),
            pltpu.VMEM((kept // 2, width), wide),
        ],
        compiler_params=pltpu.CompilerParams(vmem_limit_bytes=56 * 2**20),
        cost_estimate=cost(36),
    )(spot, first, last, ids, table)


def add_up_kernel(
    grid,
    spot_ref,
    first_ref,
    last_ref,
    ids_ref,
    mine_ref,
    theirs_ref,
    out_ref,
    square_ref,
    sum_ref,
    wide_ref,
):
    span = out_ref.shape[1]
    sum_ref[...] = jnp.zeros_like(sum_ref)
    base = spot_ref[3]
    half, width, count = ids_ref.shape[1] // 2, mine_ref.shape[2] // 2, mine_ref.shape[0]
    kept = 2 * half
    for n, in_ref in enumerate((mine_ref, theirs_ref)):

        def widen(b, carry):
            at = pl.multiple_of((n * count + b) * kept, 16)
            rows = in_ref[b].astype(wide)
            wide_ref[pl.ds(at, half), :] = rows[:half, :width]
            wide_ref[pl.ds(at + half, half), :] = rows[:half, width:]
            return carry

        lax.fori_loop(0, count, widen, 0)

    def one_sequence(s, carry):
        first, last = first_ref[s], last_ref[s]
        start = block_of(s, grid, spot_ref) * kept

        def some(i, inner):
            places = [first + 8 * i + q for q in range(8)]
            near = [jnp.minimum(k, last - 1) for k in places]
            rows = [
                jnp.where(k < last, ids_ref[s, m] - base, span) for k, m in zip(places, near)
            ]
            parts = [wide_ref[pl.ds(start + m, 1), :] for m in near]
            for row, part in zip(rows, parts):
                sum_ref[pl.ds(row, 1), :] = sum_ref[pl.ds(row, 1), :] + part
            return inner

        return lax.fori_loop(0, lax.div(last - first + 7, 8), some, carry)

    lax.fori_loop(0, first_ref.shape[0], one_sequence, 0)
    whole = span // LANES

    def turn(b, squares):
        at = pl.multiple_of(b * LANES, LANES)
        part = sum_ref[pl.ds(at, LANES), :].T
        out_ref[:, pl.ds(at, LANES)] = part
        return squares + jnp.sum(part * part, 0, keepdims=True)

    squares = lax.fori_loop(0, whole, turn, jnp.zeros((1, LANES), wide))
    if span > whole * LANES:
        rest = span - whole * LANES
        part = sum_ref[whole * LANES : (whole + 1) * LANES, :].T
        out_ref[:, whole * LANES :] = part[:, :rest]
        lane = lax.broadcasted_iota(jnp.int32, part.shape, 1)
        part = jnp.where(lane < rest, part, 0.0)
        squares = squares + jnp.sum(part * part, 0, keepdims=True)
    square_ref[...] = squares


def add_up(spot, first, last, ids, mine, theirs, span, grid):
    count, kept = ids.shape
    if not fits(count, kept):
        return add_up_plain(spot, first, last, ids, mine, theirs, span, grid)
    width = mine.shape[2] // 2
    smem = pl.BlockSpec(memory_space=pltpu.SMEM)
    vmem = pl.BlockSpec(memory_space=pltpu.VMEM)
    padded = (span // LANES + 1) * LANES
    return pl.pallas_call(
        functools.partial(add_up_kernel, grid),
        out_shape=(
            jax.ShapeDtypeStruct((width, span), wide),
            jax.ShapeDtypeStruct((1, LANES), wide),
        ),
        in_specs=[smem, smem, smem, smem, vmem, vmem],
        out_specs=(vmem, vmem),
        scratch_shapes=[
            pltpu.VMEM((padded, width), wide),
            pltpu.VMEM((count * kept, width), wide),
        ],
        compiler_params=pltpu.CompilerParams(vmem_limit_bytes=56 * 2**20),
        cost_estimate=cost(50),
    )(spot, first, last, ids, mine, theirs)


def pack_kernel(core_ref, *refs):
    *in_refs, mine_ref, theirs_ref = refs
    first = core_ref[0] == 0
    at = 0
    rows = mine_ref.shape[0]
    for ref, tall in in_refs_of(in_refs):
        width = ref.shape[1]
        blocks = [(n * rows, (n + 1) * rows) for n in range(ref.shape[0] // rows)]
        if tall:
            sides = [
                [(blocks[n], (0, width)) for n in range(k, k + len(blocks) // 2)]
                for k in (0, len(blocks) // 2)
            ]
        else:
            sides = [
                [(block, (k, k + width // 2)) for block in blocks] for k in (0, width // 2)
            ]
        for left, right in zip(*sides):
            values = [
                ref[row[0] : row[1], column[0] : column[1]] for row, column in (left, right)
            ]
            to = slice(at, at + values[0].shape[1])
            mine_ref[:, to] = jnp.where(first, values[0], values[1]).astype(low)
            theirs_ref[:, to] = jnp.where(first, values[1], values[0]).astype(low)
            at = to.stop


def in_refs_of(refs):
    return [(ref, n == 2) for n, ref in enumerate(refs)]


def packed(core, w_qkv, w_out, ada_turned, w_up, w_down):
    rows = w_up.shape[0]
    arrays = (w_qkv, w_out, ada_turned, w_up, w_down)
    width = sum(array.size for array in arrays) // rows // 2
    out = jax.ShapeDtypeStruct((rows, width), low)
    vmem = pl.BlockSpec(memory_space=pltpu.VMEM)
    return pl.pallas_call(
        pack_kernel,
        out_shape=(out, out),
        in_specs=[pl.BlockSpec(memory_space=pltpu.SMEM)] + [vmem] * 5,
        out_specs=(vmem, vmem),
    )(core, *arrays)


def prepare_kernel(
    mask_id,
    place_ref,
    level_ref,
    clean_ref,
    slots_ref,
    time_ref,
    gains_ref,
    mask_row_ref,
    small_ref,
    first_ref,
    second_ref,
    collect_ref,
    spot_ref,
    alive_ref,
    masked_ref,
):
    length, slots = clean_ref.shape[1], slots_ref.shape[1]
    kept = collect_ref.shape[0]

    def iota(shape, dim):
        return lax.broadcasted_iota(jnp.int32, shape, dim)

    def stood(row):
        size = row.shape[1]
        same = iota((size, size), 0) == iota((size, size), 1)
        return jnp.sum(jnp.where(same, row, 0.0), 1, keepdims=True)

    def laid(column):
        size = column.shape[0]
        same = iota((size, size), 0) == iota((size, size), 1)
        return jnp.sum(jnp.where(same, column, 0.0), 0, keepdims=True)

    clean = clean_ref[...].astype(wide)
    slot = stood(slots_ref[...].astype(wide))
    across = iota((slots, length), 1).astype(wide)
    masked = jnp.sum((across == slot).astype(wide), 0, keepdims=True)
    ids = jnp.where(masked > 0, wide(mask_id), clean)
    key = ids * length + iota((1, length), 1).astype(wide)
    key_column = stood(key)
    rank_column = jnp.sum((key < key_column).astype(wide), 1, keepdims=True)
    rank = jnp.sum((key_column < key).astype(wide), 0, keepdims=True)
    spread = (rank_column == iota((length, kept), 1).astype(wide)).astype(wide)
    half = kept // 2
    first_ref[...] = (rank_column == iota((length, half), 1).astype(wide)).astype(low)
    second_ref[...] = (rank_column == (iota((length, half), 1) + half).astype(wide)).astype(low)
    collect_ref[...] = (rank == iota((kept, length), 0).astype(wide)).astype(low)
    masked_ref[...] = stood(masked)
    at_spot = across == jnp.minimum(slot, length - 1.0)
    spot_ref[...] = at_spot.astype(low)
    alive_ref[...] = (across == slot).astype(low)
    target = jnp.sum(jnp.where(at_spot, clean, 0.0), 1, keepdims=True)
    target = laid(jnp.where(slot < length, target, -1.0))
    small_ref[...] = jnp.zeros_like(small_ref)
    small_ref[0:1, :kept] = jnp.sum(spread * stood(ids), 0, keepdims=True)
    small_ref[1:2, :slots] = target
    small_ref[2:3, :] = jnp.full((1, small_ref.shape[1]), level_ref[place_ref[0]], wide)
    small_ref[3:4, : mask_row_ref.shape[1]] = mask_row_ref[...].astype(low).astype(wide)
    small_ref[4:7, : gains_ref.shape[1]] = gains_ref[...].astype(low).astype(wide)
    small_ref[8 : 8 + time_ref.shape[0], : time_ref.shape[1]] = time_ref[...].astype(low).astype(wide)


def prepare(mask_id, place, level, clean, slots, w_time, gains, mask_row, kept):
    length, slot_count = clean.shape[1], slots.shape[1]
    smem = pl.BlockSpec(memory_space=pltpu.SMEM)
    vmem = pl.BlockSpec(memory_space=pltpu.VMEM)
    rows = 8 + -(-w_time.shape[0] // 8) * 8
    shapes = (
        ((rows, length), wide),
        ((length, kept // 2), low),
        ((length, kept // 2), low),
        ((kept, length), low),
        ((slot_count, length), low),
        ((slot_count, length), low),
        ((length, 1), wide),
    )
    return pl.pallas_call(
        functools.partial(prepare_kernel, mask_id),
        out_shape=tuple(jax.ShapeDtypeStruct(*shape) for shape in shapes),
        in_specs=[smem, smem] + [vmem] * 5,
        out_specs=(vmem,) * len(shapes),
    )(place, level, clean, slots, w_time, gains, mask_row)


def enter_kernel(first_ref, second_ref, masked_ref, mask_row_ref, *refs):
    *piece_refs, out_ref = refs
    width = piece_refs[0].shape[1] // 2
    for n, piece_ref in enumerate(piece_refs):
        at = slice(n * width, (n + 1) * width)
        left = jnp.dot(first_ref[...], piece_ref[...], preferred_element_type=wide)
        right = jnp.dot(second_ref[...], piece_ref[...], preferred_element_type=wide)
        rows = left[:, :width] + right[:, width:]
        out_ref[:, at] = rows + masked_ref[...] * mask_row_ref[:, at]


def enter(first, second, masked, mask_row, pieces):
    width = pieces[0].shape[1] // 2
    return pl.pallas_call(
        enter_kernel,
        out_shape=jax.ShapeDtypeStruct((first.shape[0], width * len(pieces)), wide),
    )(first, second, masked, mask_row[None, :], *pieces)


def tail_rows(width, cond):
    return -(-(6 + (1 if 2 * cond <= width else 2 * -(-cond // width))) // 8) * 8


def tail_places(width, cond):
    if 2 * cond <= width:
        return [[(6, slice(n * cond, (n + 1) * cond), 0)] for n in range(2)]
    per = -(-cond // width)
    return [
        [
            (6 + n * per + k, slice(0, min(width, cond - k * width)), k * width)
            for k in range(per)
        ]
        for n in range(2)
    ]


def finish_kernel(
    scalar_ref, tails_ref, spectrum_ref, ada_ref, time_ref, gains_ref, mask_ref, square_ref
):
    place, width = scalar_ref[0], tails_ref.shape[2]
    size, cond, half = ada_ref.shape[0], ada_ref.shape[1], mask_ref.shape[1]

    def chosen(values, at, count):
        span = values.shape[1]
        spot = (iota((span, count), 0) == iota((span, count), 1) + at).astype(wide)
        return jnp.dot(values, spot, precision=highest, preferred_element_type=wide)

    def times(left, right):
        return lax.dot_general(
            left,
            right,
            (((0,), (0,)), ((), ())),
            precision=highest,
            preferred_element_type=wide,
        )

    def vector(n):
        parts = [tails_ref[:, row, lanes] for row, lanes, _ in tail_places(width, cond)[n]]
        return parts[0] if len(parts) == 1 else jnp.concatenate(parts, 1)

    row = lax.div(place * size, width)
    mods = tails_ref[:, 0, :]
    for n in range(1, 4):
        mods = jnp.where(row == n, tails_ref[:, n, :], mods)
    ada_ref[...] = times(chosen(mods, lax.rem(place * size, width), size), vector(0))
    time_ref[...] = times(spectrum_ref[...], vector(1))
    sums = [jnp.sum(tails_ref[:, n, :], 0, keepdims=True) for n in (4, 5)]
    rows = (sums[0][:, :half], sums[0][:, half:], sums[1][:, :half])
    which = iota((8, half), 0)
    block = jnp.zeros((8, half), wide)
    for n, values in enumerate(rows):
        block = jnp.where(which == n, values, block)
    gains_ref[...] = chosen(block, place * gains_ref.shape[1], gains_ref.shape[1])[:3]
    mask_ref[...] = sums[1][:, half:] * scalar_ref[1].astype(wide)
    total = sum(
        jnp.sum(jnp.sum(ref[...] * ref[...], 0, keepdims=True), 1, keepdims=True)
        for ref in (ada_ref, time_ref, gains_ref, mask_ref)
    )
    square_ref[...] = jnp.broadcast_to(total, square_ref.shape)


def finish(scalars, tails, spectrum, ada_rows, cond, gain_width, mask_width):
    return kernel_call(
        finish_kernel,
        scalars,
        (tails, spectrum),
        (
            ((ada_rows, cond), wide),
            ((spectrum.shape[1], cond), wide),
            ((3, gain_width), wide),
            ((1, mask_width), wide),
            ((1, LANES), wide),
        ),
    )


def laid_out(block, count, rows, width):
    parts = [
        block[:, at : at + width].reshape(count, 1, rows, width)
        for at in range(0, block.shape[1], width)
    ]
    return jnp.concatenate(parts, 1).reshape(-1, width)


def beside_blocks(block, count, rows):
    width = block.shape[1]
    block = block.reshape(count, -1, rows, width)
    return [block[:, n].reshape(count * rows, width) for n in range(block.shape[1])]


def column_of(info, n):
    return info[:, n : n + 1]


ROW_BLOCK = 512


def split_kernel(columns, place_ref, in_ref, out_ref):
    values = in_ref[...]
    column = lax.broadcasted_iota(jnp.int32, values.shape, 1)
    column = column + pl.program_id(0) * values.shape[1]
    out_ref[0] = jnp.where(column < columns, values, 0.0).astype(out_ref.dtype)


def split_head(links, place, table, piece):
    rows, columns = table.shape
    return pl.pallas_call(
        functools.partial(split_kernel, columns),
        out_shape=jax.ShapeDtypeStruct((links.dp_count, rows, piece), low),
        grid_spec=pltpu.PrefetchScalarGridSpec(
            num_scalar_prefetch=1,
            grid=(links.dp_count,),
            in_specs=[pl.BlockSpec((rows, piece), lambda i, at: (0, i))],
            out_specs=pl.BlockSpec(
                (1, rows, piece), lambda i, at: (links.slot(i, at[0]), 0, 0)
            ),
        ),
        cost_estimate=cost(8),
    )(place, table)


def stood(rows):
    which = lax.broadcasted_iota(jnp.int32, (8, rows[0].shape[1]), 0)
    block = jnp.broadcast_to(rows[0], which.shape)
    for n, row in enumerate(rows[1:]):
        block = jnp.where(which == n + 1, row, block)
    return block.T


def row_place():
    half = pl.num_programs(0) // 2
    return lambda core: lax.rem(pl.program_id(0) + core * half, 2 * half)


def logits_kernel(scalar_ref, mine_ref, theirs_ref, head_ref, info_ref, out_ref, stats_ref):
    is_mine = pl.program_id(0) < pl.num_programs(0) // 2
    block = row_place()(scalar_ref[0])
    limit = scalar_ref[1]
    rows = jnp.where(is_mine, mine_ref[...], theirs_ref[...])
    target = column_of(stood([info_ref[pl.ds(block, 1), :]]), 0).astype(jnp.int32)
    parts = []
    for at in head_parts(head_ref.shape[1]):
        values = jnp.dot(rows, head_ref[:, at], preferred_element_type=wide)
        column = lax.broadcasted_iota(jnp.int32, values.shape, 1) + at.start
        values = jnp.where(column < limit, values, -1e30)
        out_ref[:, at] = values
        found = jnp.sum(jnp.where(column == target, values, 0.0), 1, keepdims=True)
        peak = jnp.max(values, 1, keepdims=True)
        parts.append((peak, jnp.sum(jnp.exp(values - peak), 1, keepdims=True), found))
    peak = functools.reduce(jnp.maximum, [part[0] for part in parts])
    summed = sum(part[1] * jnp.exp(part[0] - peak) for part in parts)
    found = sum(part[2] for part in parts)
    lane = lax.broadcasted_iota(jnp.int32, (peak.shape[0], LANES), 1)
    columns = jnp.where(lane == 0, peak, jnp.where(lane == 1, summed, found)).T
    for n in range(3):
        stats_ref[n, pl.ds(block, 1), :] = columns[n : n + 1]


def head_parts(width):
    size = 4 * LANES
    return [slice(at, min(at + size, width)) for at in range(0, width, size)]


def head_specs(half, rows=ROW_BLOCK):
    by_step = lambda width: pl.BlockSpec((rows, width), lambda i, at: (i, 0))
    mine = lambda width: pl.BlockSpec((rows, width), lambda i, at: (jnp.minimum(i, half - 1), 0))
    theirs = lambda width: pl.BlockSpec((rows, width), lambda i, at: (jnp.maximum(i - half, 0), 0))
    whole = lambda shape: pl.BlockSpec(shape, lambda i, at: (0,) * len(shape))
    return by_step, mine, theirs, whole


def head_call(kernel, half, out_shape, in_specs, out_specs, scratch=(), cost=None):
    return pl.pallas_call(
        kernel,
        out_shape=out_shape,
        grid_spec=pltpu.PrefetchScalarGridSpec(
            num_scalar_prefetch=1,
            grid=(2 * half,),
            in_specs=in_specs,
            out_specs=out_specs,
            scratch_shapes=scratch,
        ),
        compiler_params=pltpu.CompilerParams(vmem_limit_bytes=50 * 2**20),
        cost_estimate=cost,
    )


def head_cost(rows, width, columns):
    return pl.CostEstimate(
        flops=2 * rows * width * columns,
        bytes_accessed=4 * rows * columns,
        transcendentals=rows * columns,
    )


def head_logits(scalars, mine, theirs, head, target):
    count, width = mine.shape
    half, columns = count // ROW_BLOCK, head.shape[1]
    by_step, by_mine, by_theirs, whole = head_specs(half)
    stats = (3, 2 * half, ROW_BLOCK)
    return head_call(
        logits_kernel,
        half,
        (
            jax.ShapeDtypeStruct((2 * count, columns), wide),
            jax.ShapeDtypeStruct(stats, wide),
        ),
        [by_mine(width), by_theirs(width), whole(head.shape), whole(target.shape)],
        (by_step(columns), whole(stats)),
        cost=head_cost(2 * count, width, columns),
    )(scalars, mine, theirs, head, target)


def slopes_kernel(
    scalar_ref, value_ref, head_ref, info_ref, slope_ref, mine_ref, theirs_ref
):
    block = row_place()(scalar_ref[0])
    info = stood([info_ref[n, pl.ds(block, 1), :] for n in range(3)])
    target, total, weight = [column_of(info, n) for n in range(3)]
    target = target.astype(jnp.int32)
    back = 0.0
    for at in head_parts(value_ref.shape[1]):
        values = value_ref[:, at]
        column = lax.broadcasted_iota(jnp.int32, values.shape, 1) + at.start
        odds = jnp.exp(values - total)
        slope = (jnp.where(column == target, odds - 1.0, odds) * weight).astype(low)
        slope_ref[:, at] = slope
        back = back + times_transposed(slope, head_ref[:, at])
    back = back.astype(mine_ref.dtype)
    is_mine = pl.program_id(0) < pl.num_programs(0) // 2

    @pl.when(is_mine)
    def _():
        mine_ref[...] = back

    @pl.when(jnp.logical_not(is_mine))
    def _():
        theirs_ref[...] = back


def head_slopes(scalars, values, head, info):
    count, (width, columns) = values.shape[0] // 2, head.shape
    half = count // ROW_BLOCK
    by_step, by_mine, by_theirs, whole = head_specs(half)
    return head_call(
        slopes_kernel,
        half,
        (
            jax.ShapeDtypeStruct((2 * count, columns), low),
            jax.ShapeDtypeStruct((count, width), low),
            jax.ShapeDtypeStruct((count, width), low),
        ),
        [by_step(columns), whole(head.shape), whole(info.shape)],
        (by_step(columns), by_mine(width), by_theirs(width)),
        cost=head_cost(2 * count, width, columns),
    )(scalars, values, head, info)


def head_grads_kernel(
    links, scalar_ref, mine_ref, theirs_ref, slope_ref, out_ref, square_ref, sum_ref
):
    step = pl.program_id(0)
    rows = jnp.where(step < pl.num_programs(0) // 2, mine_ref[...], theirs_ref[...])

    @pl.when(step == 0)
    def _():
        sum_ref[...] = jnp.zeros_like(sum_ref)

    for at in head_parts(slope_ref.shape[1]):
        sum_ref[:, at] += times_rows(rows, slope_ref[:, at])

    @pl.when(step == pl.num_programs(0) - 1)
    def _():
        size = out_ref.shape[1]
        squares = 0.0
        for n in range(out_ref.shape[0]):
            part = sum_ref[n * size : (n + 1) * size, :].astype(out_ref.dtype)
            out_ref[links.slot(n, scalar_ref[2])] = part
            part = part.astype(wide)
            squares = squares + jnp.sum(part * part, 0, keepdims=True)
        square_ref[...] = squares


def head_grads(links, scalars, mine, theirs, slopes):
    (count, width), columns = mine.shape, slopes.shape[1]
    rows = 3 * ROW_BLOCK if count % (3 * ROW_BLOCK) == 0 else ROW_BLOCK
    by_step, by_mine, by_theirs, whole = head_specs(count // rows, rows)
    out = (links.dp_count, width // links.dp_count, columns)
    return head_call(
        functools.partial(head_grads_kernel, links),
        count // rows,
        (jax.ShapeDtypeStruct(out, low), jax.ShapeDtypeStruct((1, columns), wide)),
        [by_mine(width), by_theirs(width), by_step(columns)],
        (whole(out), whole((1, columns))),
        [pltpu.VMEM((width, columns), wide)],
        head_cost(2 * count, width, columns),
    )(scalars, mine, theirs, slopes)


def iota(shape, dim):
    return lax.broadcasted_iota(jnp.int32, shape, dim)


def as_column(row):
    size = row.shape[1]
    same = iota((size, size), 0) == iota((size, size), 1)
    return jnp.sum(jnp.where(same, row, 0.0), 1, keepdims=True)


def kernel_call(kernel, scalar, arrays, shapes, scratch=(), megabytes=8):
    vmem = pl.BlockSpec(memory_space=pltpu.VMEM)
    out = [jax.ShapeDtypeStruct(*shape) for shape in shapes]
    return pl.pallas_call(
        kernel,
        out_shape=out,
        in_specs=[pl.BlockSpec(memory_space=pltpu.SMEM)] + [vmem] * len(arrays),
        out_specs=[vmem] * len(out),
        scratch_shapes=list(scratch),
        compiler_params=pltpu.CompilerParams(vmem_limit_bytes=50 * 2**20),
        cost_estimate=cost(megabytes),
    )(scalar, *arrays)


def part_of(core_ref, width, other=False):
    core = 1 - core_ref[0] if other else core_ref[0]
    return pl.ds(pl.multiple_of(core * width, LANES), width)


def product(core_ref, left, mine, theirs, out_ref):
    width = mine.shape[1]
    for matrix, other in ((mine, False), (theirs, True)):
        values = jnp.dot(left, matrix, preferred_element_type=wide)
        out_ref[:, part_of(core_ref, width, other)] = values.astype(out_ref.dtype)


def product_back(core_ref, slope_ref, mine, theirs):
    width = mine.shape[1]
    return times_transposed(slope_ref[:, part_of(core_ref, width)], mine) + times_transposed(
        slope_ref[:, part_of(core_ref, width, True)], theirs
    )


def norm_parts(values):
    center = values - jnp.mean(values, -1, keepdims=True)
    spread = jnp.mean(center * center, -1, keepdims=True)
    factor = lax.rsqrt(spread + norm_epsilon)
    return center * factor, factor


def norm_rows(values, mods, gains, n, shift):
    hat, _ = norm_parts(values)
    gain, at = gains[n : n + 1, :], slice(shift + 1, shift + 2)
    return hat * gain * (1.0 + mods[at, :]) + mods[shift : shift + 1, :]


def norm_back(values, slope, mods, gains, n, shift):
    hat, factor = norm_parts(values)
    gain, scale = gains[n : n + 1, :], 1.0 + mods[shift + 1 : shift + 2, :]
    along = jnp.sum(slope * hat, 0, keepdims=True)
    inner = slope * gain * scale
    inner = inner - jnp.mean(inner, -1, keepdims=True) - hat * jnp.mean(inner * hat, -1, keepdims=True)
    return inner * factor, (along * scale, jnp.sum(slope, 0, keepdims=True), along * gain)


def store_rows(out_ref, rows):
    which = iota(out_ref.shape, 0)
    block = jnp.zeros(out_ref.shape, wide)
    for n, row in enumerate(rows):
        block = jnp.where(which == n, row, block)
    out_ref[...] = block


ROOT = (2.0 / 3.141592653589793) ** 0.5


def gelu_parts(values):
    bend = jnp.tanh(ROOT * (values + 0.044715 * values * values * values))
    return 0.5 * values * (1.0 + bend), bend


def gelu_slope(values):
    _, bend = gelu_parts(values)
    inner = ROOT * (1.0 + 3.0 * 0.044715 * values * values)
    return 0.5 * (1.0 + bend) + 0.5 * values * (1.0 - bend * bend) * inner


def qkv_kernel(cut, core_ref, hidden_ref, mods, gains, mine, theirs, normed_ref, triple_ref):
    normed_ref[...] = norm_rows(hidden_ref[...], mods, gains, 0, 0).astype(low)
    product(core_ref, normed_ref[...], mine[:, :cut], theirs[:, :cut], triple_ref)


def head_pair(at, triple_ref):
    third = triple_ref.shape[1] // 3
    return [triple_ref[:, n * third + at : n * third + at + 2 * HEAD_DIM] for n in range(3)]


def head_probs(query, key, same):
    scores = times_transposed(query, key) * HEAD_DIM ** (-0.5)
    scores = jnp.where(same, scores, -1e30)
    expo = jnp.exp(scores - jnp.max(scores, -1, keepdims=True))
    return expo / jnp.sum(expo, -1, keepdims=True)


def masks_of(segment_ref, triple_ref):
    segment = segment_ref[...].astype(wide)
    same = as_column(segment) == segment
    lane = iota((triple_ref.shape[0], 2 * HEAD_DIM), 1)
    return same, (lane < HEAD_DIM, lane >= HEAD_DIM)


def attend_kernel(core_ref, triple_ref, segment_ref, out_ref):
    same, sides = masks_of(segment_ref, triple_ref)
    for at in range(0, out_ref.shape[1], 2 * HEAD_DIM):
        query, key, value = head_pair(at, triple_ref)
        results = []
        for side in sides:
            probs = head_probs(jnp.where(side, query, 0.0).astype(low), key, same)
            results.append(jnp.dot(probs.astype(low), value, preferred_element_type=wide))
        out_ref[:, at : at + 2 * HEAD_DIM] = jnp.where(sides[0], *results).astype(low)


def attend_back_kernel(core_ref, triple_ref, grad_ref, segment_ref, out_ref):
    same, sides = masks_of(segment_ref, triple_ref)
    third = triple_ref.shape[1] // 3
    factor = HEAD_DIM ** (-0.5)
    for at in range(0, third, 2 * HEAD_DIM):
        query, key, value = head_pair(at, triple_ref)
        grad = grad_ref[:, at : at + 2 * HEAD_DIM]
        queries, key_back, value_back = [], 0.0, 0.0
        for side in sides:
            own_query = jnp.where(side, query, 0.0).astype(low)
            own_grad = jnp.where(side, grad, 0.0).astype(low)
            probs = head_probs(own_query, key, same)
            value_back = value_back + times_rows(probs.astype(low), own_grad)
            slope = times_transposed(own_grad, value)
            slope = probs * (slope - jnp.sum(probs * slope, -1, keepdims=True))
            slope = slope.astype(low)
            queries.append(jnp.dot(slope, key, preferred_element_type=wide))
            key_back = key_back + times_rows(slope, own_query)
        parts = (jnp.where(sides[0], *queries) * factor, key_back * factor, value_back)
        for n, part in enumerate(parts):
            out_ref[:, n * third + at : n * third + at + 2 * HEAD_DIM] = part.astype(low)


def out_kernel(
    cuts, core_ref, attended_ref, hidden_ref, mods, gains, mine, theirs, branch_ref, mid_ref, normed_ref
):
    at = slice(*cuts)
    product(core_ref, attended_ref[...], mine[:, at], theirs[:, at], branch_ref)
    mid_ref[...] = hidden_ref[...] + mods[2:3, :] * branch_ref[...]
    normed_ref[...] = norm_rows(mid_ref[...], mods, gains, 1, 3).astype(low)


def up_kernel(core_ref, normed_ref, mine, theirs, up_ref, active_ref):
    product(core_ref, normed_ref[...], mine[...], theirs[...], up_ref)
    active_ref[...] = gelu_parts(up_ref[...])[0].astype(low)


def down_kernel(
    core_ref, active_ref, mid_ref, mods, gains, spot_ref, mine, theirs, branch_ref, end_ref, picked_ref
):
    product(core_ref, active_ref[...], mine[...], theirs[...], branch_ref)
    end_ref[...] = mid_ref[...] + mods[5:6, :] * branch_ref[...]
    final = norm_rows(end_ref[...], mods, gains, 2, 6).astype(low)
    picked_ref[...] = jnp.dot(spot_ref[...], final, preferred_element_type=wide).astype(low)


def down_back_kernel(
    core_ref,
    picked_ref,
    alive_ref,
    end_ref,
    branch_ref,
    mods,
    gains,
    up_ref,
    mine,
    theirs,
    end_back_ref,
    branch_back_ref,
    up_back_ref,
    sums_ref,
):
    slope = times_rows(alive_ref[...], picked_ref[...])
    slope, sums = norm_back(end_ref[...], slope, mods, gains, 2, 6)
    end_back_ref[...] = slope
    gate = jnp.sum(slope * branch_ref[...], 0, keepdims=True)
    store_rows(sums_ref, sums + (gate,))
    branch_back_ref[...] = (mods[5:6, :] * slope).astype(low)
    active = product_back(core_ref, branch_back_ref, mine[...], theirs[...])
    up_back_ref[...] = (active * gelu_slope(up_ref[...])).astype(low)


def up_back_kernel(
    cuts,
    core_ref,
    up_back_ref,
    mid_ref,
    end_back_ref,
    branch_ref,
    mods,
    gains,
    mine,
    theirs,
    mine_out,
    theirs_out,
    mid_back_ref,
    branch_back_ref,
    attended_back_ref,
    sums_ref,
):
    slope = product_back(core_ref, up_back_ref, mine[...], theirs[...])
    slope, sums = norm_back(mid_ref[...], slope, mods, gains, 1, 3)
    slope = end_back_ref[...] + slope
    mid_back_ref[...] = slope
    gate = jnp.sum(slope * branch_ref[...], 0, keepdims=True)
    store_rows(sums_ref, sums + (gate,))
    branch_back_ref[...] = (mods[2:3, :] * slope).astype(low)
    at = slice(*cuts)
    back = product_back(core_ref, branch_back_ref, mine_out[:, at], theirs_out[:, at])
    attended_back_ref[...] = back.astype(low)


def start_back_kernel(
    cut,
    core_ref,
    triple_back_ref,
    start_ref,
    mid_back_ref,
    mods,
    gains,
    mine,
    theirs,
    collect_ref,
    masked_ref,
    sums_2,
    sums_3,
    ada_ref,
    hidden_ref,
    before_ref,
    sent_ref,
    pair_ref,
):
    slope = product_back(core_ref, triple_back_ref, mine[:, :cut], theirs[:, :cut])
    slope, sums = norm_back(start_ref[...], slope, mods, gains, 0, 0)
    slope = (mid_back_ref[...] + slope).astype(low)
    mask = jnp.sum(masked_ref[...] * slope.astype(wide), 0, keepdims=True)
    rows = jnp.dot(collect_ref[...], slope, preferred_element_type=wide)
    half, width = collect_ref.shape[0] // 2, sent_ref.shape[2] // 2

    sums_2, sums_3 = sums_2[...], sums_3[...]
    parts = list(sums[1:3]) + [sums_2[n : n + 1] for n in (3, 1, 2)]
    parts += [sums_3[n : n + 1] for n in (3, 1, 2)]
    which = iota(sums_2.shape, 0)
    grad_mods = jnp.zeros(sums_2.shape, wide)
    for n, part in enumerate(parts):
        grad_mods = jnp.where(which == n, part, grad_mods)
    columns, model_width = grad_mods.T, grad_mods.shape[1]
    total = jnp.zeros((8, ada_ref.shape[1]), wide)
    for n in range(8):
        part = columns[:, n : n + 1] * ada_ref[n * model_width : (n + 1) * model_width, :].astype(wide)
        total = total + jnp.sum(part.reshape(-1, 8, part.shape[1]), 0)
    before = before_ref[...]
    gate = 1.0 / (1.0 + jnp.exp(-before))
    back = jnp.sum(total, 0, keepdims=True) * (gate + before * gate * (1.0 - gate))
    ends = (hidden_ref[...], back)
    fours = (sums[0], sums_2[0:1], sums_3[0:1], mask)
    pair_ref[...] = jnp.zeros_like(pair_ref)
    for values, places in zip(ends, tail_places(2 * width, back.shape[1])):
        for row, lanes, start in places:
            size = lanes.stop - lanes.start
            pair_ref[half + row : half + row + 1, lanes] = values[:, start : start + size]
    for n in range(sent_ref.shape[0]):
        at = slice(n * width, (n + 1) * width)
        pair_ref[:half, :width] = rows[:half, at]
        pair_ref[:half, width:] = rows[half:, at]
        for k in range(4):
            start = (4 * n + k) * 2 * width
            row, lane = start // model_width, start % model_width
            pair_ref[half + k : half + k + 1, :] = grad_mods[row : row + 1, lane : lane + 2 * width]
            lanes = slice((k % 2) * width, (k % 2 + 1) * width)
            row = half + 4 + k // 2
            pair_ref[row : row + 1, lanes] = fours[k][:, at]
        sent_ref[core_ref[1] ^ n] = pair_ref[...].astype(low)


def advance(weight_now, moment_now, average_now, gradient, clip_factor, rate_now):
    clipped = gradient * clip_factor
    moment_next = momentum_rate * moment_now + clipped
    weight_next = weight_now - rate_now * (clipped + momentum_rate * moment_next)
    return (
        weight_next,
        moment_next,
        average_rate * average_now + (1.0 - average_rate) * weight_next,
    )


def join_stats(pieces):
    peak_value = functools.reduce(jnp.maximum, [piece[0] for piece in pieces])
    summed = sum(piece[1] * jnp.exp(piece[0] - peak_value) for piece in pieces)
    return jnp.stack([peak_value, summed, sum(piece[2] for piece in pieces)])


def shards(
    x_clean,
    mask_index,
    segment_ids,
    noise_level,
    embedding,
    head_table,
    w_time,
    w_ada,
    norm_gains,
    w_qkv,
    w_out,
    w_up,
    w_down,
    *states,
):
    vocab_index = lax.axis_index("vocab")
    dp_index = lax.axis_index("dp")
    vocab_count = lax.axis_size("vocab")
    dp_count = lax.axis_size("dp")
    links = Links(dp_count, vocab_count)
    device_count = dp_count * vocab_count
    device_index = dp_index * vocab_count + vocab_index
    length = x_clean.shape[1]
    slot_count = mask_index.shape[1]
    kept_count = length - FEWEST_MASKED
    span = embedding.shape[0]
    columns = head_table.shape[1]
    slice_width = embedding.shape[1]
    model_width = slice_width * dp_count
    cond_width = w_time.shape[1]
    mask_id = VOCAB - 1

    place = vocab_index.astype(jnp.int32)[None]
    mask_local = mask_id - vocab_index * span
    mask_owner = (mask_local >= 0) & (mask_local < span)
    mask_row = lax.dynamic_slice_in_dim(embedding.T, jnp.clip(mask_local, 0, span - 1), 1, 1)
    mask_row = jnp.where(mask_owner, mask_row, 0.0).reshape(1, -1)
    small, first_half, second_half, collect, at_spot, alive_spot, masked = prepare(
        mask_id, place, noise_level, x_clean, mask_index, w_time, norm_gains, mask_row, kept_count
    )
    core = links.place("c").astype(jnp.int32)
    pack_mine, pack_theirs = packed(core[None], w_qkv, w_out, w_ada.T, w_up, w_down)
    pair = links.pair_rows(pack_mine, pack_theirs)
    rows = w_up.shape[0]
    qkv_width, ada_width = w_qkv.shape[1], w_ada.shape[1] // rows * cond_width
    ends = [0]
    for width in (qkv_width, model_width, ada_width, w_up.shape[1], w_down.size // rows):
        ends.append(ends[-1] + width // 2)
    pair_a, pair_bc = pair[:, : ends[3]], pair[:, ends[3] :]
    width_c = model_width // 2

    piece = -(-columns // (dp_count * LANES)) * LANES
    dp_place = dp_index.astype(jnp.int32)[None]
    small_z = links.heard(small, "z")
    head_slots = split_head(links, dp_place, head_table, piece)
    a_z = links.heard(pair_a, "z")
    table = turned(embedding.T)
    small_z, head_slots, a_z, table = tie(small_z, head_slots, a_z, table)
    a_mine = links.wide_across(a_z)
    small_dp, step = links.piled(small_z, "z")[None], 1
    while step < dp_count:
        small_dp, step = links.doubled(small_dp, "dp", step), 2 * step
    small_c = links.heard(small_dp, "c")
    head_came = links.exchange(head_slots)
    small_c, pair_bc = tie(small_c, pair_bc)
    bc_z = links.heard(pair_bc, "z")

    numbers = links.piled(small_c, "c", 2).reshape((device_count,) + small.shape)
    ids_all = numbers[:, 0, :kept_count].astype(jnp.int32)

    first = jnp.sum((ids_all < vocab_index * span).astype(jnp.int32), 1)
    stop_id = jnp.minimum((vocab_index + 1) * span, mask_id)
    last = jnp.maximum(jnp.sum((ids_all < stop_id).astype(jnp.int32), 1), first)
    spot = jnp.stack(
        [dp_index, links.place("z"), links.place("c"), vocab_index * span]
    ).astype(jnp.int32)
    grid = (dp_count, links.size("z"), links.size("c"))
    looked = look_up(spot, first, last, ids_all, table, grid)
    looked, bc_z, head_came, numbers = tie(looked, bc_z, head_came, numbers)
    looked_c = looked[0], [links.hop(looked[1], "c", 1)]
    looked = links.summed(looked_c).astype(low)
    looked = looked.reshape((grid[1], grid[0]) + looked.shape[1:])
    looked_z = links.near(looked, "z")
    half_up = w_up.shape[1] // 2
    bc_first = links.across_first(bc_z, half_up)

    targets = numbers[:, 1, :slot_count].astype(jnp.int32)
    levels = numbers[:, 2, 0]
    mask_row_full = jnp.sum(
        numbers[:, 3, :slice_width].reshape(dp_count, vocab_count, slice_width), 1
    ).reshape(-1)
    gains = jnp.swapaxes(numbers[:, 4:7, : norm_gains.shape[1]], 0, 1).reshape(3, model_width)
    time_weight = numbers[:, 8 : 8 + w_time.shape[0], :cond_width].reshape(-1, cond_width)
    live = (targets >= 0).astype(wide)
    masked_count = jnp.sum(live)

    by_core = lambda values: jnp.moveaxis(
        values.reshape(dp_count * links.size("z"), links.size("c"), -1), 1, 0
    ).reshape(-1, ROW_BLOCK)
    limit = jnp.minimum(columns, VOCAB - vocab_index * columns) - dp_index * piece
    target_local = by_core(targets) - vocab_index * columns - dp_index * piece
    target_local = jnp.where((target_local >= 0) & (target_local < limit), target_local, -1)
    target_local = target_local.astype(wide)
    row_weight = by_core(nelbo_weight(levels)[:, None] * live)
    row_share = row_weight / masked_count
    scalars = jnp.stack([core, limit.astype(jnp.int32), dp_place[0]])

    level = lax.dynamic_index_in_dim(noise_level, vocab_index, keepdims=False)
    spectrum = features(level[None], FREQ)
    before_time = jnp.dot(spectrum, time_weight, precision=highest)
    hidden_time = jax.nn.silu(before_time)
    time_rows = w_time.shape[0]
    spectrum_rows = lax.dynamic_slice_in_dim(
        features(levels, FREQ), device_index * time_rows, time_rows, 1
    )
    spectrum_rows = by_steps(spectrum_rows.reshape(grid + (time_rows,)), spot, grid)
    spectrum_rows = spectrum_rows.transpose(2, 1, 0, 3).reshape(device_count, time_rows)
    early = (hidden_time, gains, mask_row_full, target_local, row_share, scalars, spectrum_rows)
    looked_z, early, bc_first = tie(looked_z, early, bc_first)
    bc_second = links.across_second(bc_first)
    hidden_time, gains, mask_row_full, target_local, row_share, scalars, spectrum_rows = early
    looked = links.summed((looked_z[0], looked_z[1:])).astype(low)
    looked_dp = links.near(looked, "dp")
    looked_dp, a_mine = tie(looked_dp, a_mine)
    a_other = links.hop(a_mine, "c", 1)
    hidden_start = enter(
        first_half, second_half, masked, mask_row_full, links.ordered(looked_dp, "dp")
    )

    ada_weight = links.halves_back(a_mine[:, ends[2] :], a_other[:, ends[2] :])
    ada_weight = ada_weight.reshape(device_count, rows, -1, cond_width)
    ada_weight = jnp.swapaxes(ada_weight, 1, 2).reshape(-1, cond_width)
    mods = lax.dot_general(
        hidden_time, ada_weight.astype(wide), (((1,), (1,)), ((), ())), precision=highest
    ).reshape(8, -1)
    here = jnp.stack([core, dp_place[0]])
    square, inner = (length, model_width), (length, w_up.shape[1])
    normed_a, triple = kernel_call(
        functools.partial(qkv_kernel, ends[1]),
        here,
        (hidden_start, mods, gains, a_mine, a_other),
        ((square, low), ((length, qkv_width), low)),
    )
    (attended,) = kernel_call(attend_kernel, here, (triple, segment_ids), ((square, low),))
    attended, bc_second = tie(attended, bc_second)
    b_mine, c_mine = links.across_done(bc_second)
    c_mine = laid_out(c_mine, device_count, rows, width_c)
    branch_a, hidden_mid, normed_b = kernel_call(
        functools.partial(out_kernel, ends[1:3]),
        here,
        (attended, hidden_start, mods, gains, a_mine, a_other),
        ((square, wide), (square, wide), (square, low)),
    )
    b_other = links.hop(b_mine, "c", 1)
    c_other = links.hop(c_mine, "c", 1)
    up_values, active = kernel_call(
        up_kernel, here, (normed_b, b_mine, b_other), ((inner, wide), (inner, low))
    )
    branch_m, hidden_end, picked = kernel_call(
        down_kernel,
        here,
        (active, hidden_mid, mods, gains, at_spot, c_mine, c_other),
        ((square, wide), (square, wide), ((slot_count, model_width), low)),
    )

    cut_rows = half_cut(model_width)
    picked, head_came = tie(picked, head_came)
    picked_z = links.heard(picked, "z")
    head_pieces = links.exchanged(head_came)
    picked_z, head_pieces = tie(picked_z, head_pieces)
    head = jnp.concatenate(links.ordered(head_pieces, "dp"), 0)
    rows_first = links.across_first(picked_z, cut_rows)
    rows_second = links.across_second(rows_first)
    rows_mine = jnp.concatenate(links.across_done(rows_second), 1)
    rows_theirs = links.hop(rows_mine, "c", 1)
    values, stats = head_logits(scalars, rows_mine, rows_theirs, head, target_local)
    stats = links.total(stats, join_stats)
    log_total = stats[0] + jnp.log(stats[1])
    slopes, rows_own, rows_given = head_slopes(
        scalars, values, head, jnp.stack([target_local, log_total, row_share])
    )
    loss_sum = jnp.sum(row_share * (log_total - stats[2])) * masked_count
    rows_fold = rows_own, [links.hop(rows_given, "c", 1)]
    rows_fold, slopes = tie(rows_fold, slopes)
    rows_fold = links.by_place(links.summed(rows_fold).astype(low))
    rows_fold = links.fold_first(rows_fold, cut_rows)
    grad_head, head_squares = head_grads(links, scalars, rows_mine, rows_theirs, slopes)
    rows_fold, grad_head = tie(rows_fold, grad_head)
    rows_fold = links.fold_second(rows_fold)
    rows_fold, grad_head = tie(links.fold_third(rows_fold), grad_head)
    grad_mine = links.summed(links.fold_z(rows_fold)).astype(low)
    back_came = links.exchange(grad_head)

    def weight_given(left_matrix, slopes):
        return times_rows(left_matrix, links.half(slopes, True)).astype(low)

    def weight_own(left_matrix, slopes):
        return times_rows(left_matrix, links.half(slopes))

    grad_end, grad_branch_m, grad_upper, sums_3 = kernel_call(
        down_back_kernel,
        here,
        (
            grad_mine,
            alive_spot,
            hidden_end,
            branch_m,
            mods,
            gains,
            up_values,
            c_mine,
            c_other,
        ),
        ((square, wide), (square, low), (inner, low), ((8, model_width), wide)),
        megabytes=16,
    )
    grad_upper, back_came = tie(grad_upper, back_came)
    down_came = links.hop(weight_given(active, grad_branch_m), "c", 1)
    up_came = links.hop(weight_given(normed_b, grad_upper), "c", 1)
    grad_mid, grad_branch_a, grad_attended, sums_2 = kernel_call(
        functools.partial(up_back_kernel, ends[1:3]),
        here,
        (
            grad_upper,
            hidden_mid,
            grad_end,
            branch_a,
            mods,
            gains,
            b_mine,
            b_other,
            a_mine,
            a_other,
        ),
        ((square, wide), (square, low), (square, low), ((8, model_width), wide)),
        megabytes=16,
    )
    grad_attended, down_came, up_came = tie(grad_attended, down_came, up_came)
    up_sum = (weight_own(normed_b, grad_upper) + up_came.astype(wide)).astype(low)
    down_sum = (weight_own(active, grad_branch_m) + down_came.astype(wide)).astype(low)
    layer_sum = jnp.concatenate([up_sum] + beside_blocks(down_sum, device_count, rows), 1)
    layer_wide = links.fold_across(links.by_place(layer_sum))
    (grad_triple,) = kernel_call(
        attend_back_kernel,
        here,
        (triple, grad_attended, segment_ids),
        (((length, qkv_width), low),),
        megabytes=16,
    )
    sent_rows = kept_count // 2 + tail_rows(2 * slice_width, cond_width)
    (sent,) = kernel_call(
        functools.partial(start_back_kernel, ends[1]),
        here,
        (
            grad_triple,
            hidden_start,
            grad_mid,
            mods,
            gains,
            a_mine,
            a_other,
            collect,
            masked,
            sums_2,
            sums_3,
            ada_weight,
            hidden_time,
            before_time,
        ),
        (((dp_count, sent_rows, 2 * slice_width), low),),
        [pltpu.VMEM((sent_rows, 2 * slice_width), wide)],
        megabytes=16,
    )

    start_dp = links.near(sent, "dp")
    a_given = [weight_given(normed_a, grad_triple), weight_given(attended, grad_branch_a)]
    a_came = links.hop(jnp.concatenate(a_given, 1), "c", 1)
    start_dp, a_came = tie(start_dp, a_came)
    start_z = links.heard(jnp.stack(start_dp), "z")
    a_own = [weight_own(normed_a, grad_triple), weight_own(attended, grad_branch_a)]
    a_sum = (jnp.concatenate(a_own, 1) + a_came.astype(wide)).astype(low)
    a_fold = links.fold_first(links.by_place(a_sum), half_cut(a_sum.shape[1]))
    start_z, a_fold = tie(start_z, a_fold)
    start_mine = jnp.concatenate(start_z, 0)
    start_theirs = links.hop(start_mine, "c", 1)
    a_fold = links.fold_second(a_fold)
    start_theirs, a_fold, layer_wide, back_came = tie(
        start_theirs, a_fold, layer_wide, back_came
    )
    back_pieces = links.exchanged(back_came)
    a_block = links.fold_third(a_fold)
    all_fold = links.fold_z(jnp.concatenate([a_block, layer_wide], 2))
    grad_table, table_squares = add_up(
        spot, first, last, ids_all, start_mine, start_theirs, span, grid
    )
    tails = jnp.concatenate([start_mine[:, kept_count // 2 :], start_theirs[:, kept_count // 2 :]], 0)
    grad_table, all_fold = tie(grad_table, all_fold)
    all_sums = links.summed(all_fold)
    cuts = (0, a_block.shape[2], a_block.shape[2] + half_up, all_sums.shape[1])
    sum_a, sum_up, sum_down = [all_sums[:, cuts[n] : cuts[n + 1]] for n in range(3)]
    sum_down = laid_out(sum_down, 2, rows, width_c)
    sums = [sum_a, sum_up, sum_down]
    grad_a, grad_up, grad_down = [links.own_rows(block) for block in sums]
    grad_a = [grad_a[:, : grad_a.shape[1] // 2], grad_a[:, grad_a.shape[1] // 2 :]]
    grad_qkv = jnp.concatenate([side[:, : ends[1]] for side in grad_a], 1)
    grad_out = jnp.concatenate([side[:, ends[1] :] for side in grad_a], 1)
    grad_head = jnp.concatenate(links.ordered(back_pieces, "dp"), 1)[:, :columns].astype(wide)
    grad_ada, grad_time, grad_gain_rows, mask_grad_own, small_square = finish(
        jnp.stack([vocab_index, mask_owner]).astype(jnp.int32),
        tails.astype(wide),
        spectrum_rows,
        w_ada.shape[1],
        cond_width,
        norm_gains.shape[1],
        slice_width,
    )
    mask_column = (jnp.arange(span) == mask_local)[None, :]
    grad_table = grad_table + jnp.where(mask_column, mask_grad_own.reshape(-1, 1), 0.0)

    grads_all = (
        grad_table,
        grad_head,
        grad_time,
        grad_ada,
        grad_gain_rows,
        grad_qkv,
        grad_out,
        grad_up,
        grad_down,
    )
    squares = jnp.sum(table_squares) + jnp.sum(head_squares) + small_square[0, 0]
    squares = squares + jnp.sum(all_sums * all_sums)
    square_total = links.total(jnp.broadcast_to(squares, (8, LANES)), sum)[0, 0]
    grad_norm = jnp.sqrt(square_total)
    clip_factor = jnp.minimum(1.0, clip_level / (grad_norm + 1e-06))
    weights_now = (embedding, head_table, w_time, w_ada, norm_gains, w_qkv, w_out, w_up, w_down)
    on_side = (0, 3)
    updated = []
    for place, (weight_now, gradient) in enumerate(zip(weights_now, grads_all)):
        state = (weight_now, states[place], states[len(weights_now) + place])
        if place in on_side:
            state = tuple(array.T for array in state)
        rate = embed_rate if place == 0 else learn_rate
        result = advance(*state, gradient, clip_factor, rate)
        if place in on_side:
            result = tuple(array.T for array in result)
        updated.append(result)
    new_arrays = tuple(result[n] for n in range(3) for result in updated)
    return (*new_arrays, loss_sum, masked_count, grad_norm)


def solution(mesh):
    both = ("dp", "vocab")
    weights_placed = (
        P("vocab", "dp"),
        P("dp", "vocab"),
        P(both, None),
        P(None, both),
        P(None, both),
        P(both, None),
        P(both, None),
        P(both, None),
        P(both, None),
    )
    return jax.shard_map(
        shards,
        mesh=mesh,
        in_specs=(P(both, None), P(both, None), P(both, None), P("dp")) + 3 * weights_placed,
        out_specs=3 * weights_placed + (P(), P(), P()),
        check_vma=False,
    )
```

```python
import functools

import jax
import jax.numpy as jnp
from jax import lax
from jax.experimental import pallas as pl
from jax.experimental.pallas import tpu as pltpu
from jax.sharding import PartitionSpec as P

HEAD_DIM = 64
VOCAB = 50258
FREQ = 256
FEWEST_MASKED = 32
LANES = 128


norm_epsilon = 1e-06
weight_cap = 20.0
clip_level = 1.0
learn_rate = 30.0
embed_rate = 2000.0
momentum_rate = 0.9
average_rate = 0.5
highest = lax.Precision.HIGHEST
low = jnp.bfloat16
wide = jnp.float32


def tie(*values):
    return lax.optimization_barrier(values)


class Links:
    def __init__(self, dp_count, vocab_count):
        core = 2 if vocab_count % 2 == 0 else 1
        side = 1
        while side * side < dp_count:
            side *= 2
        self.dp_count, self.vocab_count = dp_count, vocab_count
        self.axes = {
            "u": ("dp", side, dp_count // side),
            "v": ("dp", 1, side),
            "z": ("vocab", core, vocab_count // core),
            "c": ("vocab", 1, core),
            "dp": ("dp", 1, dp_count),
        }

    def size(self, axis):
        return self.axes[axis][2]

    def place(self, axis):
        group, unit, size = self.axes[axis]
        return (lax.axis_index(group) // unit) % size

    def hop(self, value, axis, step):
        group, unit, _ = self.axes[axis]
        flip = step * unit
        across, along = (flip, 0) if group == "dp" else (0, flip)
        pairs = [
            (d * self.vocab_count + w, (d ^ across) * self.vocab_count + (w ^ along))
            for d in range(self.dp_count)
            for w in range(self.vocab_count)
        ]
        return lax.ppermute(value, ("dp", "vocab"), pairs)

    def heard(self, value, axis):
        return [value] + [self.hop(value, axis, k) for k in range(1, self.size(axis))]

    def ordered(self, pieces, axis):
        place, count = self.place(axis), len(pieces)
        slots = []
        for slot in range(count):
            value = pieces[slot]
            for other in range(1, count):
                value = jnp.where(place == other, pieces[slot ^ other], value)
            slots.append(value)
        return slots

    def near(self, value, axis):
        return [value[0]] + [self.hop(value[k], axis, k) for k in range(1, self.size(axis))]

    def piled(self, pieces, axis, dim=0):
        return jnp.stack(self.ordered(pieces, axis), dim)

    def own(self, value, axis, dim=0):
        return lax.dynamic_index_in_dim(value, self.place(axis), dim, keepdims=False)

    def given(self, value, axis, dim=0):
        place = self.place(axis)
        return [
            self.hop(lax.dynamic_index_in_dim(value, place ^ k, dim, keepdims=False), axis, k)
            for k in range(1, self.size(axis))
        ]

    def slot(self, n, place):
        step = n ^ place
        along = self.size("v")
        return (step % along) * self.size("u") + step // along

    def exchange(self, value):
        value = value.reshape((self.size("v"), self.size("u")) + value.shape[1:])
        return self.near(value, "v")

    def exchanged(self, came):
        pieces = [piece[0] for piece in came]
        for step in range(1, self.size("u")):
            further = self.hop(jnp.stack([piece[step] for piece in came]), "u", step)
            pieces += [further[n] for n in range(self.size("v"))]
        return pieces

    def doubled(self, value, axis, step):
        came = self.hop(value, axis, step)
        upper = (self.place(axis) // step) % 2 == 1
        return jnp.concatenate([jnp.where(upper, came, value), jnp.where(upper, value, came)], 0)


    def half(self, value, other=False):
        width = value.shape[-1] // 2
        place = self.place("c")
        place = 1 - place if other else place
        return lax.dynamic_slice_in_dim(value, place * width, width, value.ndim - 1)

    def halves_back(self, mine, other):
        first = self.place("c") == 0
        return jnp.concatenate(
            [jnp.where(first, mine, other), jnp.where(first, other, mine)], -1
        )

    def pair_rows(self, mine, theirs):
        came = self.hop(theirs, "c", 1)
        return self.piled([mine, came], "c").reshape(-1, mine.shape[-1])

    def wide_across(self, pieces):
        block = lax.all_gather(self.piled(pieces, "z"), "dp", axis=0, tiled=False)
        return block.reshape(-1, block.shape[-1])

    def across_first(self, pieces, cut):
        block = self.piled(pieces, "z")
        return self.heard(block[..., :cut], "v"), self.heard(block[..., cut:], "u")

    def across_second(self, sides):
        return self.heard(self.piled(sides[0], "v"), "u"), self.heard(
            self.piled(sides[1], "u"), "v"
        )

    def across_done(self, sides):
        blocks = self.piled(sides[0], "u"), self.piled(sides[1], "v", 1)
        return [block.reshape(-1, block.shape[-1]) for block in blocks]


    def summed(self, state):
        return sum([piece.astype(wide) for piece in state[1]], state[0].astype(wide))

    def by_place(self, block):
        return block.reshape(
            self.size("u"), self.size("v"), self.size("z"), -1, block.shape[-1]
        )

    def fold_first(self, block, cut):
        left, right = block[..., :cut], block[..., cut:]
        return [
            (self.own(left, "u", 0), self.given(left, "u", 0)),
            (self.own(right, "v", 1), self.given(right, "v", 1)),
        ]

    def fold_second(self, states):
        left, right = [self.summed(state).astype(low) for state in states]
        return [
            (self.own(left, "v", 0), self.given(left, "v", 0)),
            (self.own(right, "u", 0), self.given(right, "u", 0)),
        ]

    def fold_third(self, states):
        return jnp.concatenate([self.summed(state).astype(low) for state in states], -1)

    def fold_z(self, block):
        return self.own(block, "z"), self.given(block, "z")

    def fold_across(self, block):
        block = block.reshape((self.dp_count,) + block.shape[2:])
        return lax.psum_scatter(block, "dp", scatter_dimension=0, tiled=False)

    def own_rows(self, state):
        block = state
        block = block.reshape(2, -1, block.shape[-1])
        return self.halves_back(self.own(block, "c"), self.given(block, "c")[0])

    def small_done(self, pieces):
        return self.piled(pieces, "c", 2).reshape(self.dp_count * self.vocab_count, -1)

    def total(self, value, join):
        for axis in ("z", "dp", "c"):
            value = join(self.heard(value, axis))
        return value


def half_cut(width):
    return max(LANES, (width // (2 * LANES)) * LANES) if width > LANES else width // 2


def features(level, freq_count):
    sigma_level = -jnp.log1p(-(1.0 - 0.001) * level)
    half_count = freq_count // 2
    frequency = jnp.exp(-jnp.log(10000.0) * jnp.arange(half_count, dtype=wide) / half_count)
    angles = sigma_level[..., None] * frequency
    return jnp.concatenate([jnp.cos(angles), jnp.sin(angles)], -1)


def nelbo_weight(level):
    sigma_level = -jnp.log1p(-(1.0 - 0.001) * level)
    rate_value = (1.0 - 0.001) / (1.0 - (1.0 - 0.001) * level)
    return jnp.minimum(rate_value / jnp.expm1(sigma_level), weight_cap)


def norm_mod(values, gain_row, shift_row, scale_row):
    center = values - jnp.mean(values, -1, keepdims=True)
    spread = jnp.mean(center * center, -1, keepdims=True)
    return center * lax.rsqrt(spread + norm_epsilon) * gain_row * (1.0 + scale_row) + shift_row


def times_rows(left_matrix, right_matrix):
    return lax.dot_general(
        left_matrix, right_matrix, (((0,), (0,)), ((), ())), preferred_element_type=wide
    )


def times_transposed(left_matrix, right_matrix):
    return lax.dot_general(
        left_matrix, right_matrix, (((1,), (1,)), ((), ())), preferred_element_type=wide
    )


def cost(megabytes):
    return pl.CostEstimate(flops=0, transcendentals=0, bytes_accessed=megabytes * 2**20)


def turn_kernel(in_ref, out_ref):
    out_ref[...] = in_ref[...].T


def turned(array):
    rows, columns = array.shape
    block = 8 * LANES
    return pl.pallas_call(
        turn_kernel,
        grid=(-(-columns // block),),
        out_shape=jax.ShapeDtypeStruct((columns, rows), array.dtype),
        in_specs=[pl.BlockSpec((rows, block), lambda i: (0, i))],
        out_specs=pl.BlockSpec((block, rows), lambda i: (i, 0)),
        cost_estimate=cost(24),
    )(array)


def block_of(s, grid, spot_ref):
    dp_count, z_count, core = grid
    along = lax.rem(s, z_count * core)
    across = lax.div(s, z_count * core) ^ spot_ref[0]
    deep = lax.div(along, core) ^ spot_ref[1]
    near = lax.rem(along, core) ^ spot_ref[2]
    return (near * z_count + deep) * dp_count + across


def look_up_kernel(
    grid, spot_ref, first_ref, last_ref, ids_ref, table_ref, mine_ref, theirs_ref, rows_ref, pair_ref
):
    half, width = mine_ref.shape[1], mine_ref.shape[2] // 2
    kept = 2 * half
    rows_ref[...] = jnp.zeros_like(rows_ref)
    base = spot_ref[3]

    def one_sequence(s, carry):
        first, last = first_ref[s], last_ref[s]
        to = block_of(s, grid, spot_ref) * kept

        def some(i, inner):
            places = [jnp.minimum(first + 8 * i + q, last - 1) for q in range(8)]
            found = [table_ref[pl.ds(ids_ref[s, k] - base, 1), :] for k in places]
            for k, row in zip(places, found):
                rows_ref[pl.ds(to + k, 1), :] = row
            return inner

        return lax.fori_loop(0, lax.div(last - first + 7, 8), some, carry)

    lax.fori_loop(0, first_ref.shape[0], one_sequence, 0)
    count = mine_ref.shape[0]
    for n, out_ref in enumerate((mine_ref, theirs_ref)):

        def rounded(b, carry):
            at = pl.multiple_of((n * count + b) * kept, 16)
            pair_ref[:, :width] = rows_ref[pl.ds(at, half), :]
            pair_ref[:, width:] = rows_ref[pl.ds(at + half, half), :]
            out_ref[b] = pair_ref[...].astype(out_ref.dtype)
            return carry

        lax.fori_loop(0, count, rounded, 0)


def fits(count, kept):
    return count * kept <= 16384


def by_steps(values, spot, grid):
    for axis, size in enumerate(grid):
        values = jnp.take(values, jnp.arange(size) ^ spot[axis], axis=axis)
    return values


def owned(first, last, ids):
    place = jnp.arange(ids.shape[1])[None]
    return (place >= first[:, None]) & (place < last[:, None])


def look_up_plain(spot, first, last, ids, table, grid):
    count, kept = ids.shape
    rows = table[jnp.clip(ids - spot[3], 0, table.shape[0] - 1)]
    rows = jnp.where(owned(first, last, ids)[..., None], rows, 0).astype(low)
    rows = jnp.swapaxes(rows.reshape(count, 2, kept // 2, -1), 1, 2).reshape(count, kept // 2, -1)
    rows = by_steps(rows.reshape(grid + rows.shape[1:]), spot, grid)
    rows = rows.transpose(2, 1, 0, 3, 4).reshape((2, count // 2) + rows.shape[3:])
    return rows[0], rows[1]


def add_up_plain(spot, first, last, ids, mine, theirs, span, grid):
    count, kept = ids.shape
    rows = jnp.stack([mine, theirs])[:, :, : kept // 2]
    rows = rows.reshape(grid[::-1] + rows.shape[2:])
    rows = by_steps(rows.transpose(2, 1, 0, 3, 4), spot, grid)
    rows = jnp.swapaxes(rows.reshape(count, kept // 2, 2, -1), 1, 2).astype(wide)
    places = jnp.where(owned(first, last, ids), ids - spot[3], span).reshape(-1)
    rows = rows.reshape(count * kept, -1)
    sums = jax.ops.segment_sum(rows, places, num_segments=span + 1)[:span].T
    return sums, jnp.sum(sums * sums, 0, keepdims=True)


def look_up(spot, first, last, ids, table, grid):
    count, kept = ids.shape
    width = 2 * table.shape[1]
    if not fits(count, kept):
        return look_up_plain(spot, first, last, ids, table, grid)
    smem = pl.BlockSpec(memory_space=pltpu.SMEM)
    vmem = pl.BlockSpec(memory_space=pltpu.VMEM)
    out = jax.ShapeDtypeStruct((count // 2, kept // 2, width), low)
    return pl.pallas_call(
        functools.partial(look_up_kernel, grid),
        out_shape=(out, out),
        in_specs=[smem, smem, smem, smem, vmem],
        out_specs=(vmem, vmem),
        scratch_shapes=[
            pltpu.VMEM((count * kept, width // 2), wide),
            pltpu.VMEM((kept // 2, width), wide),
        ],
        compiler_params=pltpu.CompilerParams(vmem_limit_bytes=56 * 2**20),
        cost_estimate=cost(36),
    )(spot, first, last, ids, table)


def add_up_kernel(
    grid,
    spot_ref,
    first_ref,
    last_ref,
    ids_ref,
    mine_ref,
    theirs_ref,
    out_ref,
    square_ref,
    sum_ref,
    wide_ref,
):
    span = out_ref.shape[1]
    sum_ref[...] = jnp.zeros_like(sum_ref)
    base = spot_ref[3]
    half, width, count = ids_ref.shape[1] // 2, mine_ref.shape[2] // 2, mine_ref.shape[0]
    kept = 2 * half
    for n, in_ref in enumerate((mine_ref, theirs_ref)):

        def widen(b, carry):
            at = pl.multiple_of((n * count + b) * kept, 16)
            rows = in_ref[b].astype(wide)
            wide_ref[pl.ds(at, half), :] = rows[:half, :width]
            wide_ref[pl.ds(at + half, half), :] = rows[:half, width:]
            return carry

        lax.fori_loop(0, count, widen, 0)

    def one_sequence(s, carry):
        first, last = first_ref[s], last_ref[s]
        start = block_of(s, grid, spot_ref) * kept

        def some(i, inner):
            places = [first + 8 * i + q for q in range(8)]
            near = [jnp.minimum(k, last - 1) for k in places]
            rows = [
                jnp.where(k < last, ids_ref[s, m] - base, span) for k, m in zip(places, near)
            ]
            parts = [wide_ref[pl.ds(start + m, 1), :] for m in near]
            for row, part in zip(rows, parts):
                sum_ref[pl.ds(row, 1), :] = sum_ref[pl.ds(row, 1), :] + part
            return inner

        return lax.fori_loop(0, lax.div(last - first + 7, 8), some, carry)

    lax.fori_loop(0, first_ref.shape[0], one_sequence, 0)
    whole = span // LANES

    def turn(b, squares):
        at = pl.multiple_of(b * LANES, LANES)
        part = sum_ref[pl.ds(at, LANES), :].T
        out_ref[:, pl.ds(at, LANES)] = part
        return squares + jnp.sum(part * part, 0, keepdims=True)

    squares = lax.fori_loop(0, whole, turn, jnp.zeros((1, LANES), wide))
    if span > whole * LANES:
        rest = span - whole * LANES
        part = sum_ref[whole * LANES : (whole + 1) * LANES, :].T
        out_ref[:, whole * LANES :] = part[:, :rest]
        lane = lax.broadcasted_iota(jnp.int32, part.shape, 1)
        part = jnp.where(lane < rest, part, 0.0)
        squares = squares + jnp.sum(part * part, 0, keepdims=True)
    square_ref[...] = squares


def add_up(spot, first, last, ids, mine, theirs, span, grid):
    count, kept = ids.shape
    if not fits(count, kept):
        return add_up_plain(spot, first, last, ids, mine, theirs, span, grid)
    width = mine.shape[2] // 2
    smem = pl.BlockSpec(memory_space=pltpu.SMEM)
    vmem = pl.BlockSpec(memory_space=pltpu.VMEM)
    padded = (span // LANES + 1) * LANES
    return pl.pallas_call(
        functools.partial(add_up_kernel, grid),
        out_shape=(
            jax.ShapeDtypeStruct((width, span), wide),
            jax.ShapeDtypeStruct((1, LANES), wide),
        ),
        in_specs=[smem, smem, smem, smem, vmem, vmem],
        out_specs=(vmem, vmem),
        scratch_shapes=[
            pltpu.VMEM((padded, width), wide),
            pltpu.VMEM((count * kept, width), wide),
        ],
        compiler_params=pltpu.CompilerParams(vmem_limit_bytes=56 * 2**20),
        cost_estimate=cost(50),
    )(spot, first, last, ids, mine, theirs)


def pack_kernel(core_ref, *refs):
    *in_refs, mine_ref, theirs_ref = refs
    first = core_ref[0] == 0
    at = 0
    rows = mine_ref.shape[0]
    for ref, tall in in_refs_of(in_refs):
        width = ref.shape[1]
        blocks = [(n * rows, (n + 1) * rows) for n in range(ref.shape[0] // rows)]
        if tall:
            sides = [
                [(blocks[n], (0, width)) for n in range(k, k + len(blocks) // 2)]
                for k in (0, len(blocks) // 2)
            ]
        else:
            sides = [
                [(block, (k, k + width // 2)) for block in blocks] for k in (0, width // 2)
            ]
        for left, right in zip(*sides):
            values = [
                ref[row[0] : row[1], column[0] : column[1]] for row, column in (left, right)
            ]
            to = slice(at, at + values[0].shape[1])
            mine_ref[:, to] = jnp.where(first, values[0], values[1]).astype(low)
            theirs_ref[:, to] = jnp.where(first, values[1], values[0]).astype(low)
            at = to.stop


def in_refs_of(refs):
    return [(ref, n == 2) for n, ref in enumerate(refs)]


def packed(core, w_qkv, w_out, ada_turned, w_up, w_down):
    rows = w_up.shape[0]
    arrays = (w_qkv, w_out, ada_turned, w_up, w_down)
    width = sum(array.size for array in arrays) // rows // 2
    out = jax.ShapeDtypeStruct((rows, width), low)
    vmem = pl.BlockSpec(memory_space=pltpu.VMEM)
    return pl.pallas_call(
        pack_kernel,
        out_shape=(out, out),
        in_specs=[pl.BlockSpec(memory_space=pltpu.SMEM)] + [vmem] * 5,
        out_specs=(vmem, vmem),
    )(core, *arrays)


def prepare_kernel(
    mask_id,
    place_ref,
    level_ref,
    clean_ref,
    slots_ref,
    time_ref,
    gains_ref,
    mask_row_ref,
    small_ref,
    first_ref,
    second_ref,
    collect_ref,
    spot_ref,
    alive_ref,
    masked_ref,
):
    length, slots = clean_ref.shape[1], slots_ref.shape[1]
    kept = collect_ref.shape[0]

    def iota(shape, dim):
        return lax.broadcasted_iota(jnp.int32, shape, dim)

    def stood(row):
        size = row.shape[1]
        same = iota((size, size), 0) == iota((size, size), 1)
        return jnp.sum(jnp.where(same, row, 0.0), 1, keepdims=True)

    def laid(column):
        size = column.shape[0]
        same = iota((size, size), 0) == iota((size, size), 1)
        return jnp.sum(jnp.where(same, column, 0.0), 0, keepdims=True)

    clean = clean_ref[...].astype(wide)
    slot = stood(slots_ref[...].astype(wide))
    across = iota((slots, length), 1).astype(wide)
    masked = jnp.sum((across == slot).astype(wide), 0, keepdims=True)
    ids = jnp.where(masked > 0, wide(mask_id), clean)
    key = ids * length + iota((1, length), 1).astype(wide)
    key_column = stood(key)
    rank_column = jnp.sum((key < key_column).astype(wide), 1, keepdims=True)
    rank = jnp.sum((key_column < key).astype(wide), 0, keepdims=True)
    spread = (rank_column == iota((length, kept), 1).astype(wide)).astype(wide)
    half = kept // 2
    first_ref[...] = (rank_column == iota((length, half), 1).astype(wide)).astype(low)
    second_ref[...] = (rank_column == (iota((length, half), 1) + half).astype(wide)).astype(low)
    collect_ref[...] = (rank == iota((kept, length), 0).astype(wide)).astype(low)
    masked_ref[...] = stood(masked)
    at_spot = across == jnp.minimum(slot, length - 1.0)
    spot_ref[...] = at_spot.astype(low)
    alive_ref[...] = (across == slot).astype(low)
    target = jnp.sum(jnp.where(at_spot, clean, 0.0), 1, keepdims=True)
    target = laid(jnp.where(slot < length, target, -1.0))
    small_ref[...] = jnp.zeros_like(small_ref)
    small_ref[0:1, :kept] = jnp.sum(spread * stood(ids), 0, keepdims=True)
    small_ref[1:2, :slots] = target
    small_ref[2:3, :] = jnp.full((1, small_ref.shape[1]), level_ref[place_ref[0]], wide)
    small_ref[3:4, : mask_row_ref.shape[1]] = mask_row_ref[...].astype(low).astype(wide)
    small_ref[4:7, : gains_ref.shape[1]] = gains_ref[...].astype(low).astype(wide)
    small_ref[8 : 8 + time_ref.shape[0], : time_ref.shape[1]] = time_ref[...].astype(low).astype(wide)


def prepare(mask_id, place, level, clean, slots, w_time, gains, mask_row, kept):
    length, slot_count = clean.shape[1], slots.shape[1]
    smem = pl.BlockSpec(memory_space=pltpu.SMEM)
    vmem = pl.BlockSpec(memory_space=pltpu.VMEM)
    rows = 8 + -(-w_time.shape[0] // 8) * 8
    shapes = (
        ((rows, length), wide),
        ((length, kept // 2), low),
        ((length, kept // 2), low),
        ((kept, length), low),
        ((slot_count, length), low),
        ((slot_count, length), low),
        ((length, 1), wide),
    )
    return pl.pallas_call(
        functools.partial(prepare_kernel, mask_id),
        out_shape=tuple(jax.ShapeDtypeStruct(*shape) for shape in shapes),
        in_specs=[smem, smem] + [vmem] * 5,
        out_specs=(vmem,) * len(shapes),
    )(place, level, clean, slots, w_time, gains, mask_row)


def enter_kernel(first_ref, second_ref, masked_ref, mask_row_ref, *refs):
    *piece_refs, out_ref = refs
    width = piece_refs[0].shape[1] // 2
    for n, piece_ref in enumerate(piece_refs):
        at = slice(n * width, (n + 1) * width)
        left = jnp.dot(first_ref[...], piece_ref[...], preferred_element_type=wide)
        right = jnp.dot(second_ref[...], piece_ref[...], preferred_element_type=wide)
        rows = left[:, :width] + right[:, width:]
        out_ref[:, at] = rows + masked_ref[...] * mask_row_ref[:, at]


def enter(first, second, masked, mask_row, pieces):
    width = pieces[0].shape[1] // 2
    return pl.pallas_call(
        enter_kernel,
        out_shape=jax.ShapeDtypeStruct((first.shape[0], width * len(pieces)), wide),
    )(first, second, masked, mask_row[None, :], *pieces)


def tail_rows(width, cond):
    return -(-(6 + (1 if 2 * cond <= width else 2 * -(-cond // width))) // 8) * 8


def tail_places(width, cond):
    if 2 * cond <= width:
        return [[(6, slice(n * cond, (n + 1) * cond), 0)] for n in range(2)]
    per = -(-cond // width)
    return [
        [
            (6 + n * per + k, slice(0, min(width, cond - k * width)), k * width)
            for k in range(per)
        ]
        for n in range(2)
    ]


def finish_kernel(
    scalar_ref, tails_ref, spectrum_ref, ada_ref, time_ref, gains_ref, mask_ref, square_ref
):
    place, width = scalar_ref[0], tails_ref.shape[2]
    size, cond, half = ada_ref.shape[0], ada_ref.shape[1], mask_ref.shape[1]

    def chosen(values, at, count):
        span = values.shape[1]
        spot = (iota((span, count), 0) == iota((span, count), 1) + at).astype(wide)
        return jnp.dot(values, spot, precision=highest, preferred_element_type=wide)

    def times(left, right):
        return lax.dot_general(
            left,
            right,
            (((0,), (0,)), ((), ())),
            precision=highest,
            preferred_element_type=wide,
        )

    def vector(n):
        parts = [tails_ref[:, row, lanes] for row, lanes, _ in tail_places(width, cond)[n]]
        return parts[0] if len(parts) == 1 else jnp.concatenate(parts, 1)

    row = lax.div(place * size, width)
    mods = tails_ref[:, 0, :]
    for n in range(1, 4):
        mods = jnp.where(row == n, tails_ref[:, n, :], mods)
    ada_ref[...] = times(chosen(mods, lax.rem(place * size, width), size), vector(0))
    time_ref[...] = times(spectrum_ref[...], vector(1))
    sums = [jnp.sum(tails_ref[:, n, :], 0, keepdims=True) for n in (4, 5)]
    rows = (sums[0][:, :half], sums[0][:, half:], sums[1][:, :half])
    which = iota((8, half), 0)
    block = jnp.zeros((8, half), wide)
    for n, values in enumerate(rows):
        block = jnp.where(which == n, values, block)
    gains_ref[...] = chosen(block, place * gains_ref.shape[1], gains_ref.shape[1])[:3]
    mask_ref[...] = sums[1][:, half:] * scalar_ref[1].astype(wide)
    total = sum(
        jnp.sum(jnp.sum(ref[...] * ref[...], 0, keepdims=True), 1, keepdims=True)
        for ref in (ada_ref, time_ref, gains_ref, mask_ref)
    )
    square_ref[...] = jnp.broadcast_to(total, square_ref.shape)


def finish(scalars, tails, spectrum, ada_rows, cond, gain_width, mask_width):
    return kernel_call(
        finish_kernel,
        scalars,
        (tails, spectrum),
        (
            ((ada_rows, cond), wide),
            ((spectrum.shape[1], cond), wide),
            ((3, gain_width), wide),
            ((1, mask_width), wide),
            ((1, LANES), wide),
        ),
    )


def laid_out(block, count, rows, width):
    parts = [
        block[:, at : at + width].reshape(count, 1, rows, width)
        for at in range(0, block.shape[1], width)
    ]
    return jnp.concatenate(parts, 1).reshape(-1, width)


def beside_blocks(block, count, rows):
    width = block.shape[1]
    block = block.reshape(count, -1, rows, width)
    return [block[:, n].reshape(count * rows, width) for n in range(block.shape[1])]


def column_of(info, n):
    return info[:, n : n + 1]


ROW_BLOCK = 768


def split_kernel(columns, place_ref, in_ref, out_ref):
    values = in_ref[...]
    column = lax.broadcasted_iota(jnp.int32, values.shape, 1)
    column = column + pl.program_id(0) * values.shape[1]
    out_ref[0] = jnp.where(column < columns, values, 0.0).astype(out_ref.dtype)


def split_head(links, place, table, piece):
    rows, columns = table.shape
    return pl.pallas_call(
        functools.partial(split_kernel, columns),
        out_shape=jax.ShapeDtypeStruct((links.dp_count, rows, piece), low),
        grid_spec=pltpu.PrefetchScalarGridSpec(
            num_scalar_prefetch=1,
            grid=(links.dp_count,),
            in_specs=[pl.BlockSpec((rows, piece), lambda i, at: (0, i))],
            out_specs=pl.BlockSpec(
                (1, rows, piece), lambda i, at: (links.slot(i, at[0]), 0, 0)
            ),
        ),
        cost_estimate=cost(8),
    )(place, table)


def stood(rows):
    which = lax.broadcasted_iota(jnp.int32, (8, rows[0].shape[1]), 0)
    block = jnp.broadcast_to(rows[0], which.shape)
    for n, row in enumerate(rows[1:]):
        block = jnp.where(which == n + 1, row, block)
    return block.T


def row_place():
    half = pl.num_programs(0) // 2
    return lambda core: lax.rem(pl.program_id(0) + core * half, 2 * half)


def logits_kernel(scalar_ref, mine_ref, theirs_ref, head_ref, info_ref, out_ref, stats_ref):
    is_mine = pl.program_id(0) < pl.num_programs(0) // 2
    block = row_place()(scalar_ref[0])
    limit = scalar_ref[1]
    rows = jnp.where(is_mine, mine_ref[...], theirs_ref[...])
    target = column_of(stood([info_ref[pl.ds(block, 1), :]]), 0).astype(jnp.int32)
    parts = []
    for at in head_parts(head_ref.shape[1]):
        values = jnp.dot(rows, head_ref[:, at], preferred_element_type=wide)
        column = lax.broadcasted_iota(jnp.int32, values.shape, 1) + at.start
        values = jnp.where(column < limit, values, -1e30)
        out_ref[:, at] = values
        found = jnp.sum(jnp.where(column == target, values, 0.0), 1, keepdims=True)
        peak = jnp.max(values, 1, keepdims=True)
        parts.append((peak, jnp.sum(jnp.exp(values - peak), 1, keepdims=True), found))
    peak = functools.reduce(jnp.maximum, [part[0] for part in parts])
    summed = sum(part[1] * jnp.exp(part[0] - peak) for part in parts)
    found = sum(part[2] for part in parts)
    lane = lax.broadcasted_iota(jnp.int32, (peak.shape[0], LANES), 1)
    columns = jnp.where(lane == 0, peak, jnp.where(lane == 1, summed, found)).T
    for n in range(3):
        stats_ref[n, pl.ds(block, 1), :] = columns[n : n + 1]


def head_parts(width):
    size = 4 * LANES
    return [slice(at, min(at + size, width)) for at in range(0, width, size)]


def head_specs(half, rows=ROW_BLOCK):
    by_step = lambda width: pl.BlockSpec((rows, width), lambda i, at: (i, 0))
    mine = lambda width: pl.BlockSpec((rows, width), lambda i, at: (jnp.minimum(i, half - 1), 0))
    theirs = lambda width: pl.BlockSpec((rows, width), lambda i, at: (jnp.maximum(i - half, 0), 0))
    whole = lambda shape: pl.BlockSpec(shape, lambda i, at: (0,) * len(shape))
    return by_step, mine, theirs, whole


def head_call(kernel, half, out_shape, in_specs, out_specs, scratch=(), cost=None):
    return pl.pallas_call(
        kernel,
        out_shape=out_shape,
        grid_spec=pltpu.PrefetchScalarGridSpec(
            num_scalar_prefetch=1,
            grid=(2 * half,),
            in_specs=in_specs,
            out_specs=out_specs,
            scratch_shapes=scratch,
        ),
        compiler_params=pltpu.CompilerParams(vmem_limit_bytes=50 * 2**20),
        cost_estimate=cost,
    )


def head_cost(rows, width, columns):
    return pl.CostEstimate(
        flops=2 * rows * width * columns,
        bytes_accessed=4 * rows * columns,
        transcendentals=rows * columns,
    )


def head_logits(scalars, mine, theirs, head, target):
    count, width = mine.shape
    half, columns = count // ROW_BLOCK, head.shape[1]
    by_step, by_mine, by_theirs, whole = head_specs(half)
    stats = (3, 2 * half, ROW_BLOCK)
    return head_call(
        logits_kernel,
        half,
        (
            jax.ShapeDtypeStruct((2 * count, columns), wide),
            jax.ShapeDtypeStruct(stats, wide),
        ),
        [by_mine(width), by_theirs(width), whole(head.shape), whole(target.shape)],
        (by_step(columns), whole(stats)),
        cost=head_cost(2 * count, width, columns),
    )(scalars, mine, theirs, head, target)


def slopes_kernel(
    scalar_ref, value_ref, head_ref, info_ref, slope_ref, mine_ref, theirs_ref
):
    block = row_place()(scalar_ref[0])
    info = stood([info_ref[n, pl.ds(block, 1), :] for n in range(3)])
    target, total, weight = [column_of(info, n) for n in range(3)]
    target = target.astype(jnp.int32)
    back = 0.0
    for at in head_parts(value_ref.shape[1]):
        values = value_ref[:, at]
        column = lax.broadcasted_iota(jnp.int32, values.shape, 1) + at.start
        odds = jnp.exp(values - total)
        slope = (jnp.where(column == target, odds - 1.0, odds) * weight).astype(low)
        slope_ref[:, at] = slope
        back = back + times_transposed(slope, head_ref[:, at])
    back = back.astype(mine_ref.dtype)
    is_mine = pl.program_id(0) < pl.num_programs(0) // 2

    @pl.when(is_mine)
    def _():
        mine_ref[...] = back

    @pl.when(jnp.logical_not(is_mine))
    def _():
        theirs_ref[...] = back


def head_slopes(scalars, values, head, info):
    count, (width, columns) = values.shape[0] // 2, head.shape
    half = count // ROW_BLOCK
    by_step, by_mine, by_theirs, whole = head_specs(half)
    return head_call(
        slopes_kernel,
        half,
        (
            jax.ShapeDtypeStruct((2 * count, columns), low),
            jax.ShapeDtypeStruct((count, width), low),
            jax.ShapeDtypeStruct((count, width), low),
        ),
        [by_step(columns), whole(head.shape), whole(info.shape)],
        (by_step(columns), by_mine(width), by_theirs(width)),
        cost=head_cost(2 * count, width, columns),
    )(scalars, values, head, info)


def head_grads_kernel(
    links, scalar_ref, mine_ref, theirs_ref, slope_ref, out_ref, square_ref, sum_ref
):
    step = pl.program_id(0)
    rows = jnp.where(step < pl.num_programs(0) // 2, mine_ref[...], theirs_ref[...])

    @pl.when(step == 0)
    def _():
        sum_ref[...] = jnp.zeros_like(sum_ref)

    for at in head_parts(slope_ref.shape[1]):
        sum_ref[:, at] += times_rows(rows, slope_ref[:, at])

    @pl.when(step == pl.num_programs(0) - 1)
    def _():
        size = out_ref.shape[1]
        squares = 0.0
        for n in range(out_ref.shape[0]):
            part = sum_ref[n * size : (n + 1) * size, :].astype(out_ref.dtype)
            out_ref[links.slot(n, scalar_ref[2])] = part
            part = part.astype(wide)
            squares = squares + jnp.sum(part * part, 0, keepdims=True)
        square_ref[...] = squares


def head_grads(links, scalars, mine, theirs, slopes):
    (count, width), columns = mine.shape, slopes.shape[1]
    rows = 2 * ROW_BLOCK if count % (2 * ROW_BLOCK) == 0 else ROW_BLOCK
    by_step, by_mine, by_theirs, whole = head_specs(count // rows, rows)
    out = (links.dp_count, width // links.dp_count, columns)
    return head_call(
        functools.partial(head_grads_kernel, links),
        count // rows,
        (jax.ShapeDtypeStruct(out, low), jax.ShapeDtypeStruct((1, columns), wide)),
        [by_mine(width), by_theirs(width), by_step(columns)],
        (whole(out), whole((1, columns))),
        [pltpu.VMEM((width, columns), wide)],
        head_cost(2 * count, width, columns),
    )(scalars, mine, theirs, slopes)


def iota(shape, dim):
    return lax.broadcasted_iota(jnp.int32, shape, dim)


def as_column(row):
    size = row.shape[1]
    same = iota((size, size), 0) == iota((size, size), 1)
    return jnp.sum(jnp.where(same, row, 0.0), 1, keepdims=True)


def kernel_call(kernel, scalar, arrays, shapes, scratch=(), megabytes=8):
    vmem = pl.BlockSpec(memory_space=pltpu.VMEM)
    out = [jax.ShapeDtypeStruct(*shape) for shape in shapes]
    return pl.pallas_call(
        kernel,
        out_shape=out,
        in_specs=[pl.BlockSpec(memory_space=pltpu.SMEM)] + [vmem] * len(arrays),
        out_specs=[vmem] * len(out),
        scratch_shapes=list(scratch),
        compiler_params=pltpu.CompilerParams(vmem_limit_bytes=50 * 2**20),
        cost_estimate=cost(megabytes),
    )(scalar, *arrays)


def part_of(core_ref, width, other=False):
    core = 1 - core_ref[0] if other else core_ref[0]
    return pl.ds(pl.multiple_of(core * width, LANES), width)


def product(core_ref, left, mine, theirs, out_ref):
    width = mine.shape[1]
    for matrix, other in ((mine, False), (theirs, True)):
        values = jnp.dot(left, matrix, preferred_element_type=wide)
        out_ref[:, part_of(core_ref, width, other)] = values.astype(out_ref.dtype)


def product_back(core_ref, slope_ref, mine, theirs):
    width = mine.shape[1]
    return times_transposed(slope_ref[:, part_of(core_ref, width)], mine) + times_transposed(
        slope_ref[:, part_of(core_ref, width, True)], theirs
    )


def norm_parts(values):
    center = values - jnp.mean(values, -1, keepdims=True)
    spread = jnp.mean(center * center, -1, keepdims=True)
    factor = lax.rsqrt(spread + norm_epsilon)
    return center * factor, factor


def norm_rows(values, mods, gains, n, shift):
    hat, _ = norm_parts(values)
    gain, at = gains[n : n + 1, :], slice(shift + 1, shift + 2)
    return hat * gain * (1.0 + mods[at, :]) + mods[shift : shift + 1, :]


def norm_back(values, slope, mods, gains, n, shift):
    hat, factor = norm_parts(values)
    gain, scale = gains[n : n + 1, :], 1.0 + mods[shift + 1 : shift + 2, :]
    along = jnp.sum(slope * hat, 0, keepdims=True)
    inner = slope * gain * scale
    inner = inner - jnp.mean(inner, -1, keepdims=True) - hat * jnp.mean(inner * hat, -1, keepdims=True)
    return inner * factor, (along * scale, jnp.sum(slope, 0, keepdims=True), along * gain)


def store_rows(out_ref, rows):
    which = iota(out_ref.shape, 0)
    block = jnp.zeros(out_ref.shape, wide)
    for n, row in enumerate(rows):
        block = jnp.where(which == n, row, block)
    out_ref[...] = block


ROOT = (2.0 / 3.141592653589793) ** 0.5


def gelu_parts(values):
    bend = jnp.tanh(ROOT * (values + 0.044715 * values * values * values))
    return 0.5 * values * (1.0 + bend), bend


def gelu_slope(values):
    _, bend = gelu_parts(values)
    inner = ROOT * (1.0 + 3.0 * 0.044715 * values * values)
    return 0.5 * (1.0 + bend) + 0.5 * values * (1.0 - bend * bend) * inner


def qkv_kernel(cut, core_ref, hidden_ref, mods, gains, mine, theirs, normed_ref, triple_ref):
    normed_ref[...] = norm_rows(hidden_ref[...], mods, gains, 0, 0).astype(low)
    product(core_ref, normed_ref[...], mine[:, :cut], theirs[:, :cut], triple_ref)


def head_pair(at, triple_ref):
    third = triple_ref.shape[1] // 3
    return [triple_ref[:, n * third + at : n * third + at + 2 * HEAD_DIM] for n in range(3)]


def head_probs(query, key, same):
    scores = times_transposed(query, key) * HEAD_DIM ** (-0.5)
    scores = jnp.where(same, scores, -1e30)
    expo = jnp.exp(scores - jnp.max(scores, -1, keepdims=True))
    return expo / jnp.sum(expo, -1, keepdims=True)


def masks_of(segment_ref, triple_ref):
    segment = segment_ref[...].astype(wide)
    same = as_column(segment) == segment
    lane = iota((triple_ref.shape[0], 2 * HEAD_DIM), 1)
    return same, (lane < HEAD_DIM, lane >= HEAD_DIM)


def attend_kernel(core_ref, triple_ref, segment_ref, out_ref):
    same, sides = masks_of(segment_ref, triple_ref)
    for at in range(0, out_ref.shape[1], 2 * HEAD_DIM):
        query, key, value = head_pair(at, triple_ref)
        results = []
        for side in sides:
            probs = head_probs(jnp.where(side, query, 0.0).astype(low), key, same)
            results.append(jnp.dot(probs.astype(low), value, preferred_element_type=wide))
        out_ref[:, at : at + 2 * HEAD_DIM] = jnp.where(sides[0], *results).astype(low)


def attend_back_kernel(core_ref, triple_ref, grad_ref, segment_ref, out_ref):
    same, sides = masks_of(segment_ref, triple_ref)
    third = triple_ref.shape[1] // 3
    factor = HEAD_DIM ** (-0.5)
    for at in range(0, third, 2 * HEAD_DIM):
        query, key, value = head_pair(at, triple_ref)
        grad = grad_ref[:, at : at + 2 * HEAD_DIM]
        queries, key_back, value_back = [], 0.0, 0.0
        for side in sides:
            own_query = jnp.where(side, query, 0.0).astype(low)
            own_grad = jnp.where(side, grad, 0.0).astype(low)
            probs = head_probs(own_query, key, same)
            value_back = value_back + times_rows(probs.astype(low), own_grad)
            slope = times_transposed(own_grad, value)
            slope = probs * (slope - jnp.sum(probs * slope, -1, keepdims=True))
            slope = slope.astype(low)
            queries.append(jnp.dot(slope, key, preferred_element_type=wide))
            key_back = key_back + times_rows(slope, own_query)
        parts = (jnp.where(sides[0], *queries) * factor, key_back * factor, value_back)
        for n, part in enumerate(parts):
            out_ref[:, n * third + at : n * third + at + 2 * HEAD_DIM] = part.astype(low)


def out_kernel(
    cuts, core_ref, attended_ref, hidden_ref, mods, gains, mine, theirs, branch_ref, mid_ref, normed_ref
):
    at = slice(*cuts)
    product(core_ref, attended_ref[...], mine[:, at], theirs[:, at], branch_ref)
    mid_ref[...] = hidden_ref[...] + mods[2:3, :] * branch_ref[...]
    normed_ref[...] = norm_rows(mid_ref[...], mods, gains, 1, 3).astype(low)


def up_kernel(core_ref, normed_ref, mine, theirs, up_ref, active_ref):
    product(core_ref, normed_ref[...], mine[...], theirs[...], up_ref)
    active_ref[...] = gelu_parts(up_ref[...])[0].astype(low)


def down_kernel(
    core_ref, active_ref, mid_ref, mods, gains, spot_ref, mine, theirs, branch_ref, end_ref, picked_ref
):
    product(core_ref, active_ref[...], mine[...], theirs[...], branch_ref)
    end_ref[...] = mid_ref[...] + mods[5:6, :] * branch_ref[...]
    final = norm_rows(end_ref[...], mods, gains, 2, 6).astype(low)
    picked_ref[...] = jnp.dot(spot_ref[...], final, preferred_element_type=wide).astype(low)


def down_back_kernel(
    core_ref,
    picked_ref,
    alive_ref,
    end_ref,
    branch_ref,
    mods,
    gains,
    up_ref,
    mine,
    theirs,
    end_back_ref,
    branch_back_ref,
    up_back_ref,
    sums_ref,
):
    slope = times_rows(alive_ref[...], picked_ref[...])
    slope, sums = norm_back(end_ref[...], slope, mods, gains, 2, 6)
    end_back_ref[...] = slope
    gate = jnp.sum(slope * branch_ref[...], 0, keepdims=True)
    store_rows(sums_ref, sums + (gate,))
    branch_back_ref[...] = (mods[5:6, :] * slope).astype(low)
    active = product_back(core_ref, branch_back_ref, mine[...], theirs[...])
    up_back_ref[...] = (active * gelu_slope(up_ref[...])).astype(low)


def up_back_kernel(
    cuts,
    core_ref,
    up_back_ref,
    mid_ref,
    end_back_ref,
    branch_ref,
    mods,
    gains,
    mine,
    theirs,
    mine_out,
    theirs_out,
    mid_back_ref,
    branch_back_ref,
    attended_back_ref,
    sums_ref,
):
    slope = product_back(core_ref, up_back_ref, mine[...], theirs[...])
    slope, sums = norm_back(mid_ref[...], slope, mods, gains, 1, 3)
    slope = end_back_ref[...] + slope
    mid_back_ref[...] = slope
    gate = jnp.sum(slope * branch_ref[...], 0, keepdims=True)
    store_rows(sums_ref, sums + (gate,))
    branch_back_ref[...] = (mods[2:3, :] * slope).astype(low)
    at = slice(*cuts)
    back = product_back(core_ref, branch_back_ref, mine_out[:, at], theirs_out[:, at])
    attended_back_ref[...] = back.astype(low)


def start_back_kernel(
    cut,
    core_ref,
    triple_back_ref,
    start_ref,
    mid_back_ref,
    mods,
    gains,
    mine,
    theirs,
    collect_ref,
    masked_ref,
    sums_2,
    sums_3,
    ada_ref,
    hidden_ref,
    before_ref,
    sent_ref,
    pair_ref,
):
    slope = product_back(core_ref, triple_back_ref, mine[:, :cut], theirs[:, :cut])
    slope, sums = norm_back(start_ref[...], slope, mods, gains, 0, 0)
    slope = (mid_back_ref[...] + slope).astype(low)
    mask = jnp.sum(masked_ref[...] * slope.astype(wide), 0, keepdims=True)
    rows = jnp.dot(collect_ref[...], slope, preferred_element_type=wide)
    half, width = collect_ref.shape[0] // 2, sent_ref.shape[2] // 2

    sums_2, sums_3 = sums_2[...], sums_3[...]
    parts = list(sums[1:3]) + [sums_2[n : n + 1] for n in (3, 1, 2)]
    parts += [sums_3[n : n + 1] for n in (3, 1, 2)]
    which = iota(sums_2.shape, 0)
    grad_mods = jnp.zeros(sums_2.shape, wide)
    for n, part in enumerate(parts):
        grad_mods = jnp.where(which == n, part, grad_mods)
    columns, model_width = grad_mods.T, grad_mods.shape[1]
    total = jnp.zeros((8, ada_ref.shape[1]), wide)
    for n in range(8):
        part = columns[:, n : n + 1] * ada_ref[n * model_width : (n + 1) * model_width, :].astype(wide)
        total = total + jnp.sum(part.reshape(-1, 8, part.shape[1]), 0)
    before = before_ref[...]
    gate = 1.0 / (1.0 + jnp.exp(-before))
    back = jnp.sum(total, 0, keepdims=True) * (gate + before * gate * (1.0 - gate))
    ends = (hidden_ref[...], back)
    fours = (sums[0], sums_2[0:1], sums_3[0:1], mask)
    pair_ref[...] = jnp.zeros_like(pair_ref)
    for values, places in zip(ends, tail_places(2 * width, back.shape[1])):
        for row, lanes, start in places:
            size = lanes.stop - lanes.start
            pair_ref[half + row : half + row + 1, lanes] = values[:, start : start + size]
    for n in range(sent_ref.shape[0]):
        at = slice(n * width, (n + 1) * width)
        pair_ref[:half, :width] = rows[:half, at]
        pair_ref[:half, width:] = rows[half:, at]
        for k in range(4):
            start = (4 * n + k) * 2 * width
            row, lane = start // model_width, start % model_width
            pair_ref[half + k : half + k + 1, :] = grad_mods[row : row + 1, lane : lane + 2 * width]
            lanes = slice((k % 2) * width, (k % 2 + 1) * width)
            row = half + 4 + k // 2
            pair_ref[row : row + 1, lanes] = fours[k][:, at]
        sent_ref[core_ref[1] ^ n] = pair_ref[...].astype(low)


def advance(weight_now, moment_now, average_now, gradient, clip_factor, rate_now):
    clipped = gradient * clip_factor
    moment_next = momentum_rate * moment_now + clipped
    weight_next = weight_now - rate_now * (clipped + momentum_rate * moment_next)
    return (
        weight_next,
        moment_next,
        average_rate * average_now + (1.0 - average_rate) * weight_next,
    )


def join_stats(pieces):
    peak_value = functools.reduce(jnp.maximum, [piece[0] for piece in pieces])
    summed = sum(piece[1] * jnp.exp(piece[0] - peak_value) for piece in pieces)
    return jnp.stack([peak_value, summed, sum(piece[2] for piece in pieces)])


def shards(
    x_clean,
    mask_index,
    segment_ids,
    noise_level,
    embedding,
    head_table,
    w_time,
    w_ada,
    norm_gains,
    w_qkv,
    w_out,
    w_up,
    w_down,
    *states,
):
    vocab_index = lax.axis_index("vocab")
    dp_index = lax.axis_index("dp")
    vocab_count = lax.axis_size("vocab")
    dp_count = lax.axis_size("dp")
    links = Links(dp_count, vocab_count)
    device_count = dp_count * vocab_count
    device_index = dp_index * vocab_count + vocab_index
    length = x_clean.shape[1]
    slot_count = mask_index.shape[1]
    kept_count = length - FEWEST_MASKED
    span = embedding.shape[0]
    columns = head_table.shape[1]
    slice_width = embedding.shape[1]
    model_width = slice_width * dp_count
    cond_width = w_time.shape[1]
    mask_id = VOCAB - 1

    place = vocab_index.astype(jnp.int32)[None]
    mask_local = mask_id - vocab_index * span
    mask_owner = (mask_local >= 0) & (mask_local < span)
    mask_row = lax.dynamic_slice_in_dim(embedding.T, jnp.clip(mask_local, 0, span - 1), 1, 1)
    mask_row = jnp.where(mask_owner, mask_row, 0.0).reshape(1, -1)
    small, first_half, second_half, collect, at_spot, alive_spot, masked = prepare(
        mask_id, place, noise_level, x_clean, mask_index, w_time, norm_gains, mask_row, kept_count
    )
    core = links.place("c").astype(jnp.int32)
    pack_mine, pack_theirs = packed(core[None], w_qkv, w_out, w_ada.T, w_up, w_down)
    pair = links.pair_rows(pack_mine, pack_theirs)
    rows = w_up.shape[0]
    qkv_width, ada_width = w_qkv.shape[1], w_ada.shape[1] // rows * cond_width
    ends = [0]
    for width in (qkv_width, model_width, ada_width, w_up.shape[1], w_down.size // rows):
        ends.append(ends[-1] + width // 2)
    pair_a, pair_bc = pair[:, : ends[3]], pair[:, ends[3] :]
    width_c = model_width // 2

    piece = -(-columns // (dp_count * LANES)) * LANES
    dp_place = dp_index.astype(jnp.int32)[None]
    small_z = links.heard(small, "z")
    head_slots = split_head(links, dp_place, head_table, piece)
    a_z = links.heard(pair_a, "z")
    table = turned(embedding.T)
    small_z, head_slots, a_z, table = tie(small_z, head_slots, a_z, table)
    small_dp, step = links.piled(small_z, "z")[None], 1
    while step < dp_count:
        small_dp, step = links.doubled(small_dp, "dp", step), 2 * step
    small_c = links.heard(small_dp, "c")
    head_came = links.exchange(head_slots)
    pair_bc, _ = tie(pair_bc, a_z)
    bc_z = links.heard(pair_bc, "z")

    numbers = links.piled(small_c, "c", 2).reshape((device_count,) + small.shape)
    ids_all = numbers[:, 0, :kept_count].astype(jnp.int32)

    first = jnp.sum((ids_all < vocab_index * span).astype(jnp.int32), 1)
    stop_id = jnp.minimum((vocab_index + 1) * span, mask_id)
    last = jnp.maximum(jnp.sum((ids_all < stop_id).astype(jnp.int32), 1), first)
    spot = jnp.stack(
        [dp_index, links.place("z"), links.place("c"), vocab_index * span]
    ).astype(jnp.int32)
    grid = (dp_count, links.size("z"), links.size("c"))
    looked = look_up(spot, first, last, ids_all, table, grid)
    looked, bc_z, head_came, a_z = tie(looked, bc_z, head_came, a_z)
    a_mine = links.wide_across(a_z)
    looked_c = looked[0], [links.hop(looked[1], "c", 1)]
    looked, numbers = tie(links.summed(looked_c).astype(low), numbers)
    looked = looked.reshape((grid[1], grid[0]) + looked.shape[1:])
    looked_z = links.near(looked, "z")
    half_up = w_up.shape[1] // 2
    bc_first = links.across_first(bc_z, half_up)

    targets = numbers[:, 1, :slot_count].astype(jnp.int32)
    levels = numbers[:, 2, 0]
    mask_row_full = jnp.sum(
        numbers[:, 3, :slice_width].reshape(dp_count, vocab_count, slice_width), 1
    ).reshape(-1)
    gains = jnp.swapaxes(numbers[:, 4:7, : norm_gains.shape[1]], 0, 1).reshape(3, model_width)
    time_weight = numbers[:, 8 : 8 + w_time.shape[0], :cond_width].reshape(-1, cond_width)
    live = (targets >= 0).astype(wide)
    masked_count = jnp.sum(live)

    by_core = lambda values: jnp.moveaxis(
        values.reshape(dp_count * links.size("z"), links.size("c"), -1), 1, 0
    ).reshape(-1, ROW_BLOCK)
    limit = jnp.minimum(columns, VOCAB - vocab_index * columns) - dp_index * piece
    target_local = by_core(targets) - vocab_index * columns - dp_index * piece
    target_local = jnp.where((target_local >= 0) & (target_local < limit), target_local, -1)
    target_local = target_local.astype(wide)
    row_weight = by_core(nelbo_weight(levels)[:, None] * live)
    row_share = row_weight / masked_count
    scalars = jnp.stack([core, limit.astype(jnp.int32), dp_place[0]])

    level = lax.dynamic_index_in_dim(noise_level, vocab_index, keepdims=False)
    spectrum = features(level[None], FREQ)
    before_time = jnp.dot(spectrum, time_weight, precision=highest)
    hidden_time = jax.nn.silu(before_time)
    time_rows = w_time.shape[0]
    spectrum_rows = lax.dynamic_slice_in_dim(
        features(levels, FREQ), device_index * time_rows, time_rows, 1
    )
    spectrum_rows = by_steps(spectrum_rows.reshape(grid + (time_rows,)), spot, grid)
    spectrum_rows = spectrum_rows.transpose(2, 1, 0, 3).reshape(device_count, time_rows)
    early = (hidden_time, gains, mask_row_full, target_local, row_share, scalars, spectrum_rows)
    looked_z, bc_first = tie(looked_z, bc_first)
    bc_blocks = links.piled(bc_first[0], "v"), links.piled(bc_first[1], "u")
    looked = links.summed((looked_z[0], looked_z[1:])).astype(low)
    looked_dp = links.near(looked, "dp")
    looked_dp, a_mine, early, bc_blocks = tie(looked_dp, a_mine, early, bc_blocks)
    hidden_time, gains, mask_row_full, target_local, row_share, scalars, spectrum_rows = early
    bc_second = links.heard(bc_blocks[0], "u"), links.heard(bc_blocks[1], "v")
    a_other = links.hop(a_mine, "c", 1)
    hidden_start = enter(
        first_half, second_half, masked, mask_row_full, links.ordered(looked_dp, "dp")
    )

    ada_weight = links.halves_back(a_mine[:, ends[2] :], a_other[:, ends[2] :])
    ada_weight = ada_weight.reshape(device_count, rows, -1, cond_width)
    ada_weight = jnp.swapaxes(ada_weight, 1, 2).reshape(-1, cond_width)
    mods = lax.dot_general(
        hidden_time, ada_weight.astype(wide), (((1,), (1,)), ((), ())), precision=highest
    ).reshape(8, -1)
    here = jnp.stack([core, dp_place[0]])
    square, inner = (length, model_width), (length, w_up.shape[1])
    normed_a, triple = kernel_call(
        functools.partial(qkv_kernel, ends[1]),
        here,
        (hidden_start, mods, gains, a_mine, a_other),
        ((square, low), ((length, qkv_width), low)),
    )
    (attended,) = kernel_call(attend_kernel, here, (triple, segment_ids), ((square, low),))
    attended, bc_second = tie(attended, bc_second)
    b_mine, c_mine = links.across_done(bc_second)
    c_mine = laid_out(c_mine, device_count, rows, width_c)
    branch_a, hidden_mid, normed_b = kernel_call(
        functools.partial(out_kernel, ends[1:3]),
        here,
        (attended, hidden_start, mods, gains, a_mine, a_other),
        ((square, wide), (square, wide), (square, low)),
    )
    b_other = links.hop(b_mine, "c", 1)
    c_other = links.hop(c_mine, "c", 1)
    up_values, active = kernel_call(
        up_kernel, here, (normed_b, b_mine, b_other), ((inner, wide), (inner, low))
    )
    branch_m, hidden_end, picked = kernel_call(
        down_kernel,
        here,
        (active, hidden_mid, mods, gains, at_spot, c_mine, c_other),
        ((square, wide), (square, wide), ((slot_count, model_width), low)),
    )

    cut_rows = half_cut(model_width)
    picked, head_came = tie(picked, head_came)
    picked_z = links.heard(picked, "z")
    head_pieces = links.exchanged(head_came)
    rows_first = links.across_first(picked_z, cut_rows)
    rows_first, head_pieces = tie(rows_first, head_pieces)
    head = jnp.concatenate(links.ordered(head_pieces, "dp"), 0)
    rows_second = links.across_second(rows_first)
    rows_mine = jnp.concatenate(links.across_done(rows_second), 1)
    rows_theirs = links.hop(rows_mine, "c", 1)
    values, stats = head_logits(scalars, rows_mine, rows_theirs, head, target_local)
    stats = links.total(stats, join_stats)
    log_total = stats[0] + jnp.log(stats[1])
    slopes, rows_own, rows_given = head_slopes(
        scalars, values, head, jnp.stack([target_local, log_total, row_share])
    )
    loss_sum = jnp.sum(row_share * (log_total - stats[2])) * masked_count
    rows_fold = rows_own, [links.hop(rows_given, "c", 1)]
    rows_fold, slopes = tie(rows_fold, slopes)
    rows_fold = links.by_place(links.summed(rows_fold).astype(low))
    rows_fold = links.fold_first(rows_fold, cut_rows)
    grad_head, head_squares = head_grads(links, scalars, rows_mine, rows_theirs, slopes)
    rows_fold, grad_head = tie(rows_fold, grad_head)
    rows_fold = links.fold_second(rows_fold)
    rows_fold, grad_head = tie(links.fold_third(rows_fold), grad_head)
    grad_mine = links.summed(links.fold_z(rows_fold)).astype(low)
    back_came = links.exchange(grad_head)

    def weight_given(left_matrix, slopes):
        return times_rows(left_matrix, links.half(slopes, True)).astype(low)

    def weight_own(left_matrix, slopes):
        return times_rows(left_matrix, links.half(slopes))

    grad_end, grad_branch_m, grad_upper, sums_3 = kernel_call(
        down_back_kernel,
        here,
        (
            grad_mine,
            alive_spot,
            hidden_end,
            branch_m,
            mods,
            gains,
            up_values,
            c_mine,
            c_other,
        ),
        ((square, wide), (square, low), (inner, low), ((8, model_width), wide)),
        megabytes=16,
    )
    grad_upper, back_came = tie(grad_upper, back_came)
    down_came = links.hop(weight_given(active, grad_branch_m), "c", 1)
    up_came = links.hop(weight_given(normed_b, grad_upper), "c", 1)
    grad_mid, grad_branch_a, grad_attended, sums_2 = kernel_call(
        functools.partial(up_back_kernel, ends[1:3]),
        here,
        (
            grad_upper,
            hidden_mid,
            grad_end,
            branch_a,
            mods,
            gains,
            b_mine,
            b_other,
            a_mine,
            a_other,
        ),
        ((square, wide), (square, low), (square, low), ((8, model_width), wide)),
        megabytes=16,
    )
    grad_attended, down_came, up_came = tie(grad_attended, down_came, up_came)
    up_sum = (weight_own(normed_b, grad_upper) + up_came.astype(wide)).astype(low)
    down_sum = (weight_own(active, grad_branch_m) + down_came.astype(wide)).astype(low)
    layer_sum = jnp.concatenate([up_sum] + beside_blocks(down_sum, device_count, rows), 1)
    layer_wide = links.fold_across(links.by_place(layer_sum))
    (grad_triple,) = kernel_call(
        attend_back_kernel,
        here,
        (triple, grad_attended, segment_ids),
        (((length, qkv_width), low),),
        megabytes=16,
    )
    sent_rows = kept_count // 2 + tail_rows(2 * slice_width, cond_width)
    (sent,) = kernel_call(
        functools.partial(start_back_kernel, ends[1]),
        here,
        (
            grad_triple,
            hidden_start,
            grad_mid,
            mods,
            gains,
            a_mine,
            a_other,
            collect,
            masked,
            sums_2,
            sums_3,
            ada_weight,
            hidden_time,
            before_time,
        ),
        (((dp_count, sent_rows, 2 * slice_width), low),),
        [pltpu.VMEM((sent_rows, 2 * slice_width), wide)],
        megabytes=16,
    )

    start_dp = links.near(sent, "dp")
    a_given = [weight_given(normed_a, grad_triple), weight_given(attended, grad_branch_a)]
    a_came = links.hop(jnp.concatenate(a_given, 1), "c", 1)
    start_dp, a_came = tie(start_dp, a_came)
    start_z = links.heard(jnp.stack(start_dp), "z")
    a_own = [weight_own(normed_a, grad_triple), weight_own(attended, grad_branch_a)]
    a_sum = (jnp.concatenate(a_own, 1) + a_came.astype(wide)).astype(low)
    a_fold = links.fold_first(links.by_place(a_sum), half_cut(a_sum.shape[1]))
    start_z, a_fold = tie(start_z, a_fold)
    start_mine = jnp.concatenate(start_z, 0)
    start_theirs = links.hop(start_mine, "c", 1)
    a_fold = links.fold_second(a_fold)
    start_theirs, a_fold, layer_wide, back_came = tie(
        start_theirs, a_fold, layer_wide, back_came
    )
    back_pieces = links.exchanged(back_came)
    a_block = links.fold_third(a_fold)
    all_fold = links.fold_z(jnp.concatenate([a_block, layer_wide], 2))
    grad_table, table_squares = add_up(
        spot, first, last, ids_all, start_mine, start_theirs, span, grid
    )
    tails = jnp.concatenate([start_mine[:, kept_count // 2 :], start_theirs[:, kept_count // 2 :]], 0)
    grad_table, all_fold = tie(grad_table, all_fold)
    all_sums = links.summed(all_fold)
    cuts = (0, a_block.shape[2], a_block.shape[2] + half_up, all_sums.shape[1])
    sum_a, sum_up, sum_down = [all_sums[:, cuts[n] : cuts[n + 1]] for n in range(3)]
    sum_down = laid_out(sum_down, 2, rows, width_c)
    sums = [sum_a, sum_up, sum_down]
    grad_a, grad_up, grad_down = [links.own_rows(block) for block in sums]
    grad_a = [grad_a[:, : grad_a.shape[1] // 2], grad_a[:, grad_a.shape[1] // 2 :]]
    grad_qkv = jnp.concatenate([side[:, : ends[1]] for side in grad_a], 1)
    grad_out = jnp.concatenate([side[:, ends[1] :] for side in grad_a], 1)
    grad_head = jnp.concatenate(links.ordered(back_pieces, "dp"), 1)[:, :columns].astype(wide)
    grad_ada, grad_time, grad_gain_rows, mask_grad_own, small_square = finish(
        jnp.stack([vocab_index, mask_owner]).astype(jnp.int32),
        tails.astype(wide),
        spectrum_rows,
        w_ada.shape[1],
        cond_width,
        norm_gains.shape[1],
        slice_width,
    )
    mask_column = (jnp.arange(span) == mask_local)[None, :]
    grad_table = grad_table + jnp.where(mask_column, mask_grad_own.reshape(-1, 1), 0.0)

    grads_all = (
        grad_table,
        grad_head,
        grad_time,
        grad_ada,
        grad_gain_rows,
        grad_qkv,
        grad_out,
        grad_up,
        grad_down,
    )
    squares = jnp.sum(table_squares) + jnp.sum(head_squares) + small_square[0, 0]
    squares = squares + jnp.sum(all_sums * all_sums)
    square_total = links.total(jnp.broadcast_to(squares, (8, LANES)), sum)[0, 0]
    grad_norm = jnp.sqrt(square_total)
    clip_factor = jnp.minimum(1.0, clip_level / (grad_norm + 1e-06))
    weights_now = (embedding, head_table, w_time, w_ada, norm_gains, w_qkv, w_out, w_up, w_down)
    on_side = (0, 3)
    updated = []
    for place, (weight_now, gradient) in enumerate(zip(weights_now, grads_all)):
        state = (weight_now, states[place], states[len(weights_now) + place])
        if place in on_side:
            state = tuple(array.T for array in state)
        rate = embed_rate if place == 0 else learn_rate
        result = advance(*state, gradient, clip_factor, rate)
        if place in on_side:
            result = tuple(array.T for array in result)
        updated.append(result)
    new_arrays = tuple(result[n] for n in range(3) for result in updated)
    return (*new_arrays, loss_sum, masked_count, grad_norm)


def solution(mesh):
    both = ("dp", "vocab")
    weights_placed = (
        P("vocab", "dp"),
        P("dp", "vocab"),
        P(both, None),
        P(None, both),
        P(None, both),
        P(both, None),
        P(both, None),
        P(both, None),
        P(both, None),
    )
    return jax.shard_map(
        shards,
        mesh=mesh,
        in_specs=(P(both, None), P(both, None), P(both, None), P("dp")) + 3 * weights_placed,
        out_specs=3 * weights_placed + (P(), P(), P()),
        check_vma=False,
    )
```
